32 devices in a mesh: row: 8 (over z, core), col: 4 (over y, x).
Axes of the slice: x: 2, y: 2, z: 4, core: 2. Of those that a mesh axis runs over, the one named last changes fastest.
Arguments:
- layer_input: bfloat16 [4, 4096, 2048], P('col', 'row'), may hold values from -6 to 6
- out_grad: bfloat16 [4, 4096, 2048], P('col', 'row'), may hold values from -6 to 6
- routes: int32 [4, 4096, 8], P('col', 'row'), may hold values from 0 to 31, all different within a row; in each aligned block of 512 rows (0 to 511, 512 to 1023, ..., all dimensions but the last counted through in order) at most 128 rows name the same one
- positions: int32 [4, 4096], P(None, 'row'), may hold values from 0 to 6398, as said below
- w_q: bfloat16 [2048, 4096], P('row', 'col'), may hold values from -0.125 to 0.125
- key_value_weight: bfloat16 [2048, 1024], P('row'), may hold values from -0.125 to 0.125
- w_out: bfloat16 [4096, 2048], P('col', 'row'), may hold values from -1.5 to 1.5
- router: bfloat16 [2048, 32], P('row'), may hold values from -0.0625 to 0.0625
- ln_attn: bfloat16 [2048], P('row'), may hold values from 0.5 to 1.5
- ln_moe: bfloat16 [2048], P('row'), may hold values from 0.5 to 1.5
- q_gain: bfloat16 [128], P('row'), may hold values from 0.5 to 1.5
- k_gain: bfloat16 [128], P('row'), may hold values from 0.5 to 1.5
- w_gate: bfloat16 [32, 2048, 768], P(('row', 'col')), may hold values from -0.125 to 0.125
- w_up: bfloat16 [32, 2048, 768], P(('row', 'col')), may hold values from -0.125 to 0.125
- w_down: bfloat16 [32, 768, 2048], P(('row', 'col')), may hold values from -1.25 to 1.25
Outputs:
- layer_output: bfloat16 [4, 4096, 2048], P('col', 'row')
- aux_loss: float32 [], replicated
- input_grad: float32 [4, 4096, 2048], P('col', 'row')
- grad_q: float32 [2048, 4096], P('row', 'col')
- grad_kv: float32 [2048, 1024], P(('row', 'col'))
- grad_out: float32 [4096, 2048], P('col', 'row')
- grad_router: float32 [2048, 32], P(('row', 'col'))
- grad_ln_attn: float32 [2048], P(('row', 'col'))
- grad_ln_moe: float32 [2048], P(('row', 'col'))
- grad_q_gain: float32 [128], P(('row', 'col'))
- grad_k_gain: float32 [128], P(('row', 'col'))
- grad_gate: float32 [32, 2048, 768], P(('row', 'col'))
- grad_up: float32 [32, 2048, 768], P(('row', 'col'))
- grad_down: float32 [32, 768, 2048], P(('row', 'col'))
- expert_load: float32 [2, 32], replicated
The draws below stay inside these ranges and needn't reach their ends.
Inputs may be any that keep to these rules, and one draw needn't show every extreme that they name: `routes`: within the 512 rows of one device no expert is named more than 128 times; in every draw some device names some expert exactly 128 times. `positions`: in each group, for one offset b of 0 to 4095, the prompt's place t has position b + t and a continuation's place t has position b + 2048 + (t - 2048) % 256; in every draw some group has offset 0 and another offset 4095.
All inputs are finite; a program needn't handle non-finite values.
Results may differ from the reference program's by a relative error of at most 0.025.
Values may be sent and summed in bfloat16 or wider, within the bound.
No kernel may reach another device: no remote copies, remote signals or barrier semaphores. Data moves between devices by JAX's collectives and lax.ppermute only.
A program may use at most 448 MiB of HBM per device.

```python
import math
import jax
import jax.numpy as jnp
import numpy as np
from jax import lax

MODEL_DIM = 2048
QUERY_HEADS = 32
KEY_VALUE_HEADS = 4
HEAD_SIZE = 128
FFE = 768
TOPK = 8
CONTINUATION_LEN = 256
CONTINUATIONS = 8
EXPERTS = 32
PROMPT_TOKENS = 2048
GROUP_TOKENS = 4096
GROUP_TOTAL = 4
TOK_DEV = 512
CAP = 128
N_ROW = 8
N_COL = 4
DEVICES = 32


def draw_positions(key, part):
    key = jax.random.fold_in(key, 11)
    offset_key, order_key = jax.random.split(key)
    offsets = jax.random.randint(offset_key, (GROUP_TOTAL,), 0, 4096, dtype=jnp.int32)
    order = jax.random.permutation(order_key, GROUP_TOTAL).astype(jnp.int32)
    offsets = jnp.where(order == 0, 0, jnp.where(order == 1, 4095, offsets)).astype(jnp.int32)
    places = jnp.arange(GROUP_TOKENS, dtype=jnp.int32)[None, :]
    within = jnp.where(places < PROMPT_TOKENS, places, PROMPT_TOKENS + (places - PROMPT_TOKENS) % CONTINUATION_LEN)
    return (offsets[:, None] + within).astype(jnp.int32)


def block_scale(stream_key, extent, pieces, least, largest):
    gain, own = 1.0, jax.random.fold_in(stream_key, 6)
    for axis_at, blocks in pieces:
        heights = jnp.exp(jax.random.uniform(jax.random.fold_in(own, axis_at), (blocks,), jnp.float32, least / len(pieces), largest / len(pieces)))
        gain = gain * jnp.repeat(heights, extent[axis_at] // blocks).reshape([-1 if axis == axis_at else 1 for axis in range(len(extent))])
    return gain


def routed_block(rng, own, number, rows, number_of, top, limit, lean):
    sequence = jax.random.permutation(rng, number_of)
    heavy_load, common = shares(number_of, rows * top, limit, lean, True), shares(number_of, rows * top, limit, lean, False)
    places = jnp.arange(number_of)

    def named(lengths, rotation):
        used = int((lengths > 0).sum())
        fixed = max(1, used // 4)
        shifted = fixed + (places - fixed + rotation * (used - fixed)) % max(1, number_of - fixed)
        return jnp.zeros((number_of,), jnp.int32).at[sequence[jnp.where(places < fixed, places, shifted)]].set(jnp.asarray(lengths, jnp.int32))

    lengths = jnp.where(number % 4 == 0, named(heavy_load, number // 4), named(common, number - number // 4 - 1))
    mixed = jax.random.permutation(jax.random.fold_in(own, 3), number_of)
    giver, taker = mixed[0:number_of // 2 * 2:2], mixed[1:number_of // 2 * 2:2]
    margin = jnp.minimum(lengths[giver] - 1, limit - lengths[taker]) // 2
    margin = jnp.where((giver == sequence[0]) | (taker == sequence[0]) | (lengths[taker] == 0), 0, jnp.maximum(margin, 0))
    shifted = jax.random.randint(jax.random.fold_in(own, 4), (number_of // 2,), 0, 1 << 20) % (margin + 1)
    lengths = lengths.at[giver].add(-shifted).at[taker].add(shifted)
    items = jnp.searchsorted(jnp.cumsum(lengths), jnp.arange(rows * top), side="right").astype(jnp.int32)
    listing = items.reshape(top, rows).T
    listing = listing[jax.random.permutation(jax.random.fold_in(own, 1), rows)]
    rotation = jax.random.randint(jax.random.fold_in(own, 2), (rows, 1), 0, top)
    return jnp.take_along_axis(listing, (jnp.arange(top)[None, :] + rotation) % top, axis=1)


def shares(amount, total, limit, slope, full):
    weights = [(1 << 20) // math.isqrt(standing ** slope) + 1 for standing in range(1, amount + 1)]
    largest = limit if full else min(limit, max(-(-total // amount), total * weights[0] // sum(weights)))
    least = 1 if total - largest >= amount - 1 else 0
    holding, rest = [largest] + [least] * (amount - 1), total - largest - least * (amount - 1)
    while rest > 0:
        movable = [i for i in range(1, amount) if holding[i] < largest] or [i for i in range(1, amount) if holding[i] < limit]
        whole, remaining = sum([weights[i] for i in movable]), rest
        for i in movable:
            extra = min(limit - holding[i], max(1, remaining * weights[i] // whole), rest)
            holding[i] = holding[i] + extra
            rest = rest - extra
    return np.array(holding)


def scatter_about(stream_key, extent, scale, limit, shards=(), kind=jnp.bfloat16):
    drawn = scale * jax.random.normal(stream_key, extent, jnp.float32)
    if shards:
        drawn = drawn * block_scale(stream_key, extent, shards, -0.22, 0.18)
    return jnp.clip(drawn, -limit, limit).astype(kind)


def setup_inputs(seed: int = 0) -> dict:
    arg_keys = jax.random.split(jax.random.key(seed), 16)
    layer_input = scatter_about(arg_keys[0], (GROUP_TOTAL, GROUP_TOKENS, MODEL_DIM), 1.0, 6.0, ((0, 4), (1, 8)))
    out_grad = scatter_about(arg_keys[1], (GROUP_TOTAL, GROUP_TOKENS, MODEL_DIM), 1.0, 6.0, ((0, 4), (1, 8)))
    routes_keys = jax.random.split(jax.random.fold_in(arg_keys[2], 1), GROUP_TOTAL * GROUP_TOKENS // TOK_DEV)
    routes_turns = jax.random.permutation(jax.random.fold_in(arg_keys[2], 3), GROUP_TOTAL * GROUP_TOKENS // TOK_DEV)
    routes = jax.vmap(lambda own, number: routed_block(jax.random.fold_in(arg_keys[2], 2), own, number, TOK_DEV, EXPERTS, TOPK, CAP, 0))(routes_keys, routes_turns).reshape((GROUP_TOTAL, GROUP_TOKENS, TOPK))
    positions = draw_positions(jax.random.fold_in(arg_keys[15], 71), 0)
    w_q = scatter_about(arg_keys[4], (MODEL_DIM, QUERY_HEADS * HEAD_SIZE), MODEL_DIM ** -0.5, 0.125, ((0, 8), (1, 4)))
    key_value_weight = scatter_about(arg_keys[5], (MODEL_DIM, 2 * KEY_VALUE_HEADS * HEAD_SIZE), MODEL_DIM ** -0.5, 0.125, ((0, 8),))
    w_out = scatter_about(arg_keys[6], (QUERY_HEADS * HEAD_SIZE, MODEL_DIM), (max(QUERY_HEADS * HEAD_SIZE // 256, 1)) ** -0.5, 1.5, ((0, 4), (1, 8)))
    router = scatter_about(arg_keys[7], (MODEL_DIM, EXPERTS), (4 * MODEL_DIM) ** -0.5, 0.0625, ((0, 8),))
    ln_attn = jnp.clip(1.0 + 0.1 * jax.random.normal(arg_keys[8], (MODEL_DIM,), jnp.float32), 0.5, 1.5).astype(jnp.bfloat16)
    ln_moe = jnp.clip(1.0 + 0.1 * jax.random.normal(arg_keys[9], (MODEL_DIM,), jnp.float32), 0.5, 1.5).astype(jnp.bfloat16)
    q_gain = jnp.clip(1.0 + 0.1 * jax.random.normal(arg_keys[10], (HEAD_SIZE,), jnp.float32), 0.5, 1.5).astype(jnp.bfloat16)
    k_gain = jnp.clip(1.0 + 0.1 * jax.random.normal(arg_keys[11], (HEAD_SIZE,), jnp.float32), 0.5, 1.5).astype(jnp.bfloat16)
    w_gate = scatter_about(arg_keys[12], (EXPERTS, MODEL_DIM, FFE), MODEL_DIM ** -0.5, 0.125, ((0, 32),))
    w_up = scatter_about(arg_keys[13], (EXPERTS, MODEL_DIM, FFE), MODEL_DIM ** -0.5, 0.125, ((0, 32),))
    w_down = scatter_about(arg_keys[14], (EXPERTS, FFE, MODEL_DIM), (max(FFE // 32, 1)) ** -0.5, 1.25, ((0, 32),))
    return dict(layer_input=layer_input, out_grad=out_grad, routes=routes, positions=positions, w_q=w_q, key_value_weight=key_value_weight, w_out=w_out, router=router, ln_attn=ln_attn, ln_moe=ln_moe, q_gain=q_gain, k_gain=k_gain, w_gate=w_gate, w_up=w_up, w_down=w_down)


EPS = 1e-06
THETA = 1000000.0
AUX_COEF = 0.001

@jax.custom_vjp
def low(v):
    return lax.optimization_barrier(v.astype(jnp.bfloat16)).astype(jnp.float32)

@jax.custom_vjp
def low_back(v):
    return v

def low_keep(v):
    return (low(v), None)

def low_pass(kept, grad):
    return (grad,)

def back_keep(v):
    return (v, None)

def back_low(kept, grad):
    return (low(grad),)
low.defvjp(low_keep, low_pass)
low_back.defvjp(back_keep, back_low)

def exact_dot(left, right):
    return jnp.dot(left, right, precision=lax.Precision.HIGHEST)

def row_norm(vector, scale_gain):
    return vector * lax.rsqrt(lax.optimization_barrier(jnp.mean(vector * vector, axis=-1, keepdims=True)) + EPS) * scale_gain

def apply_rotation(vector, places):
    half_dim = vector.shape[-1] // 2
    inv_freq = THETA ** (-2.0 * jnp.arange(half_dim, dtype=jnp.float32) / vector.shape[-1])
    angles = places.astype(jnp.float32)[:, None] * inv_freq[None, :]
    cos_part = jnp.cos(angles)[:, None, :]
    sin_part = jnp.sin(angles)[:, None, :]
    lower_half = vector[..., :half_dim]
    upper_half = vector[..., half_dim:]
    return jnp.concatenate([lower_half * cos_part - upper_half * sin_part, upper_half * cos_part + lower_half * sin_part], axis=-1)

def attend_heads(query_rows, key_rows, value_rows, allowed):
    row_tally = query_rows.shape[0]
    group_rows = query_rows.reshape(row_tally, KEY_VALUE_HEADS, QUERY_HEADS // KEY_VALUE_HEADS, HEAD_SIZE).transpose(1, 0, 2, 3)
    score_scale = 1.0 / math.sqrt(HEAD_SIZE)

    def one_head(packed):
        query_head, key_head, value_head = packed
        scores = low_back(jnp.einsum('qgd,kd->gqk', query_head, key_head, precision=lax.Precision.HIGHEST) * score_scale)
        scores = jnp.where(allowed[None], scores, -jnp.inf)
        attn_probs = jax.nn.softmax(scores, axis=-1)
        return jnp.einsum('gqk,kd->qgd', low(attn_probs), value_head, precision=lax.Precision.HIGHEST)
    mixed_output = lax.map(jax.checkpoint(one_head), (group_rows, key_rows.transpose(1, 0, 2), value_rows.transpose(1, 0, 2)))
    return mixed_output.transpose(1, 0, 2, 3).reshape(row_tally, QUERY_HEADS, HEAD_SIZE)

def group_attention(packed):
    query_rows, key_rows, value_rows = packed
    places = jnp.arange(PROMPT_TOKENS, dtype=jnp.int32)
    causal = places[:, None] >= places[None, :]
    prompt_mix = attend_heads(query_rows[:PROMPT_TOKENS], key_rows[:PROMPT_TOKENS], value_rows[:PROMPT_TOKENS], causal)
    later = jnp.arange(CONTINUATION_LEN, dtype=jnp.int32)
    cont_mask = jnp.concatenate([jnp.ones((CONTINUATION_LEN, PROMPT_TOKENS), jnp.bool_), later[:, None] >= later[None, :]], axis=1)

    def single_continuation(piece):
        query_cont, key_cont, value_cont = piece
        return attend_heads(query_cont, jnp.concatenate([key_rows[:PROMPT_TOKENS], key_cont], axis=0), jnp.concatenate([value_rows[:PROMPT_TOKENS], value_cont], axis=0), cont_mask)
    continuation_mix = lax.map(jax.checkpoint(single_continuation), (query_rows[PROMPT_TOKENS:].reshape(CONTINUATIONS, CONTINUATION_LEN, QUERY_HEADS, HEAD_SIZE), key_rows[PROMPT_TOKENS:].reshape(CONTINUATIONS, CONTINUATION_LEN, KEY_VALUE_HEADS, HEAD_SIZE), value_rows[PROMPT_TOKENS:].reshape(CONTINUATIONS, CONTINUATION_LEN, KEY_VALUE_HEADS, HEAD_SIZE)))
    return jnp.concatenate([prompt_mix, continuation_mix.reshape(CONTINUATIONS * CONTINUATION_LEN, QUERY_HEADS, HEAD_SIZE)], axis=0)

def build_slots(routes):
    pair_count = TOK_DEV * TOPK
    per_device = routes.reshape(N_COL, N_ROW, pair_count).transpose(1, 0, 2).reshape(DEVICES, pair_count)
    expert_ids = jnp.arange(EXPERTS, dtype=jnp.int32)
    one_hot = (per_device[:, :, None] == expert_ids[None, None, :]).astype(jnp.int32)
    before = (jnp.cumsum(one_hot, axis=1) - one_hot).astype(jnp.int32)
    slot_of = lax.optimization_barrier(jnp.sum(before * one_hot, axis=2)).astype(jnp.int32)
    source = jnp.broadcast_to(jnp.arange(DEVICES, dtype=jnp.int32)[:, None], per_device.shape)
    pair_local = jnp.broadcast_to(jnp.arange(pair_count, dtype=jnp.int32)[None, :], per_device.shape)
    token_index = source % N_COL * GROUP_TOKENS + source // N_COL * TOK_DEV + pair_local // TOPK
    flat_pair = (token_index * TOPK + pair_local % TOPK).astype(jnp.int32)
    slot_grid = jnp.full((EXPERTS, DEVICES, CAP), GROUP_TOTAL * GROUP_TOKENS * TOPK, jnp.int32)
    slot_grid = slot_grid.at[per_device, source, slot_of].set(flat_pair)
    return slot_grid.reshape(EXPERTS, DEVICES * CAP)

def reference(layer_input, out_grad, routes, positions, w_q, key_value_weight, w_out, router, ln_attn, ln_moe, q_gain, k_gain, w_gate, w_up, w_down):
    token_count = GROUP_TOTAL * GROUP_TOKENS
    flat_routes = routes.reshape(token_count, TOPK)
    expert_ids = jnp.arange(EXPERTS, dtype=jnp.int32)
    counts = lax.optimization_barrier(jnp.sum((flat_routes.reshape(-1)[:, None] == expert_ids[None, :]).astype(jnp.float32), axis=0))
    slot_grid = build_slots(routes)
    flat_position = positions.reshape(token_count)
    q_width = QUERY_HEADS * HEAD_SIZE
    key_value_width = KEY_VALUE_HEADS * HEAD_SIZE

    def forward(inputs, weight_q, weight_kv, weight_out, weight_router, gain_one, gain_two, gain_q, key_gain, weight_gate, weight_up, weight_down):
        residual = inputs.reshape(token_count, MODEL_DIM)
        normed_one = low(row_norm(residual, gain_one))
        projected_q = low_back(exact_dot(normed_one, weight_q))
        key_value_projected = exact_dot(normed_one, weight_kv)
        query_rows = low(apply_rotation(row_norm(projected_q.reshape(token_count, QUERY_HEADS, HEAD_SIZE), gain_q), flat_position))
        key_rows = low(apply_rotation(row_norm(key_value_projected[:, :key_value_width].reshape(token_count, KEY_VALUE_HEADS, HEAD_SIZE), key_gain), flat_position))
        value_rows = low(key_value_projected[:, key_value_width:].reshape(token_count, KEY_VALUE_HEADS, HEAD_SIZE))
        mixed_output = lax.map(jax.checkpoint(group_attention), (query_rows.reshape(GROUP_TOTAL, GROUP_TOKENS, QUERY_HEADS, HEAD_SIZE), key_rows.reshape(GROUP_TOTAL, GROUP_TOKENS, KEY_VALUE_HEADS, HEAD_SIZE), value_rows.reshape(GROUP_TOTAL, GROUP_TOKENS, KEY_VALUE_HEADS, HEAD_SIZE)))
        attn_low = low_back(low(mixed_output.reshape(token_count, q_width)))
        hidden = residual + low_back(exact_dot(attn_low, weight_out))
        normed_two = low(row_norm(hidden, gain_two))
        logits = low_back(exact_dot(normed_two, weight_router))
        router_probs = jax.nn.softmax(logits, axis=-1)
        picked = jnp.take_along_axis(router_probs, flat_routes, axis=1)
        gates = picked / lax.optimization_barrier(jnp.sum(picked, axis=1, keepdims=True))
        padded_norm = jnp.concatenate([normed_two, jnp.zeros((1, MODEL_DIM), jnp.float32)], axis=0)
        padded_gates = jnp.concatenate([gates.reshape(-1), jnp.zeros((1,), jnp.float32)], axis=0)

        def expert_block(packed):
            pair_index, one_gate, one_up, one_down = packed
            rows_in = low_back(padded_norm[pair_index // TOPK])
            gate_pre = low_back(exact_dot(rows_in, one_gate))
            up_pre = low_back(exact_dot(rows_in, one_up))
            inner_act = low(jax.nn.silu(gate_pre) * up_pre)
            result = low_back(low(exact_dot(inner_act, one_down)))
            return result * padded_gates[pair_index][:, None]
        weighted = lax.map(jax.checkpoint(expert_block), (slot_grid, weight_gate, weight_up, weight_down))
        moe_sum = jnp.zeros((token_count + 1, MODEL_DIM), jnp.float32).at[(slot_grid // TOPK).reshape(-1)].add(weighted.reshape(-1, MODEL_DIM))
        layer_out = hidden + low_back(moe_sum[:token_count])
        mean_probs = lax.optimization_barrier(jnp.mean(router_probs, axis=0))
        aux_value = EXPERTS * jnp.sum(counts / (token_count * TOPK) * mean_probs)
        return (layer_out, aux_value, mean_probs)
    as_float = [member.astype(jnp.float32) for member in (layer_input, w_q, key_value_weight, w_out, router, ln_attn, ln_moe, q_gain, k_gain, w_gate, w_up, w_down)]
    (layer_out, aux_loss, mean_probs), pullback = jax.vjp(forward, *as_float)
    grads = pullback((out_grad.astype(jnp.float32).reshape(token_count, MODEL_DIM), jnp.float32(AUX_COEF), jnp.zeros((EXPERTS,), jnp.float32)))
    expert_load = jnp.stack([EXPERTS * counts / (token_count * TOPK), EXPERTS * mean_probs], axis=0)
    return (layer_out.astype(jnp.bfloat16).reshape(GROUP_TOTAL, GROUP_TOKENS, MODEL_DIM), aux_loss, grads[0], grads[1], grads[2], grads[3], grads[4], grads[5], grads[6], grads[7], grads[8], grads[9], grads[10], grads[11], expert_load)
```

```python
from functools import partial
import math

import jax
import jax.numpy as jnp
from jax import lax
from jax.experimental import pallas as pl
from jax.experimental.pallas import tpu as pltpu
from jax.sharding import PartitionSpec as P

QUERY_HEADS = 32
KEY_VALUE_HEADS = 4
HEAD = 128
TOPK = 8
CONT = 256
PROMPT_TOKENS = 2048

EPS = 1e-06
THETA = 1000000.0
AUX_COEF = 0.001
LN2 = math.log(2.0)
SCALE2 = 1.0 / (math.sqrt(HEAD) * LN2)
VMEM = 56 * 1024 * 1024

BF = jnp.bfloat16
F32 = jnp.float32


def dot_nn(a, b):
    return lax.dot_general(a, b, (((1,), (0,)), ((), ())), preferred_element_type=F32)


def dot_nt(a, b):
    return lax.dot_general(a, b, (((1,), (1,)), ((), ())), preferred_element_type=F32)


def dot_tn(a, b):
    return lax.dot_general(a, b, (((0,), (0,)), ((), ())), preferred_element_type=F32)


def call(body, name, grid, in_specs, out_specs, out_shape, scratch=(), flops=0, moved=0, prefetch=0):
    return pl.pallas_call(
        body,
        name=name,
        grid_spec=pltpu.PrefetchScalarGridSpec(
            num_scalar_prefetch=prefetch,
            grid=grid,
            in_specs=in_specs,
            out_specs=out_specs,
            scratch_shapes=list(scratch),
        ),
        out_shape=out_shape,
        cost_estimate=pl.CostEstimate(flops=int(flops), bytes_accessed=int(moved), transcendentals=0),
        compiler_params=pltpu.CompilerParams(
            dimension_semantics=("arbitrary",) * len(grid), vmem_limit_bytes=VMEM
        ),
    )


def struct(shape, dtype):
    return jax.ShapeDtypeStruct(shape, dtype)


def turn(v, cos, sin):
    return v * cos + pltpu.roll(v, HEAD // 2, 1) * sin


def turn_back(v, cos, sin):
    return v * cos + pltpu.roll(v * sin, HEAD // 2, 1)


def qkv_body(heads, x_ref, gain_ref, w_ref, cos_ref, sin_ref, qg_ref, kg_ref, q_ref, kv_ref, a_ref, r_ref):
    x = x_ref[...].astype(F32)
    normed = x * lax.rsqrt(jnp.mean(x * x, axis=-1, keepdims=True) + EPS) * gain_ref[...]
    low = normed.astype(BF)
    a_ref[...] = low
    raw = dot_nn(low, w_ref[...])
    cos = cos_ref[...]
    sin = sin_ref[...]
    lane = lax.broadcasted_iota(jnp.int32, (x.shape[0], HEAD), 1)
    scales = jnp.zeros((x.shape[0], HEAD), F32)
    for h in range(heads + 1):
        v = raw[:, h * HEAD : (h + 1) * HEAD]
        r = lax.rsqrt(jnp.mean(v * v, axis=-1, keepdims=True) + EPS)
        scales = jnp.where(lane == h, r, scales)
        if h < heads:
            q_ref[h] = (turn(v * r * qg_ref[...], cos, sin) * SCALE2).astype(BF)
        else:
            kv_ref[0] = turn(v * r * kg_ref[...], cos, sin).astype(BF)
    kv_ref[1] = raw[:, (heads + 1) * HEAD :].astype(BF)
    r_ref[...] = scales


def qkv(x, gain, w, cos, sin, qg, kg, heads):
    rows, width = x.shape
    cols = w.shape[1]
    tile = 256
    whole = lambda i: (0, 0)
    row = lambda i: (i, 0)
    return call(
        partial(qkv_body, heads),
        "qkv",
        (rows // tile,),
        [
            pl.BlockSpec((tile, width), row),
            pl.BlockSpec((1, width), whole),
            pl.BlockSpec((width, cols), whole),
            pl.BlockSpec((tile, HEAD), row),
            pl.BlockSpec((tile, HEAD), row),
            pl.BlockSpec((1, HEAD), whole),
            pl.BlockSpec((1, HEAD), whole),
        ],
        [
            pl.BlockSpec((heads, tile, HEAD), lambda i: (0, i, 0)),
            pl.BlockSpec((2, tile, HEAD), lambda i: (0, i, 0)),
            pl.BlockSpec((tile, width), row),
            pl.BlockSpec((tile, HEAD), row),
        ],
        [
            struct((heads, rows, HEAD), BF),
            struct((2, rows, HEAD), BF),
            struct((rows, width), BF),
            struct((rows, HEAD), F32),
        ],
        flops=2 * rows * width * cols,
        moved=2 * (2 * rows * width + width * cols + rows * cols),
    )(x, gain, w, cos, sin, qg, kg)


def causal(count):
    q_at = lax.broadcasted_iota(jnp.int32, (count, CONT, CONT), 1)
    k_at = lax.broadcasted_iota(jnp.int32, (count, CONT, CONT), 2)
    return (k_at <= q_at).reshape(count * CONT, CONT)


def attend_body(heads, per, blocks, rows, row_ref, q_ref, kp_ref, vp_ref, kv_ref, o_ref, l_ref, vp_one, vl_one, acc):
    at = pl.program_id(0)
    part = pl.program_id(1)
    row = row_ref[0]

    @pl.when((at == 0) & (part == 0))
    def _():
        for j in range(blocks):
            vp_one[j * rows : (j + 1) * rows, :HEAD] = vp_ref[j, 0, 0]
        vp_one[:, HEAD:] = jnp.ones((blocks * rows, HEAD), BF)
        vl_one[:, :HEAD] = kv_ref[1]
        vl_one[:, HEAD:] = jnp.ones((rows, HEAD), BF)

    q = q_ref[...].reshape(per * CONT, HEAD)
    here = pl.ds(pl.multiple_of(at * CONT, CONT), CONT)
    weights = jnp.where(causal(per), jnp.exp2(dot_nt(q, kv_ref[0, here, :])), 0.0).astype(BF)
    acc[...] = dot_nn(weights, vl_one[here, :])

    @pl.when(row < blocks)
    def _():
        for j in range(rows // CONT - 1):

            @pl.when(j < at)
            def _():
                piece = slice(j * CONT, (j + 1) * CONT)
                weights = jnp.exp2(dot_nt(q, kv_ref[0, piece, :])).astype(BF)
                acc[...] += dot_nn(weights, vl_one[piece, :])

    @pl.loop(0, jnp.minimum(row, blocks))
    def _(j):
        weights = jnp.exp2(dot_nt(q, kp_ref[j, 0, 0])).astype(BF)
        acc[...] += dot_nn(weights, vp_one[pl.ds(pl.multiple_of(j * rows, rows), rows), :])

    total = acc[:, HEAD:]
    out = (acc[:, :HEAD] / total).astype(BF)
    logs = jnp.log2(total)
    lane = lax.broadcasted_iota(jnp.int32, (CONT, HEAD), 1)

    @pl.when(part == 0)
    def _():
        l_ref[...] = jnp.zeros((CONT, HEAD), F32)

    held = l_ref[...]
    for p in range(per):
        o_ref[:, p * HEAD : (p + 1) * HEAD] = out[p * CONT : (p + 1) * CONT]
        held = jnp.where(lane == part * per + p, logs[p * CONT : (p + 1) * CONT], held)
    l_ref[...] = held


def attend(row, q, every, kv, slot, blocks):
    heads, rows, _ = q.shape
    per = 2
    keys = blocks * rows
    return call(
        partial(attend_body, heads, per, blocks, rows),
        "attend",
        (rows // CONT, heads // per),
        [
            pl.BlockSpec((per, CONT, HEAD), lambda i, h, s: (h, i, 0)),
            pl.BlockSpec((blocks, 1, 1, rows, HEAD), lambda i, h, s: (0, slot, 0, 0, 0)),
            pl.BlockSpec((blocks, 1, 1, rows, HEAD), lambda i, h, s: (0, slot, 1, 0, 0)),
            pl.BlockSpec((2, rows, HEAD), lambda i, h, s: (0, 0, 0)),
        ],
        [
            pl.BlockSpec((CONT, per * HEAD), lambda i, h, s: (i, h)),
            pl.BlockSpec((CONT, HEAD), lambda i, h, s: (i, 0)),
        ],
        [struct((rows, heads * HEAD), BF), struct((rows, HEAD), F32)],
        scratch=[
            pltpu.VMEM((keys, 2 * HEAD), BF),
            pltpu.VMEM((rows, 2 * HEAD), BF),
            pltpu.VMEM((per * CONT, 2 * HEAD), F32),
        ],
        flops=8 * rows * heads * (keys + CONT) * HEAD,
        moved=2 * HEAD * (2 * rows * heads + 2 * keys),
        prefetch=1,
    )(row, q, every, every, kv)


def attend_back_body(
    heads, per, blocks, rows,
    row_ref, q_ref, kp_ref, vp_ref, kv_ref, do_ref, o_ref, l_ref, r_ref, cos_ref, sin_ref, qg_ref,
    dq_ref, dp_ref, dl_ref, g_ref,
    dq, dkp, dvp,
):
    at = pl.program_id(0)
    part = pl.program_id(1)
    row = row_ref[0]

    @pl.when((at == 0) & (part == 0))
    def _():
        dkp[...] = jnp.zeros_like(dkp)
        dvp[...] = jnp.zeros_like(dvp)
        dl_ref[...] = jnp.zeros_like(dl_ref)
        g_ref[...] = jnp.zeros_like(g_ref)

    q = q_ref[...].reshape(per * CONT, HEAD)
    lane = lax.broadcasted_iota(jnp.int32, (CONT, HEAD), 1)
    do_parts, logs, centers, scales = [], [], [], []
    for p in range(per):
        do_part = do_ref[:, p * HEAD : (p + 1) * HEAD]
        do_parts.append(do_part)
        centers.append(
            jnp.sum(
                do_part.astype(F32) * o_ref[:, p * HEAD : (p + 1) * HEAD].astype(F32),
                axis=-1,
                keepdims=True,
            )
        )
        pick = lane == part * per + p
        logs.append(jnp.sum(jnp.where(pick, l_ref[...], 0.0), axis=-1, keepdims=True))
        scales.append(jnp.sum(jnp.where(pick, r_ref[...], 0.0), axis=-1, keepdims=True))
    do = jnp.concatenate(do_parts, axis=0)
    center = jnp.concatenate(centers, axis=0)
    log = jnp.concatenate(logs, axis=0)

    def block(k, v, mask):
        probs = jnp.exp2(dot_nt(q, k) - log)
        if mask is not None:
            probs = jnp.where(mask, probs, 0.0)
        ds = (probs * (dot_nt(do, v) - center)).astype(BF)
        return dot_nn(ds, k), dot_tn(ds, q), dot_tn(probs.astype(BF), do)

    here = pl.ds(pl.multiple_of(at * CONT, CONT), CONT)
    a, b, c = block(kv_ref[0, here, :], kv_ref[1, here, :], causal(per))
    dq[...] = a
    dl_ref[0, here, :] += b
    dl_ref[1, here, :] += c

    @pl.when(row < blocks)
    def _():
        for j in range(rows // CONT - 1):

            @pl.when(j < at)
            def _():
                piece = slice(j * CONT, (j + 1) * CONT)
                a, b, c = block(kv_ref[0, piece, :], kv_ref[1, piece, :], None)
                dq[...] += a
                dl_ref[0, piece, :] += b
                dl_ref[1, piece, :] += c

    @pl.loop(0, jnp.minimum(row, blocks))
    def _(j):
        a, b, c = block(kp_ref[j, 0, 0], vp_ref[j, 0, 0], None)
        piece = pl.ds(pl.multiple_of(j * rows, rows), rows)
        dq[...] += a
        dkp[piece, :] += b
        dvp[piece, :] += c

    cos = cos_ref[...]
    sin = sin_ref[...]
    gain = qg_ref[...]
    tally = jnp.zeros((1, HEAD), F32)
    for p in range(per):
        dy = turn_back(dq[p * CONT : (p + 1) * CONT, :] * (SCALE2 * LN2), cos, sin)
        hat = turn_back(q[p * CONT : (p + 1) * CONT].astype(F32), cos, sin) * (1.0 / SCALE2) / gain
        tally += jnp.sum(dy * hat, axis=0, keepdims=True)
        dyg = dy * gain
        raw = scales[p] * (dyg - hat * jnp.mean(dyg * hat, axis=-1, keepdims=True))
        dq_ref[:, p * HEAD : (p + 1) * HEAD] = raw.astype(BF)
    g_ref[0:1, :] += tally

    @pl.when((at == rows // CONT - 1) & (part == heads // per - 1))
    def _():
        dp_ref[0] = (dkp[...] * LN2).astype(BF)
        dp_ref[1] = dvp[...].astype(BF)
        dl_ref[0] = dl_ref[0] * LN2


def attend_back(row, q, every, kv, slot, blocks, do, o, logs, scales, cos, sin, qg):
    heads, rows, _ = q.shape
    per = 2
    keys = blocks * rows
    tile = lambda i, h, s: (i, 0)
    head = lambda i, h, s: (i, h)
    return call(
        partial(attend_back_body, heads, per, blocks, rows),
        "attend_back",
        (rows // CONT, heads // per),
        [
            pl.BlockSpec((per, CONT, HEAD), lambda i, h, s: (h, i, 0)),
            pl.BlockSpec((blocks, 1, 1, rows, HEAD), lambda i, h, s: (0, slot, 0, 0, 0)),
            pl.BlockSpec((blocks, 1, 1, rows, HEAD), lambda i, h, s: (0, slot, 1, 0, 0)),
            pl.BlockSpec((2, rows, HEAD), lambda i, h, s: (0, 0, 0)),
            pl.BlockSpec((CONT, per * HEAD), head),
            pl.BlockSpec((CONT, per * HEAD), head),
            pl.BlockSpec((CONT, HEAD), tile),
            pl.BlockSpec((CONT, HEAD), tile),
            pl.BlockSpec((CONT, HEAD), tile),
            pl.BlockSpec((CONT, HEAD), tile),
            pl.BlockSpec((1, HEAD), lambda i, h, s: (0, 0)),
        ],
        [
            pl.BlockSpec((CONT, per * HEAD), head),
            pl.BlockSpec((2, keys, HEAD), lambda i, h, s: (0, 0, 0)),
            pl.BlockSpec((2, rows, HEAD), lambda i, h, s: (0, 0, 0)),
            pl.BlockSpec((8, HEAD), lambda i, h, s: (0, 0)),
        ],
        [
            struct((rows, heads * HEAD), BF),
            struct((2, keys, HEAD), BF),
            struct((2, rows, HEAD), F32),
            struct((8, HEAD), F32),
        ],
        scratch=[
            pltpu.VMEM((per * CONT, HEAD), F32),
            pltpu.VMEM((keys, HEAD), F32),
            pltpu.VMEM((keys, HEAD), F32),
        ],
        flops=20 * rows * heads * (keys + CONT) * HEAD,
        moved=2 * HEAD * (4 * rows * heads + 4 * keys),
        prefetch=1,
    )(row, q, every, every, kv, do, o, logs, scales, cos, sin, qg)


def dispatch_body(count, cap, rank_ref, rows_ref, out_ref):
    tokens = rows_ref.shape[1]
    slot = lax.broadcasted_iota(jnp.int32, (cap, tokens), 0)
    for d in range(count):
        hot = (rank_ref[0, d : d + 1, :] == slot).astype(F32).astype(BF)
        out_ref[d, 0] = dot_nn(hot, rows_ref[0]).astype(BF)


def dispatch(rank, rows, cap):
    sources, count, tokens = rank.shape
    width = rows.shape[2]
    return call(
        partial(dispatch_body, count, cap),
        "dispatch",
        (sources,),
        [
            pl.BlockSpec((1, count, tokens), lambda s: (s, 0, 0)),
            pl.BlockSpec((1, tokens, width), lambda s: (s, 0, 0)),
        ],
        pl.BlockSpec((count, 1, cap, width), lambda s: (0, s, 0, 0)),
        struct((count, sources, cap, width), BF),
        flops=2 * sources * count * cap * tokens * width,
        moved=2 * sources * width * (tokens + count * cap),
    )(rank, rows)


def combine_body(count, cap, rank_ref, *refs):
    tokens = rank_ref.shape[1]
    slot = lax.broadcasted_iota(jnp.int32, (tokens, cap), 1)
    total = None
    for d in range(count):
        hot = (rank_ref[0, :, d : d + 1] == slot).astype(F32).astype(BF)
        piece = dot_nn(hot, refs[d][0])
        total = piece if total is None else total + piece
    refs[-1][0] = total.astype(BF)


def combine(rank_t, parts):
    sources, tokens, count = rank_t.shape
    _, cap, width = parts[0].shape
    return call(
        partial(combine_body, count, cap),
        "combine",
        (sources,),
        [pl.BlockSpec((1, tokens, count), lambda s: (s, 0, 0))]
        + [pl.BlockSpec((1, cap, width), lambda s: (s, 0, 0))] * count,
        pl.BlockSpec((1, tokens, width), lambda s: (s, 0, 0)),
        struct((sources, tokens, width), BF),
        flops=2 * sources * count * cap * tokens * width,
        moved=2 * sources * width * (tokens + count * cap),
    )(rank_t, *parts)


def expert_body(
    x_ref, up_ref, gate_ref, wg_ref, wu_ref, wd_ref,
    y_ref, db_ref, m_ref, du_ref, dw_ref, dg_ref,
):
    x = x_ref[0]
    gate = gate_ref[...]
    u = dot_nn(x, wg_ref[0])
    w = dot_nn(x, wu_ref[0])
    sigma = 1.0 / (1.0 + jnp.exp(-u))
    silu = u * sigma
    inner = silu * w
    low = inner.astype(BF)
    y_ref[...] = (dot_nn(low, wd_ref[0]) * gate).astype(BF)
    m_ref[...] = (inner * gate).astype(BF)
    back = dot_nt(up_ref[0], wd_ref[0])
    dg_ref[...] = jnp.sum(low.astype(F32) * back, axis=-1, keepdims=True)
    back = back * gate
    du = (back * w * sigma * (1.0 + u * (1.0 - sigma))).astype(BF)
    dw = (back * silu).astype(BF)
    du_ref[...] = du
    dw_ref[...] = dw
    db_ref[...] = (dot_nt(du, wg_ref[0]) + dot_nt(dw, wu_ref[0])).astype(BF)


def expert(slot, x, up, gate, wg, wu, wd):
    _, rows, width = x.shape
    hidden = wg.shape[2]
    tile = min(256, rows)
    at = lambda i: (i, 0)
    mine = lambda i: (slot, i, 0)
    whole = lambda i: (0, 0, 0)
    return call(
        expert_body,
        "expert",
        (rows // tile,),
        [
            pl.BlockSpec((1, tile, width), mine),
            pl.BlockSpec((1, tile, width), mine),
            pl.BlockSpec((tile, 1), at),
            pl.BlockSpec((1, width, hidden), whole),
            pl.BlockSpec((1, width, hidden), whole),
            pl.BlockSpec((1, hidden, width), whole),
        ],
        [
            pl.BlockSpec((tile, width), at),
            pl.BlockSpec((tile, width), at),
            pl.BlockSpec((tile, hidden), at),
            pl.BlockSpec((tile, hidden), at),
            pl.BlockSpec((tile, hidden), at),
            pl.BlockSpec((tile, 1), at),
        ],
        [
            struct((rows, width), BF),
            struct((rows, width), BF),
            struct((rows, hidden), BF),
            struct((rows, hidden), BF),
            struct((rows, hidden), BF),
            struct((rows, 1), F32),
        ],
        flops=12 * rows * width * hidden,
        moved=2 * (4 * rows * width + 3 * rows * hidden + 3 * width * hidden),
    )(x, up, gate, wg, wu, wd)


def swap(v, step, count):
    return lax.ppermute(v, "col", [(i, i ^ step) for i in range(count)])


def fetch(v, count):
    if count != 4:
        return [v] + [swap(v, d, count) for d in range(1, count)]
    half = v.shape[1] // 2
    one, two = swap(v, 1, count), swap(v, 2, count)
    first = swap(one[:, :half], 2, count)
    second = swap(two[:, half:], 1, count)
    return [v, one, two, jnp.concatenate([first, second], axis=1)]


def deliver(parts, count):
    own = parts[0]
    low = [None] + [p.astype(BF) for p in parts[1:]]
    if count != 4:
        for d in range(1, count):
            own = own + swap(low[d], d, count).astype(F32)
        return own
    half = own.shape[0] // 2
    to_two = swap(low[3][:half], 1, count)
    to_one = swap(low[3][half:], 2, count)
    one = jnp.concatenate([low[1][:half], (parts[1][half:] + to_one.astype(F32)).astype(BF)], axis=0)
    two = jnp.concatenate([(parts[2][:half] + to_two.astype(F32)).astype(BF), low[2][half:]], axis=0)
    return own + swap(one, 1, count).astype(F32) + swap(two, 2, count).astype(F32)


def after(value, *earlier):
    return lax.optimization_barrier((value,) + earlier)[0]


def per_device(
    layer_input, out_grad, routes, positions, w_q, key_value_weight, w_out, router,
    ln_attn, ln_moe, q_gain, k_gain, w_gate, w_up, w_down,
):
    rows, width = layer_input.shape[1:]
    row_count, col_count = lax.axis_size("row"), lax.axis_size("col")
    row_at, col_at = lax.axis_index("row"), lax.axis_index("col")
    devices = row_count * col_count
    experts = w_gate.shape[0] * devices
    assert w_gate.shape[0] == 1
    cap = rows * TOPK // experts
    tokens = rows * devices
    heads = w_q.shape[1] // HEAD
    sharing = QUERY_HEADS // KEY_VALUE_HEADS // heads
    blocks = PROMPT_TOKENS // rows
    slots = range(col_count)
    members = [col_at ^ d for d in slots]
    row_word = row_at.astype(jnp.int32).reshape(1)

    x_own = layer_input[0]
    up_own = out_grad[0]

    key_head = col_at // sharing
    kv_cols = KEY_VALUE_HEADS * HEAD
    wkv_mine = jnp.concatenate(
        [
            lax.dynamic_slice_in_dim(key_value_weight, key_head * HEAD, HEAD, 1),
            lax.dynamic_slice_in_dim(key_value_weight, kv_cols + key_head * HEAD, HEAD, 1),
        ],
        axis=1,
    )
    wide = jnp.concatenate([w_q, wkv_mine], axis=1)
    small = jnp.concatenate([ln_attn, ln_moe, q_gain, k_gain, router.reshape(-1)])
    small_all = lax.all_gather(small, "row", axis=0)
    wqkv = lax.all_gather(wide, "row", axis=0, tiled=True)
    piece, head_piece = ln_attn.shape[0], q_gain.shape[0]
    cuts = [0, piece, 2 * piece, 2 * piece + head_piece, 2 * piece + 2 * head_piece, small.shape[0]]
    gain_one, gain_two, gain_q, gain_k, router_all = [
        small_all[:, a:b].reshape(-1) for a, b in zip(cuts[:-1], cuts[1:])
    ]
    gain_one, gain_two = gain_one.astype(F32)[None], gain_two.astype(F32)[None]
    gain_q, gain_k = gain_q.astype(F32)[None], gain_k.astype(F32)[None]
    router_all = router_all.reshape(width, experts)

    xs = [x_own] + [swap(x_own, d, col_count) for d in slots[1:]]
    wg, wu, wd = after((w_gate, w_up, w_down), xs[-1])
    wg_all, wu_all, wd_all = fetch(wg, col_count), fetch(wu, col_count), fetch(wd, col_count)

    routes_all = lax.all_gather(routes[0], "row", axis=0)
    expert_ids = jnp.arange(experts, dtype=jnp.int32)
    flat_routes = routes_all.reshape(row_count * rows, TOPK).T
    mask_all = jnp.any(flat_routes[:, None, :] == expert_ids[None, :, None], axis=0)
    mine_ids = [row_at * col_count + m for m in members]
    has = jnp.stack(
        [lax.dynamic_index_in_dim(mask_all, e, 0, keepdims=False) for e in mine_ids], axis=0
    ).reshape(col_count, row_count, rows)
    place = jnp.arange(rows)
    before = (place[:, None] <= place[None, :]).astype(BF)
    order = jnp.einsum("drt,tu->rdu", has.astype(BF), before, preferred_element_type=F32)
    rank = jnp.where(has.transpose(1, 0, 2), order.astype(jnp.int32) - 1, -1)
    rank_t = rank.transpose(0, 2, 1)

    inv_freq = THETA ** (-2.0 * jnp.arange(HEAD // 2, dtype=F32) / HEAD)
    coses, sines = [], []
    for m in members:
        spots = lax.dynamic_index_in_dim(positions, m, 0, keepdims=False).astype(F32)
        angles = spots[:, None] * inv_freq[None, :]
        cos, sin = jnp.cos(angles), jnp.sin(angles)
        coses.append(jnp.concatenate([cos, cos], axis=1))
        sines.append(jnp.concatenate([-sin, sin], axis=1))

    qs, kvs, normed, scales = [], [], [], []
    for d in slots:
        a, b, c, e = qkv(xs[d], gain_one, wqkv, coses[d], sines[d], gain_q, gain_k, heads)
        qs.append(a)
        kvs.append(b)
        normed.append(c)
        scales.append(e)
    every = lax.all_gather(jnp.stack(kvs, axis=0), "row", axis=0)
    out_all = lax.all_gather(after(w_out, every), "row", axis=1, tiled=True)
    up_all = lax.all_gather(after(up_own, out_all), "row", axis=0)
    mixes, logs = [None] * col_count, [None] * col_count
    hidden = x_own.astype(F32)
    for d in reversed(slots):
        mixes[d], logs[d] = attend(row_word, qs[d], every, kvs[d], d, blocks)
        share = jnp.dot(mixes[d], out_all, preferred_element_type=F32)
        hidden = hidden + (share if d == 0 else swap(share.astype(BF), d, col_count).astype(F32))

    spread = lax.rsqrt(jnp.mean(hidden * hidden, axis=-1, keepdims=True) + EPS)
    second = (hidden * spread * gain_two).astype(BF)
    second_all = lax.all_gather(second, "row", axis=0)

    def route(vectors, mask):
        logits = lax.dot_general(
            router_all, vectors, (((0,), (1,)), ((), ())), preferred_element_type=F32
        )
        probs = jax.nn.softmax(logits, axis=0)
        picked = jnp.where(mask, probs, 0.0)
        total = jnp.sum(picked, axis=0, keepdims=True)
        return probs, total, picked / total

    probs_all, _, gates_all = route(second_all.reshape(row_count * rows, width), mask_all)
    sums = jnp.stack([jnp.sum(mask_all.astype(F32), axis=1), jnp.sum(probs_all, axis=1)])
    step = 1
    while step < col_count:
        sums = sums + swap(sums, step, col_count)
        step *= 2
    load = sums[0] / (tokens * TOPK)
    mean_probs = sums[1] / tokens
    aux_loss = experts * jnp.sum(load * mean_probs)
    expert_load = jnp.stack([experts * load, experts * mean_probs])

    expert_in = dispatch(rank, second_all, cap)
    expert_up = dispatch(rank, up_all, cap).reshape(col_count, row_count * cap, width)
    gates_mine = jnp.stack(
        [lax.dynamic_index_in_dim(gates_all, e, 0, keepdims=False) for e in mine_ids], axis=0
    ).reshape(col_count, row_count, rows)
    slot_ids = jnp.arange(cap, dtype=jnp.int32)
    hot = rank.transpose(1, 0, 2)[:, :, None, :] == slot_ids[None, None, :, None]
    gate_pairs = jnp.sum(jnp.where(hot, gates_mine[:, :, None, :], 0.0), axis=-1)
    gate_pairs = gate_pairs.reshape(col_count, row_count * cap, 1)
    expert_in = expert_in.reshape(col_count, row_count * cap, width)
    ys, dbs, ms, dus, dws, dgs = [], [], [], [], [], []
    for d in slots:
        got = expert(d, expert_in, expert_up, gate_pairs[d], wg_all[d], wu_all[d], wd_all[d])
        for kept, value in zip((ys, dbs, ms, dus, dws, dgs), got):
            kept.append(value)
    cut = lambda parts: [p.reshape(row_count, cap, width) for p in parts]
    db_sum = lax.psum_scatter(combine(rank_t, cut(dbs)), "row", scatter_dimension=0)
    pair_scores = jnp.stack(dgs, axis=0).reshape(col_count, row_count, cap, 1)
    score_grads = jnp.sum(jnp.where(hot, pair_scores, 0.0), axis=2)
    score_grads = lax.all_to_all(
        score_grads.transpose(1, 0, 2), "row", split_axis=0, concat_axis=0, tiled=True
    )
    y_sum = lax.psum_scatter(
        after(combine(rank_t, cut(ys)), db_sum), "row", scatter_dimension=0
    )
    layer_output = (hidden + y_sum.astype(F32)).astype(BF)

    grad_down = deliver(
        [dot_tn(ms[d], expert_up[d]) for d in slots], col_count
    )
    grad_gate = deliver([dot_tn(expert_in[d], dus[d]) for d in slots], col_count)
    grad_up = deliver([dot_tn(expert_in[d], dws[d]) for d in slots], col_count)

    mask_own = jnp.any(routes[0].T[:, None, :] == expert_ids[None, :, None], axis=0)
    probs, total, gates = route(second, mask_own)
    to_member = jnp.stack(members)[:, None] == jnp.arange(col_count)[None, :]
    gate_grad = jnp.sum(
        jnp.where(to_member[None, :, :, None], score_grads[:, :, None, :], 0.0), axis=1
    ).reshape(experts, rows)
    weighted = jnp.sum(gate_grad * gates, axis=0, keepdims=True)
    prob_grad = (
        jnp.where(mask_own, (gate_grad - weighted) / total, 0.0)
        + AUX_COEF * experts * load[:, None] / tokens
    )
    logit_low = (probs * (prob_grad - jnp.sum(probs * prob_grad, axis=0, keepdims=True))).astype(BF)
    grad_router = lax.dot_general(
        second, logit_low, (((0,), (1,)), ((), ())), preferred_element_type=F32
    )
    second_grad = db_sum.astype(F32) + lax.dot_general(
        logit_low, router_all, (((0,), (1,)), ((), ())), preferred_element_type=F32
    )

    def norm_back(grad, hat, spread, gain):
        scaled = grad * gain
        return spread * (scaled - hat * jnp.mean(scaled * hat, axis=-1, keepdims=True))

    hat = hidden * spread
    gain_two_grad = jnp.sum(second_grad * hat, axis=0)
    hidden_grad = up_own.astype(F32) + norm_back(second_grad, hat, spread, gain_two)
    branch = hidden_grad.astype(BF)
    early = jnp.concatenate(
        [grad_router.reshape(devices, -1), gain_two_grad.reshape(devices, -1)], axis=1
    )
    early = lax.psum_scatter(early, ("row", "col"), scatter_dimension=0)

    branches = [branch] + [swap(branch, d, col_count) for d in slots[1:]]
    grad_qs, grad_prompts, grad_locals, gain_q_grad = [], [], [], 0.0
    for d in slots:
        mix_grad = dot_nt(branches[d], out_all).astype(BF)
        a, b, c, e = attend_back(
            row_word, qs[d], every, kvs[d], d, blocks, mix_grad, mixes[d], logs[d], scales[d],
            coses[d], sines[d], gain_q,
        )
        grad_qs.append(a)
        grad_prompts.append(b)
        grad_locals.append(c)
        gain_q_grad = gain_q_grad + e[0]
    prompt = lax.psum_scatter(
        jnp.stack(grad_prompts, axis=0), "row", scatter_dimension=2, tiled=True
    )
    chunk = prompt.shape[2]
    prompt = jnp.concatenate(
        [
            lax.ppermute(prompt, "row", [(rows // chunk * i + a, i) for i in range(blocks)])
            for a in range(rows // chunk)
        ],
        axis=2,
    )
    pair = jnp.stack(grad_locals, axis=0) + prompt.astype(F32)
    cos, sin = jnp.stack(coses), jnp.stack(sines)

    def back_turn(v):
        moved = v * sin
        half = HEAD // 2
        return v * cos + jnp.concatenate([moved[..., half:], moved[..., :half]], axis=-1)

    key_dy = back_turn(pair[:, 0])
    key_hat = back_turn(jnp.stack([kv[0] for kv in kvs]).astype(F32)) / gain_k
    gain_k_grad = jnp.sum(key_dy * key_hat, axis=(0, 1))
    key_spread = jnp.stack([s[:, heads : heads + 1] for s in scales])
    key_raw = norm_back(key_dy, key_hat, key_spread, gain_k)
    all_grads = jnp.concatenate(
        [jnp.stack(grad_qs, axis=0), key_raw.astype(BF), pair[:, 1].astype(BF)], axis=2
    )
    input_sum = None
    for d in reversed(slots):
        share = dot_nt(all_grads[d], wqkv)
        share = share if d == 0 else swap(share.astype(BF), d, col_count).astype(F32)
        input_sum = share if input_sum is None else input_sum + share
    grad_wide = lax.dot_general(
        jnp.stack(normed, axis=0), all_grads, (((0, 1), (0, 1)), ((), ())), preferred_element_type=F32
    )
    grad_wide = lax.psum_scatter(grad_wide.astype(BF), "row", scatter_dimension=0, tiled=True)
    grad_out = lax.dot_general(
        jnp.stack(mixes, axis=0),
        jnp.stack(branches, axis=0),
        (((0, 1), (0, 1)), ((), ())),
        preferred_element_type=F32,
    )
    grad_out = lax.psum_scatter(grad_out.astype(BF), "row", scatter_dimension=1, tiled=True)
    x_wide = x_own.astype(F32)
    x_spread = lax.rsqrt(jnp.mean(x_wide * x_wide, axis=-1, keepdims=True) + EPS)
    x_hat = x_wide * x_spread
    gain_one_grad = jnp.sum(input_sum * x_hat, axis=0)
    input_grad = hidden_grad + norm_back(input_sum, x_hat, x_spread, gain_one)

    late = jnp.concatenate(
        [v.reshape(devices, -1) for v in (gain_one_grad, gain_q_grad, gain_k_grad)], axis=1
    )
    late = lax.psum_scatter(late, ("row", "col"), scatter_dimension=0)
    per_one, per_q = gain_one_grad.size // devices, gain_q_grad.size // devices

    grad_kv = grad_wide[:, heads * HEAD :].astype(F32).reshape(col_count, -1, 2 * HEAD)
    grad_kv = lax.all_to_all(grad_kv, "col", split_axis=0, concat_axis=0, tiled=True)
    grad_kv = grad_kv.reshape(KEY_VALUE_HEADS, sharing, -1, 2, HEAD).sum(axis=1)
    grad_kv = grad_kv.transpose(1, 2, 0, 3).reshape(-1, 2 * kv_cols)

    return (
        layer_output[None],
        aux_loss,
        input_grad[None],
        grad_wide[:, : heads * HEAD].astype(F32),
        grad_kv,
        grad_out.astype(F32),
        early[: -(width // devices)].reshape(width // devices, experts),
        late[:per_one],
        early[-(width // devices) :],
        late[per_one : per_one + per_q],
        late[per_one + per_q :],
        grad_gate[None],
        grad_up[None],
        grad_down[None],
        expert_load,
    )


def solution(mesh):
    in_specs = (
        P("col", "row", None),
        P("col", "row", None),
        P("col", "row", None),
        P(None, "row"),
        P("row", "col"),
        P("row", None),
        P("col", "row"),
        P("row", None),
        P("row"),
        P("row"),
        P("row"),
        P("row"),
        P(("row", "col"), None, None),
        P(("row", "col"), None, None),
        P(("row", "col"), None, None),
    )
    out_specs = (
        P("col", "row", None),
        P(),
        P("col", "row", None),
        P("row", "col"),
        P(("row", "col"), None),
        P("col", "row"),
        P(("row", "col"), None),
        P(("row", "col")),
        P(("row", "col")),
        P(("row", "col")),
        P(("row", "col")),
        P(("row", "col"), None, None),
        P(("row", "col"), None, None),
        P(("row", "col"), None, None),
        P(),
    )
    return jax.shard_map(
        per_device, mesh=mesh, in_specs=in_specs, out_specs=out_specs, check_vma=False
    )
```

```python
from functools import partial
import math

import jax
import jax.numpy as jnp
from jax import lax
from jax.experimental import pallas as pl
from jax.experimental.pallas import tpu as pltpu
from jax.sharding import PartitionSpec as P

QUERY_HEADS = 32
KEY_VALUE_HEADS = 4
HEAD = 128
TOPK = 8
CONT = 256
PROMPT_TOKENS = 2048

EPS = 1e-06
THETA = 1000000.0
AUX_COEF = 0.001
LN2 = math.log(2.0)
SCALE2 = 1.0 / (math.sqrt(HEAD) * LN2)
VMEM = 56 * 1024 * 1024

BF = jnp.bfloat16
F32 = jnp.float32


def dot_nn(a, b):
    return lax.dot_general(a, b, (((1,), (0,)), ((), ())), preferred_element_type=F32)


def dot_nt(a, b):
    return lax.dot_general(a, b, (((1,), (1,)), ((), ())), preferred_element_type=F32)


def dot_tn(a, b):
    return lax.dot_general(a, b, (((0,), (0,)), ((), ())), preferred_element_type=F32)


def call(body, name, grid, in_specs, out_specs, out_shape, scratch=(), flops=0, moved=0, prefetch=0):
    return pl.pallas_call(
        body,
        name=name,
        grid_spec=pltpu.PrefetchScalarGridSpec(
            num_scalar_prefetch=prefetch,
            grid=grid,
            in_specs=in_specs,
            out_specs=out_specs,
            scratch_shapes=list(scratch),
        ),
        out_shape=out_shape,
        cost_estimate=pl.CostEstimate(flops=int(flops), bytes_accessed=int(moved), transcendentals=0),
        compiler_params=pltpu.CompilerParams(
            dimension_semantics=("arbitrary",) * len(grid), vmem_limit_bytes=VMEM
        ),
    )


def struct(shape, dtype):
    return jax.ShapeDtypeStruct(shape, dtype)


def turn(v, cos, sin):
    return v * cos + pltpu.roll(v, HEAD // 2, 1) * sin


def turn_back(v, cos, sin):
    return v * cos + pltpu.roll(v * sin, HEAD // 2, 1)


def qkv_body(heads, x_ref, gain_ref, w_ref, cos_ref, sin_ref, qg_ref, kg_ref, q_ref, kv_ref, a_ref, r_ref):
    x = x_ref[...].astype(F32)
    normed = x * lax.rsqrt(jnp.mean(x * x, axis=-1, keepdims=True) + EPS) * gain_ref[...]
    low = normed.astype(BF)
    a_ref[...] = low
    raw = dot_nn(low, w_ref[...])
    cos = cos_ref[...]
    sin = sin_ref[...]
    lane = lax.broadcasted_iota(jnp.int32, (x.shape[0], HEAD), 1)
    scales = jnp.zeros((x.shape[0], HEAD), F32)
    for h in range(heads + 1):
        v = raw[:, h * HEAD : (h + 1) * HEAD]
        r = lax.rsqrt(jnp.mean(v * v, axis=-1, keepdims=True) + EPS)
        scales = jnp.where(lane == h, r, scales)
        if h < heads:
            q_ref[h] = (turn(v * r * qg_ref[...], cos, sin) * SCALE2).astype(BF)
        else:
            kv_ref[0] = turn(v * r * kg_ref[...], cos, sin).astype(BF)
    kv_ref[1] = raw[:, (heads + 1) * HEAD :].astype(BF)
    r_ref[...] = scales


def qkv(x, gain, w, cos, sin, qg, kg, heads):
    rows, width = x.shape
    cols = (heads + 2) * HEAD
    tile = 256
    whole = lambda i: (0, 0)
    row = lambda i: (i, 0)
    return call(
        partial(qkv_body, heads),
        "qkv",
        (rows // tile,),
        [
            pl.BlockSpec((tile, width), row),
            pl.BlockSpec((1, width), whole),
            pl.BlockSpec((width, cols), whole),
            pl.BlockSpec((tile, HEAD), row),
            pl.BlockSpec((tile, HEAD), row),
            pl.BlockSpec((1, HEAD), whole),
            pl.BlockSpec((1, HEAD), whole),
        ],
        [
            pl.BlockSpec((heads, tile, HEAD), lambda i: (0, i, 0)),
            pl.BlockSpec((2, tile, HEAD), lambda i: (0, i, 0)),
            pl.BlockSpec((tile, width), row),
            pl.BlockSpec((tile, HEAD), row),
        ],
        [
            struct((heads, rows, HEAD), BF),
            struct((2, rows, HEAD), BF),
            struct((rows, width), BF),
            struct((rows, HEAD), F32),
        ],
        flops=2 * rows * width * cols,
        moved=2 * (2 * rows * width + width * cols + rows * cols),
    )(x, gain, w, cos, sin, qg, kg)


def causal(count):
    q_at = lax.broadcasted_iota(jnp.int32, (count, CONT, CONT), 1)
    k_at = lax.broadcasted_iota(jnp.int32, (count, CONT, CONT), 2)
    return (k_at <= q_at).reshape(count * CONT, CONT)


def attend_body(heads, per, blocks, rows, row_ref, q_ref, kp_ref, vp_ref, kv_ref, o_ref, l_ref, vp_one, vl_one, acc):
    at = pl.program_id(0)
    part = pl.program_id(1)
    row = row_ref[0]

    @pl.when((at == 0) & (part == 0))
    def _():
        for j in range(blocks):
            vp_one[j * rows : (j + 1) * rows, :HEAD] = vp_ref[j, 0]
        vp_one[:, HEAD:] = jnp.ones((blocks * rows, HEAD), BF)
        vl_one[:, :HEAD] = kv_ref[1]
        vl_one[:, HEAD:] = jnp.ones((rows, HEAD), BF)

    q = q_ref[...].reshape(per * CONT, HEAD)
    here = pl.ds(pl.multiple_of(at * CONT, CONT), CONT)
    weights = jnp.where(causal(per), jnp.exp2(dot_nt(q, kv_ref[0, here, :])), 0.0).astype(BF)
    acc[...] = dot_nn(weights, vl_one[here, :])

    @pl.when(row < blocks)
    def _():
        for j in range(rows // CONT - 1):

            @pl.when(j < at)
            def _():
                piece = slice(j * CONT, (j + 1) * CONT)
                weights = jnp.exp2(dot_nt(q, kv_ref[0, piece, :])).astype(BF)
                acc[...] += dot_nn(weights, vl_one[piece, :])

    @pl.loop(0, jnp.minimum(row, blocks))
    def _(j):
        weights = jnp.exp2(dot_nt(q, kp_ref[j, 0])).astype(BF)
        acc[...] += dot_nn(weights, vp_one[pl.ds(pl.multiple_of(j * rows, rows), rows), :])

    total = acc[:, HEAD:]
    out = (acc[:, :HEAD] / total).astype(BF)
    logs = jnp.log2(total)
    lane = lax.broadcasted_iota(jnp.int32, (CONT, HEAD), 1)

    @pl.when(part == 0)
    def _():
        l_ref[...] = jnp.zeros((CONT, HEAD), F32)

    held = l_ref[...]
    for p in range(per):
        o_ref[:, p * HEAD : (p + 1) * HEAD] = out[p * CONT : (p + 1) * CONT]
        held = jnp.where(lane == part * per + p, logs[p * CONT : (p + 1) * CONT], held)
    l_ref[...] = held


def attend(row, q, every, kv, blocks):
    heads, rows, _ = q.shape
    per = 2
    keys = blocks * rows
    return call(
        partial(attend_body, heads, per, blocks, rows),
        "attend",
        (rows // CONT, heads // per),
        [
            pl.BlockSpec((per, CONT, HEAD), lambda i, h, s: (h, i, 0)),
            pl.BlockSpec((blocks, 1, rows, HEAD), lambda i, h, s: (0, 0, 0, 0)),
            pl.BlockSpec((blocks, 1, rows, HEAD), lambda i, h, s: (0, 1, 0, 0)),
            pl.BlockSpec((2, rows, HEAD), lambda i, h, s: (0, 0, 0)),
        ],
        [
            pl.BlockSpec((CONT, per * HEAD), lambda i, h, s: (i, h)),
            pl.BlockSpec((CONT, HEAD), lambda i, h, s: (i, 0)),
        ],
        [struct((rows, heads * HEAD), BF), struct((rows, HEAD), F32)],
        scratch=[
            pltpu.VMEM((keys, 2 * HEAD), BF),
            pltpu.VMEM((rows, 2 * HEAD), BF),
            pltpu.VMEM((per * CONT, 2 * HEAD), F32),
        ],
        flops=8 * rows * heads * (keys + CONT) * HEAD,
        moved=2 * HEAD * (2 * rows * heads + 2 * keys),
        prefetch=1,
    )(row, q, every, every, kv)


def attend_back_body(
    heads, per, blocks, rows,
    row_ref, q_ref, kp_ref, vp_ref, kv_ref, do_ref, o_ref, l_ref, r_ref, cos_ref, sin_ref, qg_ref,
    dq_ref, dp_ref, dl_ref, g_ref,
    dq, dkp, dvp,
):
    at = pl.program_id(0)
    part = pl.program_id(1)
    row = row_ref[0]

    @pl.when((at == 0) & (part == 0))
    def _():
        dkp[...] = jnp.zeros_like(dkp)
        dvp[...] = jnp.zeros_like(dvp)
        dl_ref[...] = jnp.zeros_like(dl_ref)
        g_ref[...] = jnp.zeros_like(g_ref)

    q = q_ref[...].reshape(per * CONT, HEAD)
    lane = lax.broadcasted_iota(jnp.int32, (CONT, HEAD), 1)
    do_parts, logs, centers, scales = [], [], [], []
    for p in range(per):
        do_part = do_ref[:, p * HEAD : (p + 1) * HEAD]
        do_parts.append(do_part)
        centers.append(
            jnp.sum(
                do_part.astype(F32) * o_ref[:, p * HEAD : (p + 1) * HEAD].astype(F32),
                axis=-1,
                keepdims=True,
            )
        )
        pick = lane == part * per + p
        logs.append(jnp.sum(jnp.where(pick, l_ref[...], 0.0), axis=-1, keepdims=True))
        scales.append(jnp.sum(jnp.where(pick, r_ref[...], 0.0), axis=-1, keepdims=True))
    do = jnp.concatenate(do_parts, axis=0)
    center = jnp.concatenate(centers, axis=0)
    log = jnp.concatenate(logs, axis=0)

    def block(k, v, mask):
        probs = jnp.exp2(dot_nt(q, k) - log)
        if mask is not None:
            probs = jnp.where(mask, probs, 0.0)
        ds = (probs * (dot_nt(do, v) - center)).astype(BF)
        return dot_nn(ds, k), dot_tn(ds, q), dot_tn(probs.astype(BF), do)

    here = pl.ds(pl.multiple_of(at * CONT, CONT), CONT)
    a, b, c = block(kv_ref[0, here, :], kv_ref[1, here, :], causal(per))
    dq[...] = a
    dl_ref[0, here, :] += b
    dl_ref[1, here, :] += c

    @pl.when(row < blocks)
    def _():
        for j in range(rows // CONT - 1):

            @pl.when(j < at)
            def _():
                piece = slice(j * CONT, (j + 1) * CONT)
                a, b, c = block(kv_ref[0, piece, :], kv_ref[1, piece, :], None)
                dq[...] += a
                dl_ref[0, piece, :] += b
                dl_ref[1, piece, :] += c

    @pl.loop(0, jnp.minimum(row, blocks))
    def _(j):
        a, b, c = block(kp_ref[j, 0], vp_ref[j, 0], None)
        piece = pl.ds(pl.multiple_of(j * rows, rows), rows)
        dq[...] += a
        dkp[piece, :] += b
        dvp[piece, :] += c

    cos = cos_ref[...]
    sin = sin_ref[...]
    gain = qg_ref[...]
    tally = jnp.zeros((1, HEAD), F32)
    for p in range(per):
        dy = turn_back(dq[p * CONT : (p + 1) * CONT, :] * (SCALE2 * LN2), cos, sin)
        hat = turn_back(q[p * CONT : (p + 1) * CONT].astype(F32), cos, sin) * (1.0 / SCALE2) / gain
        tally += jnp.sum(dy * hat, axis=0, keepdims=True)
        dyg = dy * gain
        raw = scales[p] * (dyg - hat * jnp.mean(dyg * hat, axis=-1, keepdims=True))
        dq_ref[:, p * HEAD : (p + 1) * HEAD] = raw.astype(BF)
    g_ref[0:1, :] += tally

    @pl.when((at == rows // CONT - 1) & (part == heads // per - 1))
    def _():
        dp_ref[0] = (dkp[...] * LN2).astype(BF)
        dp_ref[1] = dvp[...].astype(BF)
        dl_ref[0] = dl_ref[0] * LN2


def attend_back(row, q, every, kv, blocks, do, o, logs, scales, cos, sin, qg):
    heads, rows, _ = q.shape
    per = 2
    keys = blocks * rows
    tile = lambda i, h, s: (i, 0)
    head = lambda i, h, s: (i, h)
    return call(
        partial(attend_back_body, heads, per, blocks, rows),
        "attend_back",
        (rows // CONT, heads // per),
        [
            pl.BlockSpec((per, CONT, HEAD), lambda i, h, s: (h, i, 0)),
            pl.BlockSpec((blocks, 1, rows, HEAD), lambda i, h, s: (0, 0, 0, 0)),
            pl.BlockSpec((blocks, 1, rows, HEAD), lambda i, h, s: (0, 1, 0, 0)),
            pl.BlockSpec((2, rows, HEAD), lambda i, h, s: (0, 0, 0)),
            pl.BlockSpec((CONT, per * HEAD), head),
            pl.BlockSpec((CONT, per * HEAD), head),
            pl.BlockSpec((CONT, HEAD), tile),
            pl.BlockSpec((CONT, HEAD), tile),
            pl.BlockSpec((CONT, HEAD), tile),
            pl.BlockSpec((CONT, HEAD), tile),
            pl.BlockSpec((1, HEAD), lambda i, h, s: (0, 0)),
        ],
        [
            pl.BlockSpec((CONT, per * HEAD), head),
            pl.BlockSpec((2, keys, HEAD), lambda i, h, s: (0, 0, 0)),
            pl.BlockSpec((2, rows, HEAD), lambda i, h, s: (0, 0, 0)),
            pl.BlockSpec((8, HEAD), lambda i, h, s: (0, 0)),
        ],
        [
            struct((rows, heads * HEAD), BF),
            struct((2, keys, HEAD), BF),
            struct((2, rows, HEAD), F32),
            struct((8, HEAD), F32),
        ],
        scratch=[
            pltpu.VMEM((per * CONT, HEAD), F32),
            pltpu.VMEM((keys, HEAD), F32),
            pltpu.VMEM((keys, HEAD), F32),
        ],
        flops=20 * rows * heads * (keys + CONT) * HEAD,
        moved=2 * HEAD * (4 * rows * heads + 4 * keys),
        prefetch=1,
    )(row, q, every, every, kv, do, o, logs, scales, cos, sin, qg)


def dispatch_body(count, cap, rank_ref, rows_ref, out_ref):
    tokens = rows_ref.shape[1]
    slot = lax.broadcasted_iota(jnp.int32, (cap, tokens), 0)
    for d in range(count):
        hot = (rank_ref[0, d : d + 1, :] == slot).astype(F32).astype(BF)
        out_ref[d, 0] = dot_nn(hot, rows_ref[0]).astype(BF)


def dispatch(rank, rows, cap):
    sources, count, tokens = rank.shape
    width = rows.shape[2]
    return call(
        partial(dispatch_body, count, cap),
        "dispatch",
        (sources,),
        [
            pl.BlockSpec((1, count, tokens), lambda s: (s, 0, 0)),
            pl.BlockSpec((1, tokens, width), lambda s: (s, 0, 0)),
        ],
        pl.BlockSpec((count, 1, cap, width), lambda s: (0, s, 0, 0)),
        struct((count, sources, cap, width), BF),
        flops=2 * sources * count * cap * tokens * width,
        moved=2 * sources * width * (tokens + count * cap),
    )(rank, rows)


def route_body(count, cap, ids_ref, rank_ref, rows_ref, mask_ref, router_ref, out_ref, probs_ref, gate_ref):
    tokens = rows_ref.shape[1]
    rows = rows_ref[0]
    logits = dot_nt(router_ref[...], rows)
    weights = jnp.exp(logits - jnp.max(logits, axis=0, keepdims=True))
    probs = weights / jnp.sum(weights, axis=0, keepdims=True)
    probs_ref[0] = probs
    picked = probs * mask_ref[0]
    gates = picked / jnp.sum(picked, axis=0, keepdims=True)
    expert_at = lax.broadcasted_iota(jnp.int32, gates.shape, 0)
    slot = lax.broadcasted_iota(jnp.int32, (cap, tokens), 0)
    for d in range(count):
        here = rank_ref[0, d : d + 1, :] == slot
        out_ref[d, 0] = dot_nn(here.astype(F32).astype(BF), rows).astype(BF)
        mine = jnp.sum(jnp.where(expert_at == ids_ref[d], gates, 0.0), axis=0, keepdims=True)
        gate_ref[d, 0] = jnp.sum(jnp.where(here, mine, 0.0), axis=1, keepdims=True)


def route_dispatch(ids, rank, rows, mask, router, cap):
    sources, count, tokens = rank.shape
    width = rows.shape[2]
    experts = router.shape[0]
    return call(
        partial(route_body, count, cap),
        "route_dispatch",
        (sources,),
        [
            pl.BlockSpec((1, count, tokens), lambda s, i: (s, 0, 0)),
            pl.BlockSpec((1, tokens, width), lambda s, i: (s, 0, 0)),
            pl.BlockSpec((1, experts, tokens), lambda s, i: (s, 0, 0)),
            pl.BlockSpec((experts, width), lambda s, i: (0, 0)),
        ],
        [
            pl.BlockSpec((count, 1, cap, width), lambda s, i: (0, s, 0, 0)),
            pl.BlockSpec((1, experts, tokens), lambda s, i: (s, 0, 0)),
            pl.BlockSpec((count, 1, cap, 1), lambda s, i: (0, s, 0, 0)),
        ],
        [
            struct((count, sources, cap, width), BF),
            struct((sources, experts, tokens), F32),
            struct((count, sources, cap, 1), F32),
        ],
        flops=2 * sources * count * cap * tokens * width,
        moved=2 * sources * width * (tokens + count * cap),
        prefetch=1,
    )(ids, rank, rows, mask, router)


def share_body(g_ref, w_ref, a_ref, out_ref, sum_ref):
    share = dot_nt(g_ref[...], w_ref[...])
    out_ref[...] = share.astype(out_ref.dtype)

    @pl.when(pl.program_id(0) == 0)
    def _():
        sum_ref[...] = jnp.zeros_like(sum_ref)

    sum_ref[0:1, :] += jnp.sum(share * a_ref[...].astype(F32), axis=0, keepdims=True)


def input_share(grads, w, normed, dtype):
    rows, cols = grads.shape
    width = w.shape[0]
    tile = 256
    return call(
        share_body,
        "input_share",
        (rows // tile,),
        [
            pl.BlockSpec((tile, cols), lambda i: (i, 0)),
            pl.BlockSpec((width, cols), lambda i: (0, 0)),
            pl.BlockSpec((tile, width), lambda i: (i, 0)),
        ],
        [pl.BlockSpec((tile, width), lambda i: (i, 0)), pl.BlockSpec((8, width), lambda i: (0, 0))],
        [struct((rows, width), dtype), struct((8, width), F32)],
        flops=2 * rows * width * cols,
        moved=2 * (2 * rows * width + width * cols + rows * cols),
    )(grads, w, normed)


def combine_body(count, cap, rank_ref, *refs):
    tokens = rank_ref.shape[1]
    slot = lax.broadcasted_iota(jnp.int32, (tokens, cap), 1)
    total = None
    for d in range(count):
        hot = (rank_ref[0, :, d : d + 1] == slot).astype(F32).astype(BF)
        piece = dot_nn(hot, refs[d][0])
        total = piece if total is None else total + piece
    refs[-1][0] = total.astype(BF)


def combine(rank_t, parts):
    sources, tokens, count = rank_t.shape
    _, cap, width = parts[0].shape
    return call(
        partial(combine_body, count, cap),
        "combine",
        (sources,),
        [pl.BlockSpec((1, tokens, count), lambda s: (s, 0, 0))]
        + [pl.BlockSpec((1, cap, width), lambda s: (s, 0, 0))] * count,
        pl.BlockSpec((1, tokens, width), lambda s: (s, 0, 0)),
        struct((sources, tokens, width), BF),
        flops=2 * sources * count * cap * tokens * width,
        moved=2 * sources * width * (tokens + count * cap),
    )(rank_t, *parts)


def expert_body(
    x_ref, up_ref, gate_ref, wg_ref, wu_ref, wd_ref,
    y_ref, db_ref, m_ref, du_ref, dw_ref, dg_ref,
):
    x = x_ref[0]
    gate = gate_ref[...]
    u = dot_nn(x, wg_ref[0])
    w = dot_nn(x, wu_ref[0])
    sigma = 1.0 / (1.0 + jnp.exp(-u))
    silu = u * sigma
    inner = silu * w
    low = inner.astype(BF)
    y_ref[...] = (dot_nn(low, wd_ref[0]) * gate).astype(BF)
    m_ref[...] = (inner * gate).astype(BF)
    back = dot_nt(up_ref[0], wd_ref[0])
    dg_ref[...] = jnp.sum(low.astype(F32) * back, axis=-1, keepdims=True)
    back = back * gate
    du = (back * w * sigma * (1.0 + u * (1.0 - sigma))).astype(BF)
    dw = (back * silu).astype(BF)
    du_ref[...] = du
    dw_ref[...] = dw
    db_ref[...] = (dot_nt(du, wg_ref[0]) + dot_nt(dw, wu_ref[0])).astype(BF)


def expert(slot, x, up, gate, wg, wu, wd):
    _, rows, width = x.shape
    hidden = wg.shape[2]
    tile = min(256, rows)
    at = lambda i: (i, 0)
    mine = lambda i: (slot, i, 0)
    whole = lambda i: (0, 0, 0)
    return call(
        expert_body,
        "expert",
        (rows // tile,),
        [
            pl.BlockSpec((1, tile, width), mine),
            pl.BlockSpec((1, tile, width), mine),
            pl.BlockSpec((tile, 1), at),
            pl.BlockSpec((1, width, hidden), whole),
            pl.BlockSpec((1, width, hidden), whole),
            pl.BlockSpec((1, hidden, width), whole),
        ],
        [
            pl.BlockSpec((tile, width), at),
            pl.BlockSpec((tile, width), at),
            pl.BlockSpec((tile, hidden), at),
            pl.BlockSpec((tile, hidden), at),
            pl.BlockSpec((tile, hidden), at),
            pl.BlockSpec((tile, 1), at),
        ],
        [
            struct((rows, width), BF),
            struct((rows, width), BF),
            struct((rows, hidden), BF),
            struct((rows, hidden), BF),
            struct((rows, hidden), BF),
            struct((rows, 1), F32),
        ],
        flops=12 * rows * width * hidden,
        moved=2 * (4 * rows * width + 3 * rows * hidden + 3 * width * hidden),
    )(x, up, gate, wg, wu, wd)


def swap(v, step, count):
    return lax.ppermute(v, "col", [(i, i ^ step) for i in range(count)])


def fetch(v, count):
    if count != 4:
        return [v] + [swap(v, d, count) for d in range(1, count)]
    half = v.shape[1] // 2
    one, two = swap(v, 1, count), swap(v, 2, count)
    first = swap(one[:, :half], 2, count)
    second = swap(two[:, half:], 1, count)
    return [v, one, two, jnp.concatenate([first, second], axis=1)]


def deliver(parts, count):
    own = parts[0]
    low = [None] + [p.astype(BF) for p in parts[1:]]
    if count != 4:
        for d in range(1, count):
            own = own + swap(low[d], d, count).astype(F32)
        return own
    half = own.shape[0] // 2
    to_two = swap(low[3][:half], 1, count)
    to_one = swap(low[3][half:], 2, count)
    one = jnp.concatenate([low[1][:half], (parts[1][half:] + to_one.astype(F32)).astype(BF)], axis=0)
    two = jnp.concatenate([(parts[2][:half] + to_two.astype(F32)).astype(BF), low[2][half:]], axis=0)
    return own + swap(one, 1, count).astype(F32) + swap(two, 2, count).astype(F32)


def after(value, *earlier):
    return lax.optimization_barrier((value,) + earlier)[0]


def norm_back(grad, hat, spread, gain):
    scaled = grad * gain
    return spread * (scaled - hat * jnp.mean(scaled * hat, axis=-1, keepdims=True))


def per_device(
    layer_input, out_grad, routes, positions, w_q, key_value_weight, w_out, router,
    ln_attn, ln_moe, q_gain, k_gain, w_gate, w_up, w_down,
):
    rows, width = layer_input.shape[1:]
    row_count, col_count = lax.axis_size("row"), lax.axis_size("col")
    row_at, col_at = lax.axis_index("row"), lax.axis_index("col")
    devices = row_count * col_count
    experts = w_gate.shape[0] * devices
    assert w_gate.shape[0] == 1
    cap = rows * TOPK // experts
    tokens = rows * devices
    heads = w_q.shape[1] // HEAD
    sharing = QUERY_HEADS // KEY_VALUE_HEADS // heads
    blocks = PROMPT_TOKENS // rows
    slots = range(col_count)
    others = list(slots[1:])
    members = [col_at ^ d for d in slots]
    row_word = row_at.astype(jnp.int32).reshape(1)

    x_own = layer_input[0]
    up_own = out_grad[0]

    kv_cols = KEY_VALUE_HEADS * HEAD

    def kv_pick(weight, member):
        head = member // sharing
        return [
            lax.dynamic_slice_in_dim(weight, head * HEAD, HEAD, 1),
            lax.dynamic_slice_in_dim(weight, kv_cols + head * HEAD, HEAD, 1),
        ]

    cols = (heads + 2) * HEAD
    piece, head_piece = ln_attn.shape[0], q_gain.shape[0]
    rest = [jnp.pad(g, (0, piece - head_piece))[:, None] for g in (q_gain, k_gain)]
    rest = [router, ln_attn[:, None], ln_moe[:, None]] + rest
    wide = jnp.concatenate([w_q] + kv_pick(key_value_weight, col_at) + rest, axis=1)
    wide = jnp.pad(wide, ((0, 0), (0, -wide.shape[1] % HEAD)))
    wide = lax.all_gather(wide, "row", axis=0, tiled=True)
    extra = wide[:, cols:]
    router_all = extra[:, :experts]
    gain_one = extra[:, experts].astype(F32)[None]
    gain_two = extra[:, experts + 1].astype(F32)[None]
    head_gains = extra.reshape(row_count, piece, -1)[:, :head_piece].astype(F32)
    gain_q = head_gains[:, :, experts + 2].reshape(1, HEAD)
    gain_k = head_gains[:, :, experts + 3].reshape(1, HEAD)

    xs = [v[0] for v in fetch(layer_input, col_count)]
    out_all = lax.all_gather(after(w_out, xs[1]), "row", axis=1, tiled=True)

    routes_all = lax.all_gather(routes[0], "row", axis=0)
    expert_ids = jnp.arange(experts, dtype=jnp.int32)
    flat_routes = routes_all.transpose(0, 2, 1)
    mask_all = jnp.any(flat_routes[:, :, None, :] == expert_ids[None, None, :, None], axis=1)
    mine_ids = jnp.stack([row_at * col_count + m for m in members]).astype(jnp.int32)
    has = jnp.stack(
        [lax.dynamic_index_in_dim(mask_all, e, 1, keepdims=False) for e in mine_ids], axis=1
    )
    place = jnp.arange(rows)
    before = (place[:, None] <= place[None, :]).astype(BF)
    order = jnp.einsum("rdt,tu->rdu", has.astype(BF), before, preferred_element_type=F32)
    rank = jnp.where(has, order.astype(jnp.int32) - 1, -1)
    rank_t = rank.transpose(0, 2, 1)
    mask_all = mask_all.astype(F32)

    inv_freq = THETA ** (-2.0 * jnp.arange(HEAD // 2, dtype=F32) / HEAD)
    coses, sines = [], []
    for m in members:
        spots = lax.dynamic_index_in_dim(positions, m, 0, keepdims=False).astype(F32)
        angles = spots[:, None] * inv_freq[None, :]
        cos, sin = jnp.cos(angles), jnp.sin(angles)
        coses.append(jnp.concatenate([cos, cos], axis=1))
        sines.append(jnp.concatenate([-sin, sin], axis=1))

    qs, kvs, normed, scales, every = [[None] * col_count for _ in range(5)]
    line = others + [0]
    for d in line:
        qs[d], kvs[d], normed[d], scales[d] = qkv(
            xs[d], gain_one, wide, coses[d], sines[d], gain_q, gain_k, heads
        )
        every[d] = lax.all_gather(kvs[d], "row", axis=0)
    wg_all = fetch(after(w_gate, xs[-1]), col_count)
    mixes, logs = [None] * col_count, [None] * col_count
    hidden = x_own.astype(F32)
    for d in line:
        mixes[d], logs[d] = attend(row_word, qs[d], every[d], kvs[d], blocks)
        share = jnp.dot(mixes[d], out_all, preferred_element_type=F32)
        hidden = hidden + (share if d == 0 else swap(share.astype(BF), d, col_count).astype(F32))
    up_all = lax.all_gather(after(up_own, mixes[line[0]]), "row", axis=0)

    spread = lax.rsqrt(jnp.mean(hidden * hidden, axis=-1, keepdims=True) + EPS)
    second = (hidden * spread * gain_two).astype(BF)
    second_all = lax.all_gather(second, "row", axis=0)
    wu, wd = after((w_up, w_down), second)
    wu_all, wd_all = fetch(wu, col_count), fetch(wd, col_count)

    expert_up = dispatch(rank, up_all, cap).reshape(col_count, row_count * cap, width)
    router_t = router_all.T
    expert_in, probs_all, gate_pairs = route_dispatch(
        mine_ids, rank, second_all, mask_all, router_t, cap
    )
    expert_in = expert_in.reshape(col_count, row_count * cap, width)
    gate_pairs = gate_pairs.reshape(col_count, row_count * cap, 1)
    kv_all = lax.all_gather(after(key_value_weight, expert_in), "row", axis=0, tiled=True)
    ys, dbs, ms, dus, dws, dgs = [], [], [], [], [], []
    for d in slots:
        got = expert(d, expert_in, expert_up, gate_pairs[d], wg_all[d], wu_all[d], wd_all[d])
        for kept, value in zip((ys, dbs, ms, dus, dws, dgs), got):
            kept.append(value)
    cut = lambda parts: [p.reshape(row_count, cap, width) for p in parts]
    db_sum = lax.psum_scatter(combine(rank_t, cut(dbs)), "row", scatter_dimension=0)

    slot_ids = jnp.arange(cap, dtype=jnp.int32)
    hot = rank[:, :, None, :] == slot_ids[None, None, :, None]
    pair_scores = jnp.stack(dgs, axis=0).reshape(col_count, row_count, cap, 1).transpose(1, 0, 2, 3)
    score_grads = jnp.sum(jnp.where(hot, pair_scores, 0.0), axis=2)
    score_grads = lax.all_to_all(score_grads, "row", split_axis=0, concat_axis=0, tiled=True)
    sums = jnp.stack([jnp.sum(mask_all, axis=(0, 2)), jnp.sum(probs_all, axis=(0, 2))])
    step = 1
    while step < col_count:
        sums = sums + swap(sums, step, col_count)
        step *= 2
    load = sums[0] / (tokens * TOPK)
    mean_probs = sums[1] / tokens
    aux_loss = experts * jnp.sum(load * mean_probs)
    expert_load = jnp.stack([experts * load, experts * mean_probs])

    grad_parts = [
        [dot_tn(ms[d], expert_up[d]) for d in slots],
        [dot_tn(expert_in[d], dus[d]) for d in slots],
        [dot_tn(expert_in[d], dws[d]) for d in slots],
    ]
    y_part = combine(rank_t, cut(ys))
    db_sum, grad_parts, y_part = lax.optimization_barrier((db_sum, grad_parts, y_part))
    grad_down, grad_gate, grad_up = [deliver(parts, col_count) for parts in grad_parts]
    y_sum = lax.psum_scatter(y_part, "row", scatter_dimension=0)
    layer_output = (hidden + y_sum.astype(F32)).astype(BF)

    mask_own = jnp.any(routes[0].T[:, None, :] == expert_ids[None, :, None], axis=0)
    logits = lax.dot_general(
        router_all, second, (((0,), (1,)), ((), ())), preferred_element_type=F32
    )
    probs = jax.nn.softmax(logits, axis=0)
    picked = jnp.where(mask_own, probs, 0.0)
    total = jnp.sum(picked, axis=0, keepdims=True)
    gates = picked / total
    to_member = jnp.stack(members)[:, None] == jnp.arange(col_count)[None, :]
    gate_grad = jnp.sum(
        jnp.where(to_member[None, :, :, None], score_grads[:, :, None, :], 0.0), axis=1
    ).reshape(experts, rows)
    weighted = jnp.sum(gate_grad * gates, axis=0, keepdims=True)
    prob_grad = (
        jnp.where(mask_own, (gate_grad - weighted) / total, 0.0)
        + AUX_COEF * experts * load[:, None] / tokens
    )
    logit_low = (probs * (prob_grad - jnp.sum(probs * prob_grad, axis=0, keepdims=True))).astype(BF)
    grad_router = lax.dot_general(
        second, logit_low, (((0,), (1,)), ((), ())), preferred_element_type=F32
    )
    second_grad = db_sum.astype(F32) + lax.dot_general(
        logit_low, router_all, (((0,), (1,)), ((), ())), preferred_element_type=F32
    )
    hat = hidden * spread
    gain_two_grad = jnp.sum(second_grad * hat, axis=0)
    hidden_grad = up_own.astype(F32) + norm_back(second_grad, hat, spread, gain_two)
    branch = hidden_grad.astype(BF)

    branches = [v[0] for v in fetch(branch[None], col_count)]
    grad_qs, grad_kvs, kv_moved = [], [], []
    gain_q_grad, gain_k_grad, gain_one_grad, input_sum = 0.0, 0.0, 0.0, 0.0

    def back_turn(v, cos, sin):
        moved = v * sin
        half = HEAD // 2
        return v * cos + jnp.concatenate([moved[:, half:], moved[:, :half]], axis=1)

    for d in slots:
        mix_grad = dot_nt(branches[d], out_all).astype(BF)
        grad_q, grad_prompt, pair, gain_part = attend_back(
            row_word, qs[d], every[d], kvs[d], blocks, mix_grad, mixes[d], logs[d], scales[d],
            coses[d], sines[d], gain_q,
        )
        grad_qs.append(grad_q)
        gain_q_grad = gain_q_grad + gain_part[0]
        prompt = lax.psum_scatter(grad_prompt, "row", scatter_dimension=1, tiled=True)
        share, sums_one = input_share(grad_q, wide, normed[d], F32 if d == 0 else BF)
        gain_one_grad = gain_one_grad + sums_one[0]
        input_sum = input_sum + (share if d == 0 else swap(share, d, col_count).astype(F32))
        chunk = prompt.shape[1]
        prompt = jnp.concatenate(
            [
                lax.ppermute(prompt, "row", [(rows // chunk * i + a, i) for i in range(blocks)])
                for a in range(rows // chunk)
            ],
            axis=1,
        )
        pair = pair + prompt.astype(F32)
        key_dy = back_turn(pair[0], coses[d], sines[d])
        key_hat = back_turn(kvs[d][0].astype(F32), coses[d], sines[d]) / gain_k
        gain_k_grad = gain_k_grad + jnp.sum(key_dy * key_hat, axis=0)
        key_raw = norm_back(key_dy, key_hat, scales[d][:, heads : heads + 1], gain_k)
        grad_kv = jnp.concatenate([key_raw.astype(BF), pair[1].astype(BF)], axis=1)
        grad_kvs.append(grad_kv)
        kv_moved.append(grad_kv if d == 0 else swap(grad_kv, d, col_count))
    normed_all = jnp.stack(normed, axis=0)
    over_tokens = lambda a, b: lax.dot_general(
        a, b, (((0, 1), (0, 1)), ((), ())), preferred_element_type=F32
    )
    grad_q = over_tokens(normed_all, jnp.stack(grad_qs, axis=0))
    grad_q = lax.psum_scatter(grad_q.astype(BF), "row", scatter_dimension=0, tiled=True)
    grad_out = over_tokens(jnp.stack(mixes, axis=0), jnp.stack(branches, axis=0))
    grad_out = lax.psum_scatter(grad_out.astype(BF), "row", scatter_dimension=1, tiled=True)

    kv_weight = jnp.concatenate([w for m in members for w in kv_pick(kv_all, m)], axis=1)
    kv_share = dot_nt(jnp.concatenate(kv_moved, axis=1), kv_weight)
    input_sum = input_sum + kv_share
    x_wide = x_own.astype(F32)
    x_spread = lax.rsqrt(jnp.mean(x_wide * x_wide, axis=-1, keepdims=True) + EPS)
    x_hat = x_wide * x_spread
    gain_one_grad = gain_one_grad / gain_one[0] + jnp.sum(kv_share * x_hat, axis=0)
    input_grad = hidden_grad + norm_back(input_sum, x_hat, x_spread, gain_one)

    grad_kv = over_tokens(normed_all, jnp.stack(grad_kvs, axis=0)).astype(BF)
    grad_kv = lax.all_to_all(
        grad_kv.reshape(devices, -1, 2 * HEAD), ("row", "col"), split_axis=0, concat_axis=0, tiled=True
    )
    grad_kv = jnp.sum(grad_kv.astype(F32).reshape(row_count, col_count, -1, 2 * HEAD), axis=0)
    grad_kv = grad_kv.reshape(KEY_VALUE_HEADS, sharing, -1, 2, HEAD).sum(axis=1)
    grad_kv = grad_kv.transpose(1, 2, 0, 3).reshape(-1, 2 * kv_cols)
    tail = [grad_router, gain_two_grad, gain_one_grad, gain_q_grad, gain_k_grad]
    tail = [v.reshape(devices, -1) for v in tail]
    cuts = [0]
    for v in tail:
        cuts.append(cuts[-1] + v.shape[1])
    tail = lax.all_to_all(
        jnp.concatenate(tail, axis=1), ("row", "col"), split_axis=0, concat_axis=0, tiled=True
    )
    tail = jnp.sum(tail, axis=0)
    grad_router, gain_two_grad, gain_one_grad, gain_q_grad, gain_k_grad = [
        tail[a:b] for a, b in zip(cuts[:-1], cuts[1:])
    ]

    return (
        layer_output[None],
        aux_loss,
        input_grad[None],
        grad_q.astype(F32),
        grad_kv,
        grad_out.astype(F32),
        grad_router.reshape(width // devices, experts),
        gain_one_grad,
        gain_two_grad,
        gain_q_grad,
        gain_k_grad,
        grad_gate[None],
        grad_up[None],
        grad_down[None],
        expert_load,
    )


def solution(mesh):
    in_specs = (
        P("col", "row", None),
        P("col", "row", None),
        P("col", "row", None),
        P(None, "row"),
        P("row", "col"),
        P("row", None),
        P("col", "row"),
        P("row", None),
        P("row"),
        P("row"),
        P("row"),
        P("row"),
        P(("row", "col"), None, None),
        P(("row", "col"), None, None),
        P(("row", "col"), None, None),
    )
    out_specs = (
        P("col", "row", None),
        P(),
        P("col", "row", None),
        P("row", "col"),
        P(("row", "col"), None),
        P("col", "row"),
        P(("row", "col"), None),
        P(("row", "col")),
        P(("row", "col")),
        P(("row", "col")),
        P(("row", "col")),
        P(("row", "col"), None, None),
        P(("row", "col"), None, None),
        P(("row", "col"), None, None),
        P(),
    )
    return jax.shard_map(
        per_device, mesh=mesh, in_specs=in_specs, out_specs=out_specs, check_vma=False
    )
```

```python
from functools import partial
import math

import jax
import jax.numpy as jnp
from jax import lax
from jax.experimental import pallas as pl
from jax.experimental.pallas import tpu as pltpu
from jax.sharding import PartitionSpec as P

QUERY_HEADS = 32
KEY_VALUE_HEADS = 4
HEAD = 128
TOPK = 8
CONT = 256
PROMPT_TOKENS = 2048

EPS = 1e-06
THETA = 1000000.0
AUX_COEF = 0.001
LN2 = math.log(2.0)
SCALE2 = 1.0 / (math.sqrt(HEAD) * LN2)
VMEM = 56 * 1024 * 1024

BF = jnp.bfloat16
F32 = jnp.float32


def dot_nn(a, b):
    return lax.dot_general(a, b, (((1,), (0,)), ((), ())), preferred_element_type=F32)


def dot_nt(a, b):
    return lax.dot_general(a, b, (((1,), (1,)), ((), ())), preferred_element_type=F32)


def dot_tn(a, b):
    return lax.dot_general(a, b, (((0,), (0,)), ((), ())), preferred_element_type=F32)


def call(body, name, grid, in_specs, out_specs, out_shape, scratch=(), flops=0, moved=0, prefetch=0):
    return pl.pallas_call(
        body,
        name=name,
        grid_spec=pltpu.PrefetchScalarGridSpec(
            num_scalar_prefetch=prefetch,
            grid=grid,
            in_specs=in_specs,
            out_specs=out_specs,
            scratch_shapes=list(scratch),
        ),
        out_shape=out_shape,
        cost_estimate=pl.CostEstimate(
            flops=int(flops), bytes_accessed=int(moved), transcendentals=0
        ),
        compiler_params=pltpu.CompilerParams(
            dimension_semantics=("arbitrary",) * len(grid), vmem_limit_bytes=VMEM
        ),
    )


def struct(shape, dtype):
    return jax.ShapeDtypeStruct(shape, dtype)


def turn(v, cos, sin):
    return v * cos + pltpu.roll(v, HEAD // 2, 1) * sin


def turn_back(v, cos, sin):
    return v * cos + pltpu.roll(v * sin, HEAD // 2, 1)


def qkv_body(heads, x_ref, gain_ref, w_ref, cos_ref, sin_ref, qg_ref, kg_ref, q_ref, kv_ref, a_ref, r_ref):
    x = x_ref[...].astype(F32)
    normed = x * lax.rsqrt(jnp.mean(x * x, axis=-1, keepdims=True) + EPS) * gain_ref[...]
    low = normed.astype(BF)
    a_ref[...] = low
    raw = dot_nn(low, w_ref[...])
    cos = cos_ref[...]
    sin = sin_ref[...]
    lane = lax.broadcasted_iota(jnp.int32, (x.shape[0], HEAD), 1)
    scales = jnp.zeros((x.shape[0], HEAD), F32)
    for h in range(heads + 1):
        v = raw[:, h * HEAD : (h + 1) * HEAD]
        r = lax.rsqrt(jnp.mean(v * v, axis=-1, keepdims=True) + EPS)
        scales = jnp.where(lane == h, r, scales)
        if h < heads:
            q_ref[h] = (turn(v * r * qg_ref[...], cos, sin) * SCALE2).astype(BF)
        else:
            kv_ref[0] = turn(v * r * kg_ref[...], cos, sin).astype(BF)
    kv_ref[1] = raw[:, (heads + 1) * HEAD :].astype(BF)
    r_ref[...] = scales


def qkv(x, gain, w, cos, sin, qg, kg, heads):
    rows, width = x.shape
    cols = (heads + 2) * HEAD
    tile = 256
    whole = lambda i: (0, 0)
    row = lambda i: (i, 0)
    return call(
        partial(qkv_body, heads),
        "qkv",
        (rows // tile,),
        [
            pl.BlockSpec((tile, width), row),
            pl.BlockSpec((1, width), whole),
            pl.BlockSpec((width, cols), whole),
            pl.BlockSpec((tile, HEAD), row),
            pl.BlockSpec((tile, HEAD), row),
            pl.BlockSpec((1, HEAD), whole),
            pl.BlockSpec((1, HEAD), whole),
        ],
        [
            pl.BlockSpec((heads, tile, HEAD), lambda i: (0, i, 0)),
            pl.BlockSpec((2, tile, HEAD), lambda i: (0, i, 0)),
            pl.BlockSpec((tile, width), row),
            pl.BlockSpec((tile, HEAD), row),
        ],
        [
            struct((heads, rows, HEAD), BF),
            struct((2, rows, HEAD), BF),
            struct((rows, width), BF),
            struct((rows, HEAD), F32),
        ],
        flops=2 * rows * width * cols,
        moved=2 * (2 * rows * width + width * cols + rows * cols),
    )(x, gain, w, cos, sin, qg, kg)


def causal(count):
    q_at = lax.broadcasted_iota(jnp.int32, (count, CONT, CONT), 1)
    k_at = lax.broadcasted_iota(jnp.int32, (count, CONT, CONT), 2)
    return (k_at <= q_at).reshape(count * CONT, CONT)


def attend_body(heads, per, blocks, rows, row_ref, q_ref, kp_ref, vp_ref, kv_ref, o_ref, l_ref, vp_one, vl_one, acc):
    at = pl.program_id(0)
    part = pl.program_id(1)
    row = row_ref[0]

    @pl.when((at == 0) & (part == 0))
    def _():
        for j in range(blocks):
            vp_one[j * rows : (j + 1) * rows, :HEAD] = vp_ref[j, 0]
        vp_one[:, HEAD:] = jnp.ones((blocks * rows, HEAD), BF)
        vl_one[:, :HEAD] = kv_ref[1]
        vl_one[:, HEAD:] = jnp.ones((rows, HEAD), BF)

    q = q_ref[...].reshape(per * CONT, HEAD)
    here = pl.ds(pl.multiple_of(at * CONT, CONT), CONT)
    weights = jnp.where(causal(per), jnp.exp2(dot_nt(q, kv_ref[0, here, :])), 0.0).astype(BF)
    acc[...] = dot_nn(weights, vl_one[here, :])

    @pl.when(row < blocks)
    def _():
        for j in range(rows // CONT - 1):

            @pl.when(j < at)
            def _():
                piece = slice(j * CONT, (j + 1) * CONT)
                weights = jnp.exp2(dot_nt(q, kv_ref[0, piece, :])).astype(BF)
                acc[...] += dot_nn(weights, vl_one[piece, :])

    @pl.loop(0, jnp.minimum(row, blocks))
    def _(j):
        weights = jnp.exp2(dot_nt(q, kp_ref[j, 0])).astype(BF)
        acc[...] += dot_nn(weights, vp_one[pl.ds(pl.multiple_of(j * rows, rows), rows), :])

    total = acc[:, HEAD:]
    out = (acc[:, :HEAD] / total).astype(BF)
    logs = jnp.log2(total)
    lane = lax.broadcasted_iota(jnp.int32, (CONT, HEAD), 1)

    @pl.when(part == 0)
    def _():
        l_ref[...] = jnp.zeros((CONT, HEAD), F32)

    held = l_ref[...]
    for p in range(per):
        o_ref[:, p * HEAD : (p + 1) * HEAD] = out[p * CONT : (p + 1) * CONT]
        held = jnp.where(lane == part * per + p, logs[p * CONT : (p + 1) * CONT], held)
    l_ref[...] = held


def attend(row, q, every, kv, blocks):
    heads, rows, _ = q.shape
    per = 2
    every, place = every
    keys = blocks * rows
    return call(
        partial(attend_body, heads, per, blocks, rows),
        "attend",
        (rows // CONT, heads // per),
        [
            pl.BlockSpec((per, CONT, HEAD), lambda i, h, s: (h, i, 0)),
            pl.BlockSpec((blocks, 1, rows, HEAD), lambda i, h, s: (0, 2 * place, 0, 0)),
            pl.BlockSpec((blocks, 1, rows, HEAD), lambda i, h, s: (0, 2 * place + 1, 0, 0)),
            pl.BlockSpec((2, rows, HEAD), lambda i, h, s: (0, 0, 0)),
        ],
        [
            pl.BlockSpec((CONT, per * HEAD), lambda i, h, s: (i, h)),
            pl.BlockSpec((CONT, HEAD), lambda i, h, s: (i, 0)),
        ],
        [struct((rows, heads * HEAD), BF), struct((rows, HEAD), F32)],
        scratch=[
            pltpu.VMEM((keys, 2 * HEAD), BF),
            pltpu.VMEM((rows, 2 * HEAD), BF),
            pltpu.VMEM((per * CONT, 2 * HEAD), F32),
        ],
        flops=8 * rows * heads * (keys + CONT) * HEAD,
        moved=2 * HEAD * (2 * rows * heads + 2 * keys),
        prefetch=1,
    )(row, q, every, every, kv)


def attend_back_body(
    heads, per, blocks, rows,
    row_ref, q_ref, kp_ref, vp_ref, kv_ref, do_ref, o_ref, l_ref, r_ref, cos_ref, sin_ref, qg_ref,
    dq_ref, dp_ref, dl_ref, g_ref,
    dq, dkp, dvp,
):
    at = pl.program_id(0)
    part = pl.program_id(1)
    row = row_ref[0]

    @pl.when((at == 0) & (part == 0))
    def _():
        dkp[...] = jnp.zeros_like(dkp)
        dvp[...] = jnp.zeros_like(dvp)
        dl_ref[...] = jnp.zeros_like(dl_ref)
        g_ref[...] = jnp.zeros_like(g_ref)

    q = q_ref[...].reshape(per * CONT, HEAD)
    lane = lax.broadcasted_iota(jnp.int32, (CONT, HEAD), 1)
    do_parts, logs, centers, scales = [], [], [], []
    for p in range(per):
        do_part = do_ref[:, p * HEAD : (p + 1) * HEAD]
        do_parts.append(do_part)
        centers.append(
            jnp.sum(
                do_part.astype(F32) * o_ref[:, p * HEAD : (p + 1) * HEAD].astype(F32),
                axis=-1,
                keepdims=True,
            )
        )
        pick = lane == part * per + p
        logs.append(jnp.sum(jnp.where(pick, l_ref[...], 0.0), axis=-1, keepdims=True))
        scales.append(jnp.sum(jnp.where(pick, r_ref[...], 0.0), axis=-1, keepdims=True))
    do = jnp.concatenate(do_parts, axis=0)
    center = jnp.concatenate(centers, axis=0)
    log = jnp.concatenate(logs, axis=0)

    def block(k, v, mask):
        probs = jnp.exp2(dot_nt(q, k) - log)
        if mask is not None:
            probs = jnp.where(mask, probs, 0.0)
        ds = (probs * (dot_nt(do, v) - center)).astype(BF)
        return dot_nn(ds, k), dot_tn(ds, q), dot_tn(probs.astype(BF), do)

    here = pl.ds(pl.multiple_of(at * CONT, CONT), CONT)
    a, b, c = block(kv_ref[0, here, :], kv_ref[1, here, :], causal(per))
    dq[...] = a
    dl_ref[0, here, :] += b
    dl_ref[1, here, :] += c

    @pl.when(row < blocks)
    def _():
        for j in range(rows // CONT - 1):

            @pl.when(j < at)
            def _():
                piece = slice(j * CONT, (j + 1) * CONT)
                a, b, c = block(kv_ref[0, piece, :], kv_ref[1, piece, :], None)
                dq[...] += a
                dl_ref[0, piece, :] += b
                dl_ref[1, piece, :] += c

    @pl.loop(0, jnp.minimum(row, blocks))
    def _(j):
        a, b, c = block(kp_ref[j, 0], vp_ref[j, 0], None)
        piece = pl.ds(pl.multiple_of(j * rows, rows), rows)
        dq[...] += a
        dkp[piece, :] += b
        dvp[piece, :] += c

    cos = cos_ref[...]
    sin = sin_ref[...]
    gain = qg_ref[...]
    tally = jnp.zeros((1, HEAD), F32)
    for p in range(per):
        dy = turn_back(dq[p * CONT : (p + 1) * CONT, :] * (SCALE2 * LN2), cos, sin)
        hat = turn_back(q[p * CONT : (p + 1) * CONT].astype(F32), cos, sin) * (1.0 / SCALE2) / gain
        tally += jnp.sum(dy * hat, axis=0, keepdims=True)
        dyg = dy * gain
        raw = scales[p] * (dyg - hat * jnp.mean(dyg * hat, axis=-1, keepdims=True))
        dq_ref[:, p * HEAD : (p + 1) * HEAD] = raw.astype(BF)
    g_ref[0:1, :] += tally

    @pl.when((at == rows // CONT - 1) & (part == heads // per - 1))
    def _():
        dp_ref[0] = (dkp[...] * LN2).astype(BF)
        dp_ref[1] = dvp[...].astype(BF)
        dl_ref[0] = dl_ref[0] * LN2


def attend_back(row, q, every, kv, blocks, do, o, logs, scales, cos, sin, qg):
    heads, rows, _ = q.shape
    per = 2
    every, place = every
    keys = blocks * rows
    tile = lambda i, h, s: (i, 0)
    head = lambda i, h, s: (i, h)
    return call(
        partial(attend_back_body, heads, per, blocks, rows),
        "attend_back",
        (rows // CONT, heads // per),
        [
            pl.BlockSpec((per, CONT, HEAD), lambda i, h, s: (h, i, 0)),
            pl.BlockSpec((blocks, 1, rows, HEAD), lambda i, h, s: (0, 2 * place, 0, 0)),
            pl.BlockSpec((blocks, 1, rows, HEAD), lambda i, h, s: (0, 2 * place + 1, 0, 0)),
            pl.BlockSpec((2, rows, HEAD), lambda i, h, s: (0, 0, 0)),
            pl.BlockSpec((CONT, per * HEAD), head),
            pl.BlockSpec((CONT, per * HEAD), head),
            pl.BlockSpec((CONT, HEAD), tile),
            pl.BlockSpec((CONT, HEAD), tile),
            pl.BlockSpec((CONT, HEAD), tile),
            pl.BlockSpec((CONT, HEAD), tile),
            pl.BlockSpec((1, HEAD), lambda i, h, s: (0, 0)),
        ],
        [
            pl.BlockSpec((CONT, per * HEAD), head),
            pl.BlockSpec((2, keys, HEAD), lambda i, h, s: (0, 0, 0)),
            pl.BlockSpec((2, rows, HEAD), lambda i, h, s: (0, 0, 0)),
            pl.BlockSpec((8, HEAD), lambda i, h, s: (0, 0)),
        ],
        [
            struct((rows, heads * HEAD), BF),
            struct((2, keys, HEAD), BF),
            struct((2, rows, HEAD), F32),
            struct((8, HEAD), F32),
        ],
        scratch=[
            pltpu.VMEM((per * CONT, HEAD), F32),
            pltpu.VMEM((keys, HEAD), F32),
            pltpu.VMEM((keys, HEAD), F32),
        ],
        flops=20 * rows * heads * (keys + CONT) * HEAD,
        moved=2 * HEAD * (4 * rows * heads + 4 * keys),
        prefetch=1,
    )(row, q, every, every, kv, do, o, logs, scales, cos, sin, qg)


def dispatch_body(count, cap, rank_ref, rows_ref, *out_refs):
    tokens = rows_ref.shape[1]
    slot = lax.broadcasted_iota(jnp.int32, (cap, tokens), 0)
    for d in range(count):
        hot = (rank_ref[0, d : d + 1, :] == slot).astype(F32).astype(BF)
        out_refs[d][0] = dot_nn(hot, rows_ref[0]).astype(BF)


def dispatch(rank, rows, cap):
    sources, count, tokens = rank.shape
    width = rows.shape[2]
    return call(
        partial(dispatch_body, count, cap),
        "dispatch",
        (sources,),
        [
            pl.BlockSpec((1, count, tokens), lambda s: (s, 0, 0)),
            pl.BlockSpec((1, tokens, width), lambda s: (s, 0, 0)),
        ],
        [pl.BlockSpec((1, cap, width), lambda s: (s, 0, 0))] * count,
        [struct((sources, cap, width), BF)] * count,
        flops=2 * sources * count * cap * tokens * width,
        moved=2 * sources * width * (tokens + count * cap),
    )(rank, rows)


def route_body(count, cap, ids_ref, rank_ref, rows_ref, mask_ref, router_ref, gate_ref, *out_refs):
    tokens = rows_ref.shape[1]
    rows = rows_ref[0]
    logits = dot_nt(router_ref[...], rows)
    weights = jnp.exp(logits - jnp.max(logits, axis=0, keepdims=True))
    probs = weights / jnp.sum(weights, axis=0, keepdims=True)
    picked = probs * mask_ref[0]
    gates = picked / jnp.sum(picked, axis=0, keepdims=True)
    expert_at = lax.broadcasted_iota(jnp.int32, gates.shape, 0)
    slot = lax.broadcasted_iota(jnp.int32, (cap, tokens), 0)
    for d in range(count):
        here = rank_ref[0, d : d + 1, :] == slot
        out_refs[d][0] = dot_nn(here.astype(F32).astype(BF), rows).astype(BF)
        mine = jnp.sum(jnp.where(expert_at == ids_ref[d], gates, 0.0), axis=0, keepdims=True)
        gate_ref[d, 0] = jnp.sum(jnp.where(here, mine, 0.0), axis=1, keepdims=True)


def route_dispatch(ids, rank, rows, mask, router, cap):
    sources, count, tokens = rank.shape
    width = rows.shape[2]
    experts = router.shape[0]
    return call(
        partial(route_body, count, cap),
        "route_dispatch",
        (sources,),
        [
            pl.BlockSpec((1, count, tokens), lambda s, i: (s, 0, 0)),
            pl.BlockSpec((1, tokens, width), lambda s, i: (s, 0, 0)),
            pl.BlockSpec((1, experts, tokens), lambda s, i: (s, 0, 0)),
            pl.BlockSpec((experts, width), lambda s, i: (0, 0)),
        ],
        [
            pl.BlockSpec((count, 1, cap, 1), lambda s, i: (0, s, 0, 0)),
        ]
        + [pl.BlockSpec((1, cap, width), lambda s, i: (s, 0, 0))] * count,
        [struct((count, sources, cap, 1), F32)]
        + [struct((sources, cap, width), BF)] * count,
        flops=2 * sources * count * cap * tokens * width,
        moved=2 * sources * width * (tokens + count * cap),
        prefetch=1,
    )(ids, rank, rows, mask, router)


def share_body(g_ref, w_ref, out_ref):
    out_ref[...] = dot_nt(g_ref[...], w_ref[...]).astype(out_ref.dtype)


def input_share(grads, w, dtype):
    rows, cols = grads.shape
    width = w.shape[0]
    tile = 256
    return call(
        share_body,
        "input_share",
        (rows // tile,),
        [
            pl.BlockSpec((tile, cols), lambda i: (i, 0)),
            pl.BlockSpec((width, cols), lambda i: (0, 0)),
        ],
        pl.BlockSpec((tile, width), lambda i: (i, 0)),
        struct((rows, width), dtype),
        flops=2 * rows * width * cols,
        moved=2 * (rows * width + width * cols + rows * cols),
    )(grads, w)


def combine_body(count, cap, scored, rank_ref, *refs):
    tokens = rank_ref.shape[1]
    slot = lax.broadcasted_iota(jnp.int32, (tokens, cap), 1)
    out_ref = refs[count * (2 if scored else 1)]
    total = None
    for d in range(count):
        hot = (rank_ref[0, :, d : d + 1] == slot).astype(F32).astype(BF)
        piece = dot_nn(hot, refs[d][0])
        total = piece if total is None else total + piece
        if scored:
            score = dot_nn(hot, refs[count + d][0])
            refs[-1][0, :, d : d + 1] = jnp.sum(score, axis=-1, keepdims=True)
    out_ref[0] = total.astype(BF)


def combine(rank_t, parts, scores=()):
    sources, tokens, count = rank_t.shape
    cap = parts[0].shape[0] // sources
    width = parts[0].shape[1]
    at = lambda s: (s, 0, 0)
    cut = lambda v: v.reshape(sources, cap, v.shape[1])
    out_specs = [pl.BlockSpec((1, tokens, width), at)]
    out_shape = [struct((sources, tokens, width), BF)]
    if scores:
        out_specs.append(pl.BlockSpec((1, tokens, count), at))
        out_shape.append(struct((sources, tokens, count), F32))
    return call(
        partial(combine_body, count, cap, bool(scores)),
        "combine",
        (sources,),
        [pl.BlockSpec((1, tokens, count), at)]
        + [pl.BlockSpec((1, cap, width), at)] * count
        + [pl.BlockSpec((1, cap, HEAD), at)] * len(scores),
        out_specs,
        out_shape,
        flops=2 * sources * count * cap * tokens * width,
        moved=2 * sources * width * (tokens + count * cap),
    )(rank_t, *[cut(p) for p in parts], *[cut(p) for p in scores])


def expert_body(
    x_ref, up_ref, gate_ref, wga_ref, wgb_ref, wua_ref, wub_ref, wda_ref, wdb_ref,
    y_ref, db_ref, m_ref, duw_ref, dg_ref,
):
    half = wga_ref.shape[1]
    deep = wda_ref.shape[1]
    hidden = wga_ref.shape[2]
    xa, xb = x_ref[:, :half], x_ref[:, half:]
    gate = gate_ref[...]
    u = dot_nn(xa, wga_ref[0]) + dot_nn(xb, wgb_ref[0])
    w = dot_nn(xa, wua_ref[0]) + dot_nn(xb, wub_ref[0])
    sigma = 1.0 / (1.0 + jnp.exp(-u))
    silu = u * sigma
    inner = silu * w
    low = inner.astype(BF)
    y = dot_nn(low[:, :deep], wda_ref[0]) + dot_nn(low[:, deep:], wdb_ref[0])
    y_ref[...] = (y * gate).astype(BF)
    m_ref[...] = (inner * gate).astype(BF)
    up = up_ref[...]
    back = jnp.concatenate([dot_nt(up, wda_ref[0]), dot_nt(up, wdb_ref[0])], axis=1)
    score = jnp.sum(low.astype(F32) * back, axis=-1, keepdims=True)
    lane = lax.broadcasted_iota(jnp.int32, dg_ref.shape, 1)
    high = score.astype(BF)
    rest = score - high.astype(F32)
    middle = rest.astype(BF)
    last = (rest - middle.astype(F32)).astype(BF)
    pieces = jnp.where(lane == 0, high.astype(F32), 0.0)
    pieces = jnp.where(lane == 1, middle.astype(F32), pieces)
    dg_ref[...] = jnp.where(lane == 2, last.astype(F32), pieces).astype(BF)
    back = back * gate
    du = (back * w * sigma * (1.0 + u * (1.0 - sigma))).astype(BF)
    dw = (back * silu).astype(BF)
    duw_ref[:, :hidden] = du
    duw_ref[:, hidden:] = dw
    db_ref[:, :half] = (dot_nt(du, wga_ref[0]) + dot_nt(dw, wua_ref[0])).astype(BF)
    db_ref[:, half:] = (dot_nt(du, wgb_ref[0]) + dot_nt(dw, wub_ref[0])).astype(BF)


def expert(x, up, gate, weights):
    rows, width = x.shape
    hidden = weights[0][0].shape[2]
    tile = min(256, rows)
    at = lambda i: (i, 0)
    specs, arrays = [], []
    for parts in weights:
        shape = (1, parts[0].shape[1] * len(parts) // 2, parts[0].shape[2])
        for j in range(2):
            place = j if len(parts) == 1 else 0
            specs.append(pl.BlockSpec(shape, lambda i, place=place: (0, place, 0)))
            arrays.append(parts[0] if len(parts) == 1 else parts[j])
    return call(
        expert_body,
        "expert",
        (rows // tile,),
        [
            pl.BlockSpec((tile, width), at),
            pl.BlockSpec((tile, width), at),
            pl.BlockSpec((tile, 1), at),
        ]
        + specs,
        [
            pl.BlockSpec((tile, width), at),
            pl.BlockSpec((tile, width), at),
            pl.BlockSpec((tile, hidden), at),
            pl.BlockSpec((tile, 2 * hidden), at),
            pl.BlockSpec((tile, HEAD), at),
        ],
        [
            struct((rows, width), BF),
            struct((rows, width), BF),
            struct((rows, hidden), BF),
            struct((rows, 2 * hidden), BF),
            struct((rows, HEAD), BF),
        ],
        flops=12 * rows * width * hidden,
        moved=2 * (4 * rows * width + 3 * rows * hidden + 3 * width * hidden),
    )(x, up, gate, *arrays)


def swap(v, step, count):
    return lax.ppermute(v, "col", [(i, i ^ step) for i in range(count)])


def near(v, count):
    return [swap(v, d, count) for d in ((1, 2) if count == 4 else range(1, count))]


def far(one, two, count):
    half = one.shape[1] // 2
    return [swap(one[:, :half], 2, count), swap(two[:, half:], 1, count)]


def halves(v):
    return v[:, : v.shape[1] // 2], v[:, v.shape[1] // 2 :]


def deliver_far(part, count):
    half = part.shape[0] // 2
    return swap(part[:half], 1, count), swap(part[half:], 2, count)


def join(part, got, first):
    half = part.shape[0] // 2
    wide = jnp.pad(got.astype(F32), ((0, half) if first else (half, 0), (0, 0)))
    return (part.astype(F32) + wide).astype(BF)


def after(value, *earlier):
    return lax.optimization_barrier((value,) + earlier)[0]


def norm_back(grad, hat, spread, gain):
    scaled = grad * gain
    return spread * (scaled - hat * jnp.mean(scaled * hat, axis=-1, keepdims=True))


def per_device(
    layer_input, out_grad, routes, positions, w_q, key_value_weight, w_out, router,
    ln_attn, ln_moe, q_gain, k_gain, w_gate, w_up, w_down,
):
    rows, width = layer_input.shape[1:]
    row_count, col_count = lax.axis_size("row"), lax.axis_size("col")
    row_at, col_at = lax.axis_index("row"), lax.axis_index("col")
    devices = row_count * col_count
    experts = w_gate.shape[0] * devices
    assert w_gate.shape[0] == 1
    cap = rows * TOPK // experts
    tokens = rows * devices
    heads = w_q.shape[1] // HEAD
    sharing = QUERY_HEADS // KEY_VALUE_HEADS // heads
    blocks = PROMPT_TOKENS // rows
    slots = range(col_count)
    others = list(slots[1:])
    members = [col_at ^ d for d in slots]
    row_word = row_at.astype(jnp.int32).reshape(1)

    x_own = layer_input[0]
    up_own = out_grad[0]

    kv_cols = KEY_VALUE_HEADS * HEAD

    def kv_pick(weight, member):
        head = member // sharing
        return [
            lax.dynamic_slice_in_dim(weight, head * HEAD, HEAD, 1),
            lax.dynamic_slice_in_dim(weight, kv_cols + head * HEAD, HEAD, 1),
        ]

    cols = (heads + 2) * HEAD
    piece, head_piece = ln_attn.shape[0], q_gain.shape[0]
    rest = [jnp.pad(g, (0, piece - head_piece))[:, None] for g in (q_gain, k_gain)]
    rest = [router, ln_attn[:, None], ln_moe[:, None]] + rest
    wide = jnp.concatenate([w_q] + kv_pick(key_value_weight, col_at) + rest, axis=1)
    wide = jnp.pad(wide, ((0, 0), (0, -wide.shape[1] % HEAD)))
    wide = lax.all_gather(wide, "row", axis=0, tiled=True)
    extra = wide[:, cols:]
    router_all = extra[:, :experts]
    gain_one = extra[:, experts].astype(F32)[None]
    gain_two = extra[:, experts + 1].astype(F32)[None]
    head_gains = extra.reshape(row_count, piece, -1)[:, :head_piece].astype(F32)
    gain_q = head_gains[:, :, experts + 2].reshape(1, HEAD)
    gain_k = head_gains[:, :, experts + 3].reshape(1, HEAD)

    four = col_count == 4
    beside = near(layer_input, col_count)

    routes_all = lax.all_gather(routes[0], "row", axis=0)
    expert_ids = jnp.arange(experts, dtype=jnp.int32)
    flat_routes = routes_all.transpose(0, 2, 1)
    mask_all = jnp.any(flat_routes[:, :, None, :] == expert_ids[None, None, :, None], axis=1)
    mine_ids = jnp.stack([row_at * col_count + m for m in members]).astype(jnp.int32)
    has = jnp.stack(
        [lax.dynamic_index_in_dim(mask_all, e, 1, keepdims=False) for e in mine_ids], axis=1
    )
    place = jnp.arange(rows)
    before = (place[:, None] <= place[None, :]).astype(BF)
    order = jnp.einsum("rdt,tu->rdu", has.astype(BF), before, preferred_element_type=F32)
    rank = jnp.where(has, order.astype(jnp.int32) - 1, -1)
    rank_t = rank.transpose(0, 2, 1)
    mask_all = mask_all.astype(F32)

    def over_col(v):
        step = 1
        while step < col_count:
            v = v + swap(v, step, col_count)
            step *= 2
        return v

    load = over_col(jnp.sum(mask_all, axis=(0, 2))) / (tokens * TOPK)

    inv_freq = THETA ** (-2.0 * jnp.arange(HEAD // 2, dtype=F32) / HEAD)
    coses, sines = [], []
    for m in members:
        spots = lax.dynamic_index_in_dim(positions, m, 0, keepdims=False).astype(F32)
        angles = spots[:, None] * inv_freq[None, :]
        cos, sin = jnp.cos(angles), jnp.sin(angles)
        coses.append(jnp.concatenate([cos, cos], axis=1))
        sines.append(jnp.concatenate([-sin, sin], axis=1))

    beside, rank, rank_t, mask_all, coses, sines, load = lax.optimization_barrier(
        (beside, rank, rank_t, mask_all, coses, sines, load)
    )
    out_all = lax.all_gather(after(w_out, beside), "row", axis=1, tiled=True)
    xs = [x_own] + [v[0] for v in beside]
    if four:
        xs.append(jnp.concatenate(far(*beside, col_count), axis=1)[0])
    qs, kvs, normed, scales, every = [[None] * col_count for _ in range(5)]
    line = others + [0]
    batch = max(1, col_count // 2)
    for first in range(0, col_count, batch):
        ahead = line[first : first + batch]
        for d in ahead:
            qs[d], kvs[d], normed[d], scales[d] = qkv(
                xs[d], gain_one, wide, coses[d], sines[d], gain_q, gain_k, heads
            )
        got = jnp.concatenate([kvs[d] for d in ahead], axis=0)
        if first == 0:
            got, out_all, xs[-1] = lax.optimization_barrier((got, out_all, xs[-1]))
        got = lax.all_gather(got, "row", axis=0)
        for j, d in enumerate(ahead):
            every[d] = (got, j)
    gates, ups = after((w_gate, w_up), xs[-1])
    if four:
        gates_near, ups_near = [[near(v, col_count) for v in halves(w)] for w in (gates, ups)]
    else:
        gates_near, ups_near = [near(gates, col_count)], [near(ups, col_count)]
    mixes, logs = [None] * col_count, [None] * col_count
    hidden = x_own.astype(F32)
    share, sent = None, []
    for at, d in enumerate(line):
        q = qs[d]
        if at > 0:
            q = after(q, share)
        else:
            q, gates_near[0] = lax.optimization_barrier((q, gates_near[0]))
        mixes[d], logs[d] = attend(row_word, q, every[d], kvs[d], blocks)
        mix = mixes[d]
        if at == 0:
            mix, gates_near[-1] = lax.optimization_barrier((mix, gates_near[-1]))
        elif at == 1:
            mix, ups_near[0] = lax.optimization_barrier((mix, ups_near[0]))
        elif d == 0:
            mix, sent[: at - 1] = lax.optimization_barrier((mix, sent[: at - 1]))
        share = jnp.dot(mix, out_all, preferred_element_type=F32)
        if d != 0:
            share = share.astype(BF)
            sent.append(swap(share, d, col_count))
    share, sent = lax.optimization_barrier((share, sent))
    for got in sent:
        hidden = hidden + got.astype(F32)
    hidden = hidden + share
    up_all = lax.all_gather(after(up_own, mixes[line[0]]), "row", axis=0)

    spread = lax.rsqrt(jnp.mean(hidden * hidden, axis=-1, keepdims=True) + EPS)
    second = (hidden * spread * gain_two).astype(BF)
    second_all = lax.all_gather(second, "row", axis=0)

    downs_near = near(after(w_down, share), col_count)
    gate_all = [[w_gate]] + [list(v) for v in zip(*gates_near)]
    up_w_all = [[w_up]] + [list(v) for v in zip(*ups_near)]
    down_all = [[w_down]] + [[w] for w in downs_near]
    if four:
        rank, ups_near, down_all = lax.optimization_barrier((rank, ups_near, down_all))
        up_w_all = [[w_up]] + [list(v) for v in zip(*ups_near)]
        gates_near, _ = lax.optimization_barrier((gates_near, ups_near))
        far_of = lambda one, two: [swap(one[0], 2, col_count), swap(two[1], 1, col_count)]
        gate_all.append(far_of(*zip(*gates_near)))

    expert_up = [v.reshape(row_count * cap, width) for v in dispatch(rank, up_all, cap)]
    router_t = router_all.T
    second_all, expert_up, gate_all = lax.optimization_barrier((second_all, expert_up, gate_all))
    gate_pairs, *expert_in = route_dispatch(
        mine_ids, rank, second_all, mask_all, router_t, cap
    )
    expert_in = [v.reshape(row_count * cap, width) for v in expert_in]
    gate_pairs = gate_pairs.reshape(col_count, row_count * cap, 1)
    if four:
        up_w_all.append(far_of(*zip(*ups_near)))
        expert_in[0], up_w_all = lax.optimization_barrier((expert_in[0], up_w_all))
        down_far = far_of(*[halves(v[0]) for v in down_all[1:3]])
    kv_all = lax.all_gather(after(key_value_weight, expert_in[0]), "row", axis=0, tiled=True)
    ys, dbs, ms, duws, dgs = [[None] * col_count for _ in range(5)]
    grad_gu, grad_dn = [None] * col_count, [None] * col_count

    def gate_up_grad(d):
        grad_gu[d] = dot_tn(expert_in[d], duws[d]).astype(F32 if d == 0 else BF)

    def down_grad(d):
        grad_dn[d] = dot_tn(ms[d], expert_up[d]).astype(F32 if d == 0 else BF)

    far_sent = []
    order = [0, 3, 1, 2] if four else list(slots)
    for at, d in enumerate(order):
        if at > 0:
            held = [g for g in grad_gu + grad_dn if g is not None]
            expert_in[d] = after(expert_in[d], dgs[order[at - 1]], held)
        if four and at == 1:
            expert_in[d], down_far = lax.optimization_barrier((expert_in[d], down_far))
            down_all.append(down_far)
        weights = [gate_all[d], up_w_all[d], down_all[d]]
        ys[d], dbs[d], ms[d], duws[d], dgs[d] = expert(
            expert_in[d], expert_up[d], gate_pairs[d], weights
        )
        if four and at == 1:
            gate_up_grad(d)
            down_grad(d)
            far_sent = [deliver_far(grad_gu[d], col_count), deliver_far(grad_dn[d], col_count)]
    if four:
        dbs[0], far_sent[0] = lax.optimization_barrier((dbs[0], far_sent[0]))
    dbs[0], kv_all = lax.optimization_barrier((dbs[0], kv_all))
    db_part, score_grads = combine(rank_t, dbs, dgs)
    if four:
        score_grads, far_sent[1] = lax.optimization_barrier((score_grads, far_sent[1]))
    db_sum = lax.psum_scatter(db_part, "row", scatter_dimension=0)
    duws, ms, ys, _ = lax.optimization_barrier((duws, ms, ys, db_part))
    remaining = (1, 2) if four else range(1, col_count)
    for d in remaining:
        gate_up_grad(d)
    exchange = lambda sends: [swap(v, d, col_count) for d, v in enumerate(sends, 1)]
    gu_sends = grad_gu[1:]
    if four:
        gu_two, gu_one = far_sent[0]
        gu_sends = [join(grad_gu[1], gu_one, False), join(grad_gu[2], gu_two, True)]
    gu_got = exchange(gu_sends)
    ms, gu_sends = lax.optimization_barrier((ms, gu_sends))
    for d in remaining:
        down_grad(d)
    dn_sends = grad_dn[1:]
    if four:
        dn_two, dn_one = far_sent[1]
        dn_sends = [join(grad_dn[1], dn_one, False), join(grad_dn[2], dn_two, True)]
    gate_up_grad(0)
    down_grad(0)
    (y_part,) = combine(rank_t, ys)

    score_grads = lax.all_to_all(score_grads, "row", split_axis=0, concat_axis=0, tiled=True)
    mask_own = jnp.any(routes[0].T[:, None, :] == expert_ids[None, :, None], axis=0)
    logits = lax.dot_general(
        router_all, second, (((0,), (1,)), ((), ())), preferred_element_type=F32
    )
    probs = jax.nn.softmax(logits, axis=0)
    picked = jnp.where(mask_own, probs, 0.0)
    total = jnp.sum(picked, axis=0, keepdims=True)
    gates = picked / total
    to_member = jnp.stack(members)[:, None] == jnp.arange(col_count)[None, :]
    gate_grad = jnp.sum(
        jnp.where(to_member, score_grads[..., None], 0.0), axis=2
    )
    gate_grad = gate_grad.transpose(0, 2, 1).reshape(experts, rows)
    weighted = jnp.sum(gate_grad * gates, axis=0, keepdims=True)
    prob_grad = (
        jnp.where(mask_own, (gate_grad - weighted) / total, 0.0)
        + AUX_COEF * experts * load[:, None] / tokens
    )
    logit_low = (probs * (prob_grad - jnp.sum(probs * prob_grad, axis=0, keepdims=True))).astype(BF)
    grad_router = lax.dot_general(
        second, logit_low, (((0,), (1,)), ((), ())), preferred_element_type=F32
    )
    router_part = lax.dot_general(
        logit_low, router_all, (((0,), (1,)), ((), ())), preferred_element_type=F32
    )

    kv_weight = jnp.concatenate([w for m in members for w in kv_pick(kv_all, m)], axis=1)
    db_sum, gu_got, y_part, router_part, grad_router, kv_weight, own_grads, dn_sends = (
        lax.optimization_barrier(
            (
                db_sum, gu_got, y_part, router_part, grad_router, kv_weight,
                (grad_gu[0], grad_dn[0]), dn_sends,
            )
        )
    )
    y_sum = lax.psum_scatter(y_part, "row", scatter_dimension=0)
    second_grad = db_sum.astype(F32) + router_part
    hat = hidden * spread
    gain_two_grad = jnp.sum(second_grad * hat, axis=0)
    hidden_grad = up_own.astype(F32) + norm_back(second_grad, hat, spread, gain_two)
    branch = hidden_grad.astype(BF)

    beside = near(branch[None], col_count)
    branches = [branch] + [v[0] for v in beside]
    grad_qs, prompts, pairs, shares, sent, grad_kvs, kv_moved = [], [], [], [], [], [], []
    gain_q_grad, gain_k_grad = 0.0, 0.0

    def back_turn(v, cos, sin):
        moved = v * sin
        half = HEAD // 2
        return v * cos + jnp.concatenate([moved[:, half:], moved[:, :half]], axis=1)

    normed_all = jnp.stack(normed, axis=0)
    over_tokens = lambda a, b: lax.dot_general(
        a, b, (((0, 1), (0, 1)), ((), ())), preferred_element_type=F32
    )
    mixes_all = jnp.stack(mixes, axis=0)
    grad_out = None

    def to_owners(prompt):
        chunk = prompt.shape[2]
        return jnp.concatenate(
            [
                lax.ppermute(prompt, "row", [(rows // chunk * i + a, i) for i in range(blocks)])
                for a in range(rows // chunk)
            ],
            axis=2,
        )

    for d in slots:
        if d == col_count - 1:
            grad_out = jnp.stack(branches, axis=0)
            grad_out, y_sum, _ = lax.optimization_barrier((grad_out, y_sum, shares[-1]))
            grad_out = over_tokens(mixes_all, grad_out).astype(BF)
        if d == 1:
            beside, shares[0] = lax.optimization_barrier((beside, shares[0]))
            branches = [branch] + [v[0] for v in beside]
            if four:
                branches.append(jnp.concatenate(far(*beside, col_count), axis=1)[0])
            dn_sends, _ = lax.optimization_barrier((dn_sends, branches[-1]))
            dn_got = exchange(dn_sends)
        elif d > 1:
            branches[d], shares[-1] = lax.optimization_barrier((branches[d], shares[-1]))
        if d == 2 and four:
            branches[2], branches[3] = lax.optimization_barrier((branches[2], branches[3]))
        if d == col_count - 1:
            early_prompt = lax.psum_scatter(
                jnp.stack(prompts[:batch], axis=0), "row", scatter_dimension=2, tiled=True
            )
            branches[d], dn_got, grad_out, early_prompt = lax.optimization_barrier(
                (branches[d], dn_got, grad_out, early_prompt)
            )
            early_prompt = to_owners(early_prompt)
            grad_out = lax.psum_scatter(grad_out, "row", scatter_dimension=1, tiled=True)
        mix_grad = dot_nt(branches[d], out_all).astype(BF)
        if d == 2:
            sent[0] = swap(after(shares[1], mix_grad), 1, col_count)
        grad_q, grad_prompt, pair, gain_part = attend_back(
            row_word, qs[d], every[d], kvs[d], blocks, mix_grad, mixes[d], logs[d], scales[d],
            coses[d], sines[d], gain_q,
        )
        grad_qs.append(grad_q)
        prompts.append(grad_prompt)
        pairs.append(pair)
        gain_q_grad = gain_q_grad + gain_part[0]
        if d == col_count - 1:
            grad_q, prompts[-1], pairs[-1], sent, early_prompt, grad_out = lax.optimization_barrier(
                (grad_q, prompts[-1], pairs[-1], sent, early_prompt, grad_out)
            )
        share = input_share(grad_q, wide, F32 if d == 0 else BF)
        shares.append(share)
        if d > 0:
            sent.append(swap(share, d, col_count))
    grad_q = over_tokens(normed_all, after(jnp.stack(grad_qs, axis=0), shares[-1]))
    gain_one_grad = jnp.sum(grad_q * wide[:, : heads * HEAD].astype(F32), axis=1)
    grad_q = grad_q.astype(BF)
    late_prompt = lax.psum_scatter(
        jnp.stack(prompts[batch:], axis=0), "row", scatter_dimension=2, tiled=True
    )
    early_prompt = after(early_prompt, shares[-1])
    for first in range(0, col_count, batch):
        prompt = early_prompt
        if first > 0:
            late_prompt, grad_q, _ = lax.optimization_barrier((late_prompt, grad_q, grad_kvs))
            prompt = to_owners(late_prompt)
        for d in range(first, first + batch):
            pair = pairs[d] + prompt[d - first].astype(F32)
            key_dy = back_turn(pair[0], coses[d], sines[d])
            key_hat = back_turn(kvs[d][0].astype(F32), coses[d], sines[d]) / gain_k
            gain_k_grad = gain_k_grad + jnp.sum(key_dy * key_hat, axis=0)
            key_raw = norm_back(key_dy, key_hat, scales[d][:, heads : heads + 1], gain_k)
            grad_kv = jnp.concatenate([key_raw.astype(BF), pair[1].astype(BF)], axis=1)
            grad_kvs.append(grad_kv)
            kv_moved.append(grad_kv if d == 0 else swap(grad_kv, d, col_count))
    grad_q = lax.psum_scatter(grad_q, "row", scatter_dimension=0, tiled=True)

    grad_kv = over_tokens(normed_all, jnp.stack(grad_kvs, axis=0))
    gain_one_grad = gain_one_grad + jnp.sum(
        grad_kv * wide[:, heads * HEAD : cols].astype(F32), axis=1
    )
    gain_one_grad = gain_one_grad / gain_one[0]
    grad_kv = lax.all_to_all(
        grad_kv.astype(BF).reshape(devices, -1, 2 * HEAD),
        ("row", "col"),
        split_axis=0,
        concat_axis=0,
        tiled=True,
    )
    grad_kv = jnp.sum(grad_kv.astype(F32).reshape(row_count, col_count, -1, 2 * HEAD), axis=0)
    grad_kv = grad_kv.reshape(KEY_VALUE_HEADS, sharing, -1, 2, HEAD).sum(axis=1)
    grad_kv = grad_kv.transpose(1, 2, 0, 3).reshape(-1, 2 * kv_cols)
    tail = [grad_router, gain_two_grad, gain_one_grad, gain_q_grad, gain_k_grad]
    tail = [v.reshape(devices, -1) for v in tail]
    tail.append(jnp.broadcast_to(jnp.sum(probs, axis=1)[None], (devices, experts)))
    cuts = [0]
    for v in tail:
        cuts.append(cuts[-1] + v.shape[1])
    tail = lax.all_to_all(
        jnp.concatenate(tail, axis=1), ("row", "col"), split_axis=0, concat_axis=0, tiled=True
    )
    tail = jnp.sum(tail, axis=0)
    grad_router, gain_two_grad, gain_one_grad, gain_q_grad, gain_k_grad, mean_probs = [
        tail[a:b] for a, b in zip(cuts[:-1], cuts[1:])
    ]
    mean_probs = mean_probs / tokens
    aux_loss = experts * jnp.sum(load * mean_probs)
    expert_load = jnp.stack([experts * load, experts * mean_probs])

    kv_share = dot_nt(jnp.concatenate(kv_moved, axis=1), kv_weight)
    input_sum = shares[0] + kv_share
    for got in sent:
        input_sum = input_sum + got.astype(F32)
    x_wide = x_own.astype(F32)
    x_spread = lax.rsqrt(jnp.mean(x_wide * x_wide, axis=-1, keepdims=True) + EPS)
    x_hat = x_wide * x_spread
    input_grad = hidden_grad + norm_back(input_sum, x_hat, x_spread, gain_one)

    own_grads, _ = lax.optimization_barrier((own_grads, shares[-1]))
    ffe = w_gate.shape[2]
    grad_gate = own_grads[0][:, :ffe] + sum(v[:, :ffe].astype(F32) for v in gu_got)
    grad_up = own_grads[0][:, ffe:] + sum(v[:, ffe:].astype(F32) for v in gu_got)
    grad_down = own_grads[1] + sum(v.astype(F32) for v in dn_got)
    layer_output = (hidden + y_sum.astype(F32)).astype(BF)

    return (
        layer_output[None],
        aux_loss,
        input_grad[None],
        grad_q.astype(F32),
        grad_kv,
        grad_out.astype(F32),
        grad_router.reshape(width // devices, experts),
        gain_one_grad,
        gain_two_grad,
        gain_q_grad,
        gain_k_grad,
        grad_gate[None],
        grad_up[None],
        grad_down[None],
        expert_load,
    )


def solution(mesh):
    in_specs = (
        P("col", "row", None),
        P("col", "row", None),
        P("col", "row", None),
        P(None, "row"),
        P("row", "col"),
        P("row", None),
        P("col", "row"),
        P("row", None),
        P("row"),
        P("row"),
        P("row"),
        P("row"),
        P(("row", "col"), None, None),
        P(("row", "col"), None, None),
        P(("row", "col"), None, None),
    )
    out_specs = (
        P("col", "row", None),
        P(),
        P("col", "row", None),
        P("row", "col"),
        P(("row", "col"), None),
        P("col", "row"),
        P(("row", "col"), None),
        P(("row", "col")),
        P(("row", "col")),
        P(("row", "col")),
        P(("row", "col")),
        P(("row", "col"), None, None),
        P(("row", "col"), None, None),
        P(("row", "col"), None, None),
        P(),
    )
    return jax.shard_map(
        per_device, mesh=mesh, in_specs=in_specs, out_specs=out_specs, check_vma=False
    )
```

```python
from functools import partial
import math

import jax
import jax.numpy as jnp
from jax import lax
from jax.experimental import pallas as pl
from jax.experimental.pallas import tpu as pltpu
from jax.sharding import PartitionSpec as P

QUERY_HEADS = 32
KEY_VALUE_HEADS = 4
HEAD = 128
TOPK = 8
CONT = 256
PROMPT_TOKENS = 2048

EPS = 1e-06
THETA = 1000000.0
AUX_COEF = 0.001
LN2 = math.log(2.0)
SCALE2 = 1.0 / (math.sqrt(HEAD) * LN2)
VMEM = 56 * 1024 * 1024

BF = jnp.bfloat16
F32 = jnp.float32


def dot_nn(a, b):
    return lax.dot_general(a, b, (((1,), (0,)), ((), ())), preferred_element_type=F32)


def dot_nt(a, b):
    return lax.dot_general(a, b, (((1,), (1,)), ((), ())), preferred_element_type=F32)


def dot_tn(a, b):
    return lax.dot_general(a, b, (((0,), (0,)), ((), ())), preferred_element_type=F32)


def call(body, name, grid, in_specs, out_specs, out_shape, scratch=(), flops=0, moved=0, prefetch=0):
    return pl.pallas_call(
        body,
        name=name,
        grid_spec=pltpu.PrefetchScalarGridSpec(
            num_scalar_prefetch=prefetch,
            grid=grid,
            in_specs=in_specs,
            out_specs=out_specs,
            scratch_shapes=list(scratch),
        ),
        out_shape=out_shape,
        cost_estimate=pl.CostEstimate(
            flops=int(flops), bytes_accessed=int(moved), transcendentals=0
        ),
        compiler_params=pltpu.CompilerParams(
            dimension_semantics=("arbitrary",) * len(grid), vmem_limit_bytes=VMEM
        ),
    )


def struct(shape, dtype):
    return jax.ShapeDtypeStruct(shape, dtype)


def turn(v, cos, sin):
    return v * cos + pltpu.roll(v, HEAD // 2, 1) * sin


def turn_back(v, cos, sin):
    return v * cos + pltpu.roll(v * sin, HEAD // 2, 1)


def qkv_body(heads, x_ref, gain_ref, w_ref, cos_ref, sin_ref, qg_ref, kg_ref, q_ref, kv_ref, a_ref, r_ref):
    x = x_ref[...].astype(F32)
    normed = x * lax.rsqrt(jnp.mean(x * x, axis=-1, keepdims=True) + EPS) * gain_ref[...]
    low = normed.astype(BF)
    a_ref[...] = low
    raw = dot_nn(low, w_ref[...])
    cos = cos_ref[...]
    sin = sin_ref[...]
    lane = lax.broadcasted_iota(jnp.int32, (x.shape[0], HEAD), 1)
    scales = jnp.zeros((x.shape[0], HEAD), F32)
    for h in range(heads + 1):
        v = raw[:, h * HEAD : (h + 1) * HEAD]
        r = lax.rsqrt(jnp.mean(v * v, axis=-1, keepdims=True) + EPS)
        scales = jnp.where(lane == h, r, scales)
        if h < heads:
            q_ref[h] = (turn(v * r * qg_ref[...], cos, sin) * SCALE2).astype(BF)
        else:
            kv_ref[0] = turn(v * r * kg_ref[...], cos, sin).astype(BF)
    kv_ref[1] = raw[:, (heads + 1) * HEAD :].astype(BF)
    r_ref[...] = scales


def qkv(x, gain, w, cos, sin, qg, kg, heads):
    rows, width = x.shape
    cols = (heads + 2) * HEAD
    tile = 256
    whole = lambda i: (0, 0)
    row = lambda i: (i, 0)
    return call(
        partial(qkv_body, heads),
        "qkv",
        (rows // tile,),
        [
            pl.BlockSpec((tile, width), row),
            pl.BlockSpec((1, width), whole),
            pl.BlockSpec((width, cols), whole),
            pl.BlockSpec((tile, HEAD), row),
            pl.BlockSpec((tile, HEAD), row),
            pl.BlockSpec((1, HEAD), whole),
            pl.BlockSpec((1, HEAD), whole),
        ],
        [
            pl.BlockSpec((heads, tile, HEAD), lambda i: (0, i, 0)),
            pl.BlockSpec((2, tile, HEAD), lambda i: (0, i, 0)),
            pl.BlockSpec((tile, width), row),
            pl.BlockSpec((tile, HEAD), row),
        ],
        [
            struct((heads, rows, HEAD), BF),
            struct((2, rows, HEAD), BF),
            struct((rows, width), BF),
            struct((rows, HEAD), F32),
        ],
        flops=2 * rows * width * cols,
        moved=2 * (2 * rows * width + width * cols + rows * cols),
    )(x, gain, w, cos, sin, qg, kg)


def causal(count):
    q_at = lax.broadcasted_iota(jnp.int32, (count, CONT, CONT), 1)
    k_at = lax.broadcasted_iota(jnp.int32, (count, CONT, CONT), 2)
    return (k_at <= q_at).reshape(count * CONT, CONT)


def attend_body(heads, per, blocks, rows, row_ref, q_ref, kp_ref, vp_ref, kv_ref, o_ref, l_ref, vp_one, vl_one, acc):
    at = pl.program_id(0)
    part = pl.program_id(1)
    row = row_ref[0]

    @pl.when((at == 0) & (part == 0))
    def _():
        for j in range(blocks):
            vp_one[j * rows : (j + 1) * rows, :HEAD] = vp_ref[j, 0]
        vp_one[:, HEAD:] = jnp.ones((blocks * rows, HEAD), BF)
        vl_one[:, :HEAD] = kv_ref[1]
        vl_one[:, HEAD:] = jnp.ones((rows, HEAD), BF)

    q = q_ref[...].reshape(per * CONT, HEAD)
    here = pl.ds(pl.multiple_of(at * CONT, CONT), CONT)
    weights = jnp.where(causal(per), jnp.exp2(dot_nt(q, kv_ref[0, here, :])), 0.0).astype(BF)
    acc[...] = dot_nn(weights, vl_one[here, :])

    @pl.when(row < blocks)
    def _():
        for j in range(rows // CONT - 1):

            @pl.when(j < at)
            def _():
                piece = slice(j * CONT, (j + 1) * CONT)
                weights = jnp.exp2(dot_nt(q, kv_ref[0, piece, :])).astype(BF)
                acc[...] += dot_nn(weights, vl_one[piece, :])

        @pl.loop(0, row)
        def _(j):
            weights = jnp.exp2(dot_nt(q, kp_ref[j, 0])).astype(BF)
            acc[...] += dot_nn(weights, vp_one[pl.ds(pl.multiple_of(j * rows, rows), rows), :])

    @pl.when(row >= blocks)
    def _():
        keys = kp_ref[...].reshape(blocks * rows, HEAD)
        weights = jnp.exp2(dot_nt(q, keys)).astype(BF)
        acc[...] += dot_nn(weights, vp_one[...])

    total = acc[:, HEAD:]
    out = (acc[:, :HEAD] / total).astype(BF)
    logs = jnp.log2(total)
    lane = lax.broadcasted_iota(jnp.int32, (CONT, HEAD), 1)

    @pl.when(part == 0)
    def _():
        l_ref[...] = jnp.zeros((CONT, HEAD), F32)

    held = l_ref[...]
    for p in range(per):
        o_ref[:, p * HEAD : (p + 1) * HEAD] = out[p * CONT : (p + 1) * CONT]
        held = jnp.where(lane == part * per + p, logs[p * CONT : (p + 1) * CONT], held)
    l_ref[...] = held


def attend(row, q, every, kv, blocks):
    heads, rows, _ = q.shape
    per = min(4, heads)
    every, place = every
    keys = blocks * rows
    return call(
        partial(attend_body, heads, per, blocks, rows),
        "attend",
        (rows // CONT, heads // per),
        [
            pl.BlockSpec((per, CONT, HEAD), lambda i, h, s: (h, i, 0)),
            pl.BlockSpec((blocks, 1, rows, HEAD), lambda i, h, s: (0, 2 * place, 0, 0)),
            pl.BlockSpec((blocks, 1, rows, HEAD), lambda i, h, s: (0, 2 * place + 1, 0, 0)),
            pl.BlockSpec((2, rows, HEAD), lambda i, h, s: (0, 0, 0)),
        ],
        [
            pl.BlockSpec((CONT, per * HEAD), lambda i, h, s: (i, h)),
            pl.BlockSpec((CONT, HEAD), lambda i, h, s: (i, 0)),
        ],
        [struct((rows, heads * HEAD), BF), struct((rows, HEAD), F32)],
        scratch=[
            pltpu.VMEM((keys, 2 * HEAD), BF),
            pltpu.VMEM((rows, 2 * HEAD), BF),
            pltpu.VMEM((per * CONT, 2 * HEAD), F32),
        ],
        flops=8 * rows * heads * (keys + CONT) * HEAD,
        moved=2 * HEAD * (2 * rows * heads + 2 * keys),
        prefetch=1,
    )(row, q, every, every, kv)


def attend_back_body(
    heads, per, blocks, rows,
    row_ref, q_ref, kp_ref, vp_ref, kv_ref, do_ref, o_ref, l_ref, r_ref, cos_ref, sin_ref, qg_ref,
    dq_ref, dp_ref, dl_ref, g_ref,
    dq, dkp, dvp,
):
    at = pl.program_id(0)
    part = pl.program_id(1)
    row = row_ref[0]

    @pl.when((at == 0) & (part == 0))
    def _():
        dkp[...] = jnp.zeros_like(dkp)
        dvp[...] = jnp.zeros_like(dvp)
        dl_ref[...] = jnp.zeros_like(dl_ref)
        g_ref[...] = jnp.zeros_like(g_ref)

    q = q_ref[...].reshape(per * CONT, HEAD)
    lane = lax.broadcasted_iota(jnp.int32, (CONT, HEAD), 1)
    line = lax.broadcasted_iota(jnp.int32, (HEAD, CONT), 0)
    logs_t = l_ref[...].T
    do_parts, logs, centers, scales = [], [], [], []
    for p in range(per):
        do_part = do_ref[:, p * HEAD : (p + 1) * HEAD]
        do_parts.append(do_part)
        both = do_part.astype(F32) * o_ref[:, p * HEAD : (p + 1) * HEAD].astype(F32)
        centers.append(jnp.sum(both.T, axis=0, keepdims=True))
        head = part * per + p
        logs.append(jnp.sum(jnp.where(line == head, logs_t, 0.0), axis=0, keepdims=True))
        scales.append(jnp.sum(jnp.where(lane == head, r_ref[...], 0.0), axis=-1, keepdims=True))
    do = jnp.concatenate(do_parts, axis=0)
    center = jnp.concatenate(centers, axis=1)
    log = jnp.concatenate(logs, axis=1)

    def block(k, v, mask):
        probs = jnp.exp2(dot_nt(k, q) - log)
        if mask is not None:
            probs = jnp.where(mask, probs, 0.0)
        ds = (probs * (dot_nt(v, do) - center)).astype(BF)
        return dot_tn(ds, k), dot_nn(ds, q), dot_nn(probs.astype(BF), do)

    k_at = lax.broadcasted_iota(jnp.int32, (CONT, CONT), 0)
    q_at = lax.broadcasted_iota(jnp.int32, (CONT, CONT), 1)
    seen = jnp.concatenate([k_at <= q_at] * per, axis=1)
    here = pl.ds(pl.multiple_of(at * CONT, CONT), CONT)
    a, b, c = block(kv_ref[0, here, :], kv_ref[1, here, :], seen)
    dq[...] = a
    dl_ref[0, here, :] += b
    dl_ref[1, here, :] += c

    @pl.when(row < blocks)
    def _():
        for j in range(rows // CONT - 1):

            @pl.when(j < at)
            def _():
                piece = slice(j * CONT, (j + 1) * CONT)
                a, b, c = block(kv_ref[0, piece, :], kv_ref[1, piece, :], None)
                dq[...] += a
                dl_ref[0, piece, :] += b
                dl_ref[1, piece, :] += c

    @pl.loop(0, jnp.minimum(row, blocks))
    def _(j):
        a, b, c = block(kp_ref[j, 0], vp_ref[j, 0], None)
        piece = pl.ds(pl.multiple_of(j * rows, rows), rows)
        dq[...] += a
        dkp[piece, :] += b
        dvp[piece, :] += c

    cos = cos_ref[...]
    sin = sin_ref[...]
    gain = qg_ref[...]
    tally = jnp.zeros((1, HEAD), F32)
    for p in range(per):
        dy = turn_back(dq[p * CONT : (p + 1) * CONT, :] * (SCALE2 * LN2), cos, sin)
        hat = turn_back(q[p * CONT : (p + 1) * CONT].astype(F32), cos, sin) * (1.0 / SCALE2) / gain
        tally += jnp.sum(dy * hat, axis=0, keepdims=True)
        dyg = dy * gain
        raw = scales[p] * (dyg - hat * jnp.mean(dyg * hat, axis=-1, keepdims=True))
        dq_ref[:, p * HEAD : (p + 1) * HEAD] = raw.astype(BF)
    g_ref[0:1, :] += tally

    @pl.when((at == rows // CONT - 1) & (part == heads // per - 1))
    def _():
        dp_ref[0] = (dkp[...] * LN2).astype(BF)
        dp_ref[1] = dvp[...].astype(BF)
        dl_ref[0] = dl_ref[0] * LN2


def attend_back(row, q, every, kv, blocks, do, o, logs, scales, cos, sin, qg):
    heads, rows, _ = q.shape
    per = min(8, heads)
    every, place = every
    keys = blocks * rows
    tile = lambda i, h, s: (i, 0)
    head = lambda i, h, s: (i, h)
    return call(
        partial(attend_back_body, heads, per, blocks, rows),
        "attend_back",
        (rows // CONT, heads // per),
        [
            pl.BlockSpec((per, CONT, HEAD), lambda i, h, s: (h, i, 0)),
            pl.BlockSpec((blocks, 1, rows, HEAD), lambda i, h, s: (0, 2 * place, 0, 0)),
            pl.BlockSpec((blocks, 1, rows, HEAD), lambda i, h, s: (0, 2 * place + 1, 0, 0)),
            pl.BlockSpec((2, rows, HEAD), lambda i, h, s: (0, 0, 0)),
            pl.BlockSpec((CONT, per * HEAD), head),
            pl.BlockSpec((CONT, per * HEAD), head),
            pl.BlockSpec((CONT, HEAD), tile),
            pl.BlockSpec((CONT, HEAD), tile),
            pl.BlockSpec((CONT, HEAD), tile),
            pl.BlockSpec((CONT, HEAD), tile),
            pl.BlockSpec((1, HEAD), lambda i, h, s: (0, 0)),
        ],
        [
            pl.BlockSpec((CONT, per * HEAD), head),
            pl.BlockSpec((2, keys, HEAD), lambda i, h, s: (0, 0, 0)),
            pl.BlockSpec((2, rows, HEAD), lambda i, h, s: (0, 0, 0)),
            pl.BlockSpec((8, HEAD), lambda i, h, s: (0, 0)),
        ],
        [
            struct((rows, heads * HEAD), BF),
            struct((2, keys, HEAD), BF),
            struct((2, rows, HEAD), F32),
            struct((8, HEAD), F32),
        ],
        scratch=[
            pltpu.VMEM((per * CONT, HEAD), F32),
            pltpu.VMEM((keys, HEAD), F32),
            pltpu.VMEM((keys, HEAD), F32),
        ],
        flops=20 * rows * heads * (keys + CONT) * HEAD,
        moved=2 * HEAD * (4 * rows * heads + 4 * keys),
        prefetch=1,
    )(row, q, every, every, kv, do, o, logs, scales, cos, sin, qg)


def dispatch_body(count, cap, rank_ref, rows_ref, *out_refs):
    tokens = rows_ref.shape[1]
    slot = lax.broadcasted_iota(jnp.int32, (cap, tokens), 0)
    for d in range(count):
        hot = (rank_ref[0, d : d + 1, :] == slot).astype(F32).astype(BF)
        out_refs[d][0] = dot_nn(hot, rows_ref[0]).astype(BF)


def dispatch(rank, rows, cap):
    sources, count, tokens = rank.shape
    width = rows.shape[2]
    return call(
        partial(dispatch_body, count, cap),
        "dispatch",
        (sources,),
        [
            pl.BlockSpec((1, count, tokens), lambda s: (s, 0, 0)),
            pl.BlockSpec((1, tokens, width), lambda s: (s, 0, 0)),
        ],
        [pl.BlockSpec((1, cap, width), lambda s: (s, 0, 0))] * count,
        [struct((sources, cap, width), BF)] * count,
        flops=2 * sources * count * cap * tokens * width,
        moved=2 * sources * width * (tokens + count * cap),
    )(rank, rows)


def route_body(count, cap, ids_ref, rank_ref, rows_ref, mask_ref, router_ref, gate_ref, *out_refs):
    tokens = rows_ref.shape[1]
    rows = rows_ref[0]
    logits = dot_nt(router_ref[...], rows)
    weights = jnp.exp(logits - jnp.max(logits, axis=0, keepdims=True))
    probs = weights / jnp.sum(weights, axis=0, keepdims=True)
    picked = probs * mask_ref[0]
    gates = picked / jnp.sum(picked, axis=0, keepdims=True)
    expert_at = lax.broadcasted_iota(jnp.int32, gates.shape, 0)
    slot = lax.broadcasted_iota(jnp.int32, (cap, tokens), 0)
    for d in range(count):
        here = rank_ref[0, d : d + 1, :] == slot
        out_refs[d][0] = dot_nn(here.astype(F32).astype(BF), rows).astype(BF)
        mine = jnp.sum(jnp.where(expert_at == ids_ref[d], gates, 0.0), axis=0, keepdims=True)
        gate_ref[d, 0] = jnp.sum(jnp.where(here, mine, 0.0), axis=1, keepdims=True)


def route_dispatch(ids, rank, rows, mask, router, cap):
    sources, count, tokens = rank.shape
    width = rows.shape[2]
    experts = router.shape[0]
    return call(
        partial(route_body, count, cap),
        "route_dispatch",
        (sources,),
        [
            pl.BlockSpec((1, count, tokens), lambda s, i: (s, 0, 0)),
            pl.BlockSpec((1, tokens, width), lambda s, i: (s, 0, 0)),
            pl.BlockSpec((1, experts, tokens), lambda s, i: (s, 0, 0)),
            pl.BlockSpec((experts, width), lambda s, i: (0, 0)),
        ],
        [
            pl.BlockSpec((count, 1, cap, 1), lambda s, i: (0, s, 0, 0)),
        ]
        + [pl.BlockSpec((1, cap, width), lambda s, i: (s, 0, 0))] * count,
        [struct((count, sources, cap, 1), F32)]
        + [struct((sources, cap, width), BF)] * count,
        flops=2 * sources * count * cap * tokens * width,
        moved=2 * sources * width * (tokens + count * cap),
        prefetch=1,
    )(ids, rank, rows, mask, router)


def share_body(g_ref, w_ref, out_ref):
    out_ref[...] = dot_nt(g_ref[...], w_ref[...]).astype(out_ref.dtype)


def input_share(grads, w, dtype):
    rows, cols = grads.shape
    width = w.shape[0]
    tile = 256
    return call(
        share_body,
        "input_share",
        (rows // tile,),
        [
            pl.BlockSpec((tile, cols), lambda i: (i, 0)),
            pl.BlockSpec((width, cols), lambda i: (0, 0)),
        ],
        pl.BlockSpec((tile, width), lambda i: (i, 0)),
        struct((rows, width), dtype),
        flops=2 * rows * width * cols,
        moved=2 * (rows * width + width * cols + rows * cols),
    )(grads, w)


def combine_body(count, cap, scored, rank_ref, *refs):
    tokens = rank_ref.shape[1]
    slot = lax.broadcasted_iota(jnp.int32, (tokens, cap), 1)
    hots = [(rank_ref[0, :, d : d + 1] == slot).astype(F32).astype(BF) for d in range(count)]

    def gathered(parts):
        if cap % HEAD:
            return sum(dot_nn(hot, part[0]) for hot, part in zip(hots, parts))
        return dot_nn(
            jnp.concatenate(hots, axis=1), jnp.concatenate([p[0] for p in parts], axis=0)
        )

    refs[count * (2 if scored else 1)][0] = gathered(refs[:count]).astype(BF)
    if scored:
        scores = gathered(refs[count : 2 * count])
        lane = lax.broadcasted_iota(jnp.int32, scores.shape, 1)
        for d in range(count):
            mine = jnp.where(lane // 4 == d, scores, 0.0)
            refs[-1][0, :, d : d + 1] = jnp.sum(mine, axis=-1, keepdims=True)


def combine(rank_t, parts, scores=()):
    sources, tokens, count = rank_t.shape
    cap = parts[0].shape[0] // sources
    width = parts[0].shape[1]
    at = lambda s: (s, 0, 0)
    cut = lambda v: v.reshape(sources, cap, v.shape[1])
    out_specs = [pl.BlockSpec((1, tokens, width), at)]
    out_shape = [struct((sources, tokens, width), BF)]
    if scores:
        out_specs.append(pl.BlockSpec((1, tokens, count), at))
        out_shape.append(struct((sources, tokens, count), F32))
    return call(
        partial(combine_body, count, cap, bool(scores)),
        "combine",
        (sources,),
        [pl.BlockSpec((1, tokens, count), at)]
        + [pl.BlockSpec((1, cap, width), at)] * count
        + [pl.BlockSpec((1, cap, HEAD), at)] * len(scores),
        out_specs,
        out_shape,
    )(rank_t, *[cut(p) for p in parts], *[cut(p) for p in scores])


def expert_body(
    slot, x_ref, up_ref, gate_ref, wga_ref, wgb_ref, wua_ref, wub_ref, wda_ref, wdb_ref,
    db_ref, m_ref, duw_ref, dg_ref,
):
    half = wga_ref.shape[1]
    hidden = wga_ref.shape[2]
    xa, xb = x_ref[:, :half], x_ref[:, half:]
    gate = gate_ref[...]
    u = dot_nn(xa, wga_ref[0]) + dot_nn(xb, wgb_ref[0])
    w = dot_nn(xa, wua_ref[0]) + dot_nn(xb, wub_ref[0])
    sigma = 1.0 / (1.0 + jnp.exp(-u))
    silu = u * sigma
    inner = silu * w
    low = inner.astype(BF)
    m_ref[...] = (inner * gate).astype(BF)
    up = up_ref[...]
    back = jnp.concatenate([dot_nt(up, wda_ref[0]), dot_nt(up, wdb_ref[0])], axis=1)
    score = jnp.sum(low.astype(F32) * back, axis=-1, keepdims=True)
    lane = lax.broadcasted_iota(jnp.int32, dg_ref.shape, 1)
    high = score.astype(BF)
    rest = score - high.astype(F32)
    middle = rest.astype(BF)
    last = (rest - middle.astype(F32)).astype(BF)
    pieces = jnp.where(lane == 4 * slot, high.astype(F32), 0.0)
    pieces = jnp.where(lane == 4 * slot + 1, middle.astype(F32), pieces)
    dg_ref[...] = jnp.where(lane == 4 * slot + 2, last.astype(F32), pieces).astype(BF)
    back = back * gate
    du = (back * w * sigma * (1.0 + u * (1.0 - sigma))).astype(BF)
    dw = (back * silu).astype(BF)
    duw_ref[:, :hidden] = du
    duw_ref[:, hidden:] = dw
    db_ref[:, :half] = (dot_nt(du, wga_ref[0]) + dot_nt(dw, wua_ref[0])).astype(BF)
    db_ref[:, half:] = (dot_nt(du, wgb_ref[0]) + dot_nt(dw, wub_ref[0])).astype(BF)


def expert(slot, x, up, gate, weights):
    rows, width = x.shape
    hidden = weights[0][0].shape[2]
    tile = min(256, rows)
    at = lambda i: (i, 0)
    specs, arrays = [], []
    for parts in weights:
        shape = (1, parts[0].shape[1] * len(parts) // 2, parts[0].shape[2])
        for j in range(2):
            place = j if len(parts) == 1 else 0
            specs.append(pl.BlockSpec(shape, lambda i, place=place: (0, place, 0)))
            arrays.append(parts[0] if len(parts) == 1 else parts[j])
    return call(
        partial(expert_body, slot),
        "expert",
        (rows // tile,),
        [
            pl.BlockSpec((tile, width), at),
            pl.BlockSpec((tile, width), at),
            pl.BlockSpec((tile, 1), at),
        ]
        + specs,
        [
            pl.BlockSpec((tile, width), at),
            pl.BlockSpec((tile, hidden), at),
            pl.BlockSpec((tile, 2 * hidden), at),
            pl.BlockSpec((tile, HEAD), at),
        ],
        [
            struct((rows, width), BF),
            struct((rows, hidden), BF),
            struct((rows, 2 * hidden), BF),
            struct((rows, HEAD), BF),
        ],
        flops=10 * rows * width * hidden,
        moved=2 * (3 * rows * width + 3 * rows * hidden + 3 * width * hidden),
    )(x, up, gate, *arrays)


def swap(v, step, count):
    return lax.ppermute(v, "col", [(i, i ^ step) for i in range(count)])


def near(v, count):
    return [swap(v, d, count) for d in ((1, 2) if count == 4 else range(1, count))]


def far(one, two, count):
    half = one.shape[1] // 2
    return [swap(one[:, :half], 2, count), swap(two[:, half:], 1, count)]


def halves(v):
    return v[:, : v.shape[1] // 2], v[:, v.shape[1] // 2 :]


def whole(parts):
    return parts[0] if len(parts) == 1 else jnp.concatenate(parts, axis=1)


def deliver_far(part, count):
    half = part.shape[0] // 2
    return swap(part[:half], 1, count), swap(part[half:], 2, count)


def join(part, got, first):
    half = part.shape[0] // 2
    wide = jnp.pad(got.astype(F32), ((0, half) if first else (half, 0), (0, 0)))
    return (part.astype(F32) + wide).astype(BF)


def after(value, *earlier):
    return lax.optimization_barrier((value,) + earlier)[0]


def norm_back(grad, hat, spread, gain):
    scaled = grad * gain
    return spread * (scaled - hat * jnp.mean(scaled * hat, axis=-1, keepdims=True))


def per_device(
    layer_input, out_grad, routes, positions, w_q, key_value_weight, w_out, router,
    ln_attn, ln_moe, q_gain, k_gain, w_gate, w_up, w_down,
):
    rows, width = layer_input.shape[1:]
    row_count, col_count = lax.axis_size("row"), lax.axis_size("col")
    row_at, col_at = lax.axis_index("row"), lax.axis_index("col")
    devices = row_count * col_count
    experts = w_gate.shape[0] * devices
    assert w_gate.shape[0] == 1
    cap = rows * TOPK // experts
    tokens = rows * devices
    heads = w_q.shape[1] // HEAD
    sharing = QUERY_HEADS // KEY_VALUE_HEADS // heads
    blocks = PROMPT_TOKENS // rows
    slots = range(col_count)
    others = list(slots[1:])
    members = [col_at ^ d for d in slots]
    row_word = row_at.astype(jnp.int32).reshape(1)

    x_own = layer_input[0]
    up_own = out_grad[0]

    kv_cols = KEY_VALUE_HEADS * HEAD

    def kv_pick(weight, member):
        head = member // sharing
        return [
            lax.dynamic_slice_in_dim(weight, head * HEAD, HEAD, 1),
            lax.dynamic_slice_in_dim(weight, kv_cols + head * HEAD, HEAD, 1),
        ]

    cols = (heads + 2) * HEAD
    piece, head_piece = ln_attn.shape[0], q_gain.shape[0]
    rest = [jnp.pad(g, (0, piece - head_piece))[:, None] for g in (q_gain, k_gain)]
    rest = [router, ln_attn[:, None], ln_moe[:, None]] + rest
    wide = jnp.concatenate([w_q] + kv_pick(key_value_weight, col_at) + rest, axis=1)
    wide = jnp.pad(wide, ((0, 0), (0, -wide.shape[1] % HEAD)))
    wide = lax.all_gather(wide, "row", axis=0, tiled=True)
    extra = wide[:, cols:]
    router_all = extra[:, :experts]
    gain_one = extra[:, experts].astype(F32)[None]
    gain_two = extra[:, experts + 1].astype(F32)[None]
    head_gains = extra.reshape(row_count, piece, -1)[:, :head_piece].astype(F32)
    gain_q = head_gains[:, :, experts + 2].reshape(1, HEAD)
    gain_k = head_gains[:, :, experts + 3].reshape(1, HEAD)

    four = col_count == 4
    beside = near(layer_input, col_count)

    routes_all = lax.all_gather(routes[0], "row", axis=0)
    expert_ids = jnp.arange(experts, dtype=jnp.int32)
    flat_routes = routes_all.transpose(0, 2, 1)
    mask_all = jnp.any(flat_routes[:, :, None, :] == expert_ids[None, None, :, None], axis=1)
    mine_ids = jnp.stack([row_at * col_count + m for m in members]).astype(jnp.int32)
    has = jnp.stack(
        [lax.dynamic_index_in_dim(mask_all, e, 1, keepdims=False) for e in mine_ids], axis=1
    )
    place = jnp.arange(rows)
    before = (place[:, None] <= place[None, :]).astype(BF)
    order = jnp.einsum("rdt,tu->rdu", has.astype(BF), before, preferred_element_type=F32)
    rank = jnp.where(has, order.astype(jnp.int32) - 1, -1)
    rank_t = rank.transpose(0, 2, 1)
    mask_all = mask_all.astype(F32)

    def over_col(v):
        step = 1
        while step < col_count:
            v = v + swap(v, step, col_count)
            step *= 2
        return v

    load = over_col(jnp.sum(mask_all, axis=(0, 2))) / (tokens * TOPK)

    inv_freq = THETA ** (-2.0 * jnp.arange(HEAD // 2, dtype=F32) / HEAD)
    coses, sines = [], []
    for m in members:
        spots = lax.dynamic_index_in_dim(positions, m, 0, keepdims=False).astype(F32)
        angles = spots[:, None] * inv_freq[None, :]
        cos, sin = jnp.cos(angles), jnp.sin(angles)
        coses.append(jnp.concatenate([cos, cos], axis=1))
        sines.append(jnp.concatenate([-sin, sin], axis=1))

    beside, rank, rank_t, mask_all, coses, sines, load = lax.optimization_barrier(
        (beside, rank, rank_t, mask_all, coses, sines, load)
    )
    out_all = lax.all_gather(after(w_out, beside), "row", axis=1, tiled=True)
    xs = [x_own] + [v[0] for v in beside]
    if four:
        xs.append(jnp.concatenate(far(*beside, col_count), axis=1)[0])
    qs, kvs, normed, scales, every = [[None] * col_count for _ in range(5)]
    line = others + [0]
    batch = max(1, col_count // 2)
    for first in range(0, col_count, batch):
        ahead = line[first : first + batch]
        for d in ahead:
            qs[d], kvs[d], normed[d], scales[d] = qkv(
                xs[d], gain_one, wide, coses[d], sines[d], gain_q, gain_k, heads
            )
        got = jnp.concatenate([kvs[d] for d in ahead], axis=0)
        if first == 0:
            got, out_all, xs[-1] = lax.optimization_barrier((got, out_all, xs[-1]))
        got = lax.all_gather(got, "row", axis=0)
        for j, d in enumerate(ahead):
            every[d] = (got, j)
    gates, ups = after((w_gate, w_up), xs[-1])
    if four:
        gates_near, ups_near = [[near(v, col_count) for v in halves(w)] for w in (gates, ups)]
    else:
        gates_near, ups_near = [near(gates, col_count)], [near(ups, col_count)]
    mixes, logs = [None] * col_count, [None] * col_count
    hidden = x_own.astype(F32)
    share, sent = None, []
    for at, d in enumerate(line):
        q = qs[d]
        if at > 0:
            q = after(q, share)
        else:
            q, gates_near[0] = lax.optimization_barrier((q, gates_near[0]))
        mixes[d], logs[d] = attend(row_word, q, every[d], kvs[d], blocks)
        mix = mixes[d]
        if at == 0:
            mix, gates_near[-1] = lax.optimization_barrier((mix, gates_near[-1]))
        elif at == 1:
            mix, ups_near[0] = lax.optimization_barrier((mix, ups_near[0]))
        elif d == 0:
            mix, sent[: at - 1] = lax.optimization_barrier((mix, sent[: at - 1]))
        share = jnp.dot(mix, out_all, preferred_element_type=F32)
        if d != 0:
            share = share.astype(BF)
            sent.append(swap(share, d, col_count))
    share, sent = lax.optimization_barrier((share, sent))
    for got in sent:
        hidden = hidden + got.astype(F32)
    hidden = hidden + share
    up_all = lax.all_gather(after(up_own, mixes[line[0]]), "row", axis=0)

    spread = lax.rsqrt(jnp.mean(hidden * hidden, axis=-1, keepdims=True) + EPS)
    second = (hidden * spread * gain_two).astype(BF)
    second_all = lax.all_gather(second, "row", axis=0)

    downs_near = near(after(w_down, share), col_count)
    gate_all = [[w_gate]] + [list(v) for v in zip(*gates_near)]
    up_w_all = [[w_up]] + [list(v) for v in zip(*ups_near)]
    down_all = [[w_down]] + [[w] for w in downs_near]
    if four:
        rank, ups_near, down_all = lax.optimization_barrier((rank, ups_near, down_all))
        up_w_all = [[w_up]] + [list(v) for v in zip(*ups_near)]
        gates_near, _ = lax.optimization_barrier((gates_near, ups_near))
        far_of = lambda one, two: [swap(one[0], 2, col_count), swap(two[1], 1, col_count)]
        gate_all.append(far_of(*zip(*gates_near)))

    expert_up = [v.reshape(row_count * cap, width) for v in dispatch(rank, up_all, cap)]
    router_t = router_all.T
    second_all, expert_up, gate_all = lax.optimization_barrier((second_all, expert_up, gate_all))
    gate_pairs, *expert_in = route_dispatch(
        mine_ids, rank, second_all, mask_all, router_t, cap
    )
    expert_in = [v.reshape(row_count * cap, width) for v in expert_in]
    gate_pairs = gate_pairs.reshape(col_count, row_count * cap, 1)
    if four:
        up_w_all.append(far_of(*zip(*ups_near)))
        expert_in[0], up_w_all = lax.optimization_barrier((expert_in[0], up_w_all))
        down_far = far_of(*[halves(v[0]) for v in down_all[1:3]])
    kv_all = lax.all_gather(after(key_value_weight, expert_in[0]), "row", axis=0, tiled=True)
    dbs, ms, duws, dgs = [[None] * col_count for _ in range(4)]
    grad_gu, grad_dn = [None] * col_count, [None] * col_count

    def gate_up_grad(d):
        grad_gu[d] = dot_tn(expert_in[d], duws[d]).astype(F32 if d == 0 else BF)

    def down_grad(d):
        grad_dn[d] = dot_tn(ms[d], expert_up[d]).astype(F32 if d == 0 else BF)

    far_sent = []
    order = [0, 3, 1, 2] if four else list(slots)
    for at, d in enumerate(order):
        if at > 0:
            held = [g for g in grad_gu + grad_dn if g is not None]
            expert_in[d] = after(expert_in[d], dgs[order[at - 1]], held)
        if four and at == 1:
            expert_in[d], down_far = lax.optimization_barrier((expert_in[d], down_far))
            down_all.append(down_far)
        weights = [gate_all[d], up_w_all[d], down_all[d]]
        dbs[d], ms[d], duws[d], dgs[d] = expert(
            d, expert_in[d], expert_up[d], gate_pairs[d], weights
        )
        if four and at == 1:
            gate_up_grad(d)
            down_grad(d)
            far_sent = [deliver_far(grad_gu[d], col_count), deliver_far(grad_dn[d], col_count)]
    if four:
        dbs[0], far_sent[0] = lax.optimization_barrier((dbs[0], far_sent[0]))
    dbs[0], kv_all = lax.optimization_barrier((dbs[0], kv_all))
    db_part, score_grads = combine(rank_t, dbs, dgs)
    db_sum = lax.psum_scatter(db_part, "row", scatter_dimension=0)
    duws, ms, _ = lax.optimization_barrier((duws, ms, db_part))
    remaining = (1, 2) if four else range(1, col_count)
    for d in remaining:
        gate_up_grad(d)
    exchange = lambda sends: [swap(v, d, col_count) for d, v in enumerate(sends, 1)]
    gu_sends = grad_gu[1:]
    if four:
        gu_two, gu_one = far_sent[0]
        gu_sends = [join(grad_gu[1], gu_one, False), join(grad_gu[2], gu_two, True)]
    if four:
        gu_sends, far_sent[1] = lax.optimization_barrier((gu_sends, far_sent[1]))
    gu_got = exchange(gu_sends)
    ms, gu_sends = lax.optimization_barrier((ms, gu_sends))
    for d in remaining:
        down_grad(d)
    dn_sends = grad_dn[1:]
    if four:
        dn_two, dn_one = far_sent[1]
        dn_sends = [join(grad_dn[1], dn_one, False), join(grad_dn[2], dn_two, True)]
    gate_up_grad(0)
    down_grad(0)
    ys = [dot_nn(m, whole(w)[0]).astype(BF) for m, w in zip(ms, down_all)]
    (y_part,) = combine(rank_t, ys)

    score_grads = lax.all_to_all(score_grads, "row", split_axis=0, concat_axis=0, tiled=True)
    mask_own = jnp.any(routes[0].T[:, None, :] == expert_ids[None, :, None], axis=0)
    logits = lax.dot_general(
        router_all, second, (((0,), (1,)), ((), ())), preferred_element_type=F32
    )
    probs = jax.nn.softmax(logits, axis=0)
    picked = jnp.where(mask_own, probs, 0.0)
    total = jnp.sum(picked, axis=0, keepdims=True)
    gates = picked / total
    to_member = jnp.stack(members)[:, None] == jnp.arange(col_count)[None, :]
    gate_grad = jnp.sum(
        jnp.where(to_member, score_grads[..., None], 0.0), axis=2
    )
    gate_grad = gate_grad.transpose(0, 2, 1).reshape(experts, rows)
    weighted = jnp.sum(gate_grad * gates, axis=0, keepdims=True)
    prob_grad = (
        jnp.where(mask_own, (gate_grad - weighted) / total, 0.0)
        + AUX_COEF * experts * load[:, None] / tokens
    )
    logit_low = (probs * (prob_grad - jnp.sum(probs * prob_grad, axis=0, keepdims=True))).astype(BF)
    grad_router = lax.dot_general(
        second, logit_low, (((0,), (1,)), ((), ())), preferred_element_type=F32
    )
    router_part = lax.dot_general(
        logit_low, router_all, (((0,), (1,)), ((), ())), preferred_element_type=F32
    )

    kv_weight = jnp.concatenate([w for m in members for w in kv_pick(kv_all, m)], axis=1)
    db_sum, gu_got, y_part, router_part, grad_router, kv_weight, own_grads, dn_sends = (
        lax.optimization_barrier(
            (
                db_sum, gu_got, y_part, router_part, grad_router, kv_weight,
                (grad_gu[0], grad_dn[0]), dn_sends,
            )
        )
    )
    y_sum = lax.psum_scatter(y_part, "row", scatter_dimension=0)
    second_grad = db_sum.astype(F32) + router_part
    hat = hidden * spread
    gain_two_grad = jnp.sum(second_grad * hat, axis=0)
    hidden_grad = up_own.astype(F32) + norm_back(second_grad, hat, spread, gain_two)
    branch = hidden_grad.astype(BF)

    beside = near(branch[None], col_count)
    branches = [branch] + [v[0] for v in beside]
    grad_qs, prompts, pairs, shares, sent, grad_kvs, kv_moved = [], [], [], [], [], [], []
    gain_q_grad, gain_k_grad = 0.0, 0.0

    def back_turn(v, cos, sin):
        moved = v * sin
        half = HEAD // 2
        return v * cos + jnp.concatenate([moved[:, half:], moved[:, :half]], axis=1)

    normed_all = jnp.stack(normed, axis=0)
    over_tokens = lambda a, b: lax.dot_general(
        a, b, (((0, 1), (0, 1)), ((), ())), preferred_element_type=F32
    )
    mixes_all = jnp.stack(mixes, axis=0)
    grad_out = None

    def to_owners(prompt):
        chunk = prompt.shape[2]
        return jnp.concatenate(
            [
                lax.ppermute(prompt, "row", [(rows // chunk * i + a, i) for i in range(blocks)])
                for a in range(rows // chunk)
            ],
            axis=2,
        )

    for d in slots:
        if d == col_count - 1:
            grad_out = jnp.stack(branches, axis=0)
            grad_out = over_tokens(mixes_all, after(grad_out, shares[-1])).astype(BF)
        if d == 1:
            beside, shares[0] = lax.optimization_barrier((beside, shares[0]))
            branches = [branch] + [v[0] for v in beside]
            if four:
                branches.append(jnp.concatenate(far(*beside, col_count), axis=1)[0])
            dn_sends, _ = lax.optimization_barrier((dn_sends, branches[-1]))
            dn_got = exchange(dn_sends)
        elif d > 1:
            branches[d], shares[-1] = lax.optimization_barrier((branches[d], shares[-1]))
        if d == 2 and four:
            branches[2], branches[3] = lax.optimization_barrier((branches[2], branches[3]))
        if d == col_count - 1:
            early_prompt = lax.psum_scatter(
                jnp.stack(prompts[:batch], axis=0), "row", scatter_dimension=2, tiled=True
            )
            branches[d], dn_got, grad_out, y_sum = lax.optimization_barrier(
                (branches[d], dn_got, grad_out, y_sum)
            )
            grad_out = lax.psum_scatter(grad_out, "row", scatter_dimension=1, tiled=True)
        mix_grad = dot_nt(branches[d], out_all).astype(BF)
        grad_q, grad_prompt, pair, gain_part = attend_back(
            row_word, qs[d], every[d], kvs[d], blocks, mix_grad, mixes[d], logs[d], scales[d],
            coses[d], sines[d], gain_q,
        )
        grad_qs.append(grad_q)
        prompts.append(grad_prompt)
        pairs.append(pair)
        gain_q_grad = gain_q_grad + gain_part[0]
        if d == col_count - 1:
            grad_q, prompts[-1], pairs[-1], sent, early_prompt, grad_out = lax.optimization_barrier(
                (grad_q, prompts[-1], pairs[-1], sent, early_prompt, grad_out)
            )
        share = input_share(grad_q, wide, F32 if d == 0 else BF)
        shares.append(share)
        if d == 2:
            sent[0] = swap(after(shares[1], share), 1, col_count)
        if d > 0:
            sent.append(swap(share, d, col_count))
    grad_q = over_tokens(normed_all, after(jnp.stack(grad_qs, axis=0), shares[-1]))
    gain_one_grad = jnp.sum(grad_q * wide[:, : heads * HEAD].astype(F32), axis=1)
    grad_q = grad_q.astype(BF)
    late_prompt = lax.psum_scatter(
        jnp.stack(prompts[batch:], axis=0), "row", scatter_dimension=2, tiled=True
    )
    early_prompt = to_owners(after(early_prompt, shares[-1]))
    early_prompt, grad_q = lax.optimization_barrier((early_prompt, grad_q))
    for first in range(0, col_count, batch):
        prompt = early_prompt
        if first > 0:
            prompt = to_owners(late_prompt)
        for d in range(first, first + batch):
            pair = pairs[d] + prompt[d - first].astype(F32)
            key_dy = back_turn(pair[0], coses[d], sines[d])
            key_hat = back_turn(kvs[d][0].astype(F32), coses[d], sines[d]) / gain_k
            gain_k_grad = gain_k_grad + jnp.sum(key_dy * key_hat, axis=0)
            key_raw = norm_back(key_dy, key_hat, scales[d][:, heads : heads + 1], gain_k)
            grad_kv = jnp.concatenate([key_raw.astype(BF), pair[1].astype(BF)], axis=1)
            grad_kvs.append(grad_kv)
            kv_moved.append(grad_kv if d == 0 else swap(grad_kv, d, col_count))
    grad_q = lax.psum_scatter(grad_q, "row", scatter_dimension=0, tiled=True)

    grad_kv = over_tokens(normed_all, jnp.stack(grad_kvs, axis=0))
    gain_one_grad = gain_one_grad + jnp.sum(
        grad_kv * wide[:, heads * HEAD : cols].astype(F32), axis=1
    )
    gain_one_grad = gain_one_grad / gain_one[0]
    grad_kv = lax.all_to_all(
        grad_kv.astype(BF).reshape(devices, -1, 2 * HEAD),
        ("row", "col"),
        split_axis=0,
        concat_axis=0,
        tiled=True,
    )
    grad_kv = jnp.sum(grad_kv.astype(F32).reshape(row_count, col_count, -1, 2 * HEAD), axis=0)
    grad_kv = grad_kv.reshape(KEY_VALUE_HEADS, sharing, -1, 2, HEAD).sum(axis=1)
    grad_kv = grad_kv.transpose(1, 2, 0, 3).reshape(-1, 2 * kv_cols)
    tail = [grad_router, gain_two_grad, gain_one_grad, gain_q_grad, gain_k_grad]
    tail = [v.reshape(devices, -1) for v in tail]
    tail.append(jnp.broadcast_to(jnp.sum(probs, axis=1)[None], (devices, experts)))
    cuts = [0]
    for v in tail:
        cuts.append(cuts[-1] + v.shape[1])
    tail = lax.all_to_all(
        jnp.concatenate(tail, axis=1), ("row", "col"), split_axis=0, concat_axis=0, tiled=True
    )
    tail = jnp.sum(tail, axis=0)
    grad_router, gain_two_grad, gain_one_grad, gain_q_grad, gain_k_grad, mean_probs = [
        tail[a:b] for a, b in zip(cuts[:-1], cuts[1:])
    ]
    mean_probs = mean_probs / tokens
    aux_loss = experts * jnp.sum(load * mean_probs)
    expert_load = jnp.stack([experts * load, experts * mean_probs])

    kv_share = dot_nt(jnp.concatenate(kv_moved, axis=1), kv_weight)
    input_sum = shares[0] + kv_share
    for got in sent:
        input_sum = input_sum + got.astype(F32)
    x_wide = x_own.astype(F32)
    x_spread = lax.rsqrt(jnp.mean(x_wide * x_wide, axis=-1, keepdims=True) + EPS)
    x_hat = x_wide * x_spread
    input_grad = hidden_grad + norm_back(input_sum, x_hat, x_spread, gain_one)

    own_grads, _ = lax.optimization_barrier((own_grads, kv_share))
    ffe = w_gate.shape[2]
    grad_gate = own_grads[0][:, :ffe] + sum(v[:, :ffe].astype(F32) for v in gu_got)
    grad_up = own_grads[0][:, ffe:] + sum(v[:, ffe:].astype(F32) for v in gu_got)
    grad_down = own_grads[1] + sum(v.astype(F32) for v in dn_got)
    layer_output = (hidden + y_sum.astype(F32)).astype(BF)

    return (
        layer_output[None],
        aux_loss,
        input_grad[None],
        grad_q.astype(F32),
        grad_kv,
        grad_out.astype(F32),
        grad_router.reshape(width // devices, experts),
        gain_one_grad,
        gain_two_grad,
        gain_q_grad,
        gain_k_grad,
        grad_gate[None],
        grad_up[None],
        grad_down[None],
        expert_load,
    )


def solution(mesh):
    in_specs = (
        P("col", "row", None),
        P("col", "row", None),
        P("col", "row", None),
        P(None, "row"),
        P("row", "col"),
        P("row", None),
        P("col", "row"),
        P("row", None),
        P("row"),
        P("row"),
        P("row"),
        P("row"),
        P(("row", "col"), None, None),
        P(("row", "col"), None, None),
        P(("row", "col"), None, None),
    )
    out_specs = (
        P("col", "row", None),
        P(),
        P("col", "row", None),
        P("row", "col"),
        P(("row", "col"), None),
        P("col", "row"),
        P(("row", "col"), None),
        P(("row", "col")),
        P(("row", "col")),
        P(("row", "col")),
        P(("row", "col")),
        P(("row", "col"), None, None),
        P(("row", "col"), None, None),
        P(("row", "col"), None, None),
        P(),
    )
    return jax.shard_map(
        per_device, mesh=mesh, in_specs=in_specs, out_specs=out_specs, check_vma=False
    )
```

```python
from functools import partial
import math

import jax
import jax.numpy as jnp
from jax import lax
from jax.experimental import pallas as pl
from jax.experimental.pallas import tpu as pltpu
from jax.sharding import PartitionSpec as P

QUERY_HEADS = 32
KEY_VALUE_HEADS = 4
HEAD = 128
TOPK = 8
CONT = 256
PROMPT_TOKENS = 2048

EPS = 1e-06
THETA = 1000000.0
AUX_COEF = 0.001
LN2 = math.log(2.0)
SCALE2 = 1.0 / (math.sqrt(HEAD) * LN2)
VMEM = 56 * 1024 * 1024

BF = jnp.bfloat16
F32 = jnp.float32


def dot_nn(a, b):
    return lax.dot_general(a, b, (((1,), (0,)), ((), ())), preferred_element_type=F32)


def dot_nt(a, b):
    return lax.dot_general(a, b, (((1,), (1,)), ((), ())), preferred_element_type=F32)


def dot_tn(a, b):
    return lax.dot_general(a, b, (((0,), (0,)), ((), ())), preferred_element_type=F32)


def call(body, name, grid, in_specs, out_specs, out_shape, scratch=(), flops=0, moved=0, prefetch=0):
    return pl.pallas_call(
        body,
        name=name,
        grid_spec=pltpu.PrefetchScalarGridSpec(
            num_scalar_prefetch=prefetch,
            grid=grid,
            in_specs=in_specs,
            out_specs=out_specs,
            scratch_shapes=list(scratch),
        ),
        out_shape=out_shape,
        cost_estimate=pl.CostEstimate(
            flops=int(flops), bytes_accessed=int(moved), transcendentals=0
        ),
        compiler_params=pltpu.CompilerParams(
            dimension_semantics=("arbitrary",) * len(grid), vmem_limit_bytes=VMEM
        ),
    )


def struct(shape, dtype):
    return jax.ShapeDtypeStruct(shape, dtype)


def turn(v, cos, sin):
    return v * cos + pltpu.roll(v, HEAD // 2, 1) * sin


def turn_back(v, cos, sin):
    return v * cos + pltpu.roll(v * sin, HEAD // 2, 1)


def qkv_body(heads, x_ref, gain_ref, w_ref, cos_ref, sin_ref, qg_ref, kg_ref, q_ref, kv_ref, a_ref, r_ref):
    x = x_ref[...].astype(F32)
    normed = x * lax.rsqrt(jnp.mean(x * x, axis=-1, keepdims=True) + EPS) * gain_ref[...]
    low = normed.astype(BF)
    a_ref[...] = low
    raw = dot_nn(low, w_ref[...])
    cos = cos_ref[...]
    sin = sin_ref[...]
    lane = lax.broadcasted_iota(jnp.int32, (x.shape[0], HEAD), 1)
    scales = jnp.zeros((x.shape[0], HEAD), F32)
    for h in range(heads + 1):
        v = raw[:, h * HEAD : (h + 1) * HEAD]
        r = lax.rsqrt(jnp.mean(v * v, axis=-1, keepdims=True) + EPS)
        scales = jnp.where(lane == h, r, scales)
        if h < heads:
            q_ref[h] = (turn(v * r * qg_ref[...], cos, sin) * SCALE2).astype(BF)
        else:
            kv_ref[0] = turn(v * r * kg_ref[...], cos, sin).astype(BF)
    kv_ref[1] = raw[:, (heads + 1) * HEAD :].astype(BF)
    r_ref[...] = scales


def qkv(x, gain, w, cos, sin, qg, kg, heads):
    rows, width = x.shape
    cols = (heads + 2) * HEAD
    tile = 256
    whole = lambda i: (0, 0)
    row = lambda i: (i, 0)
    return call(
        partial(qkv_body, heads),
        "qkv",
        (rows // tile,),
        [
            pl.BlockSpec((tile, width), row),
            pl.BlockSpec((1, width), whole),
            pl.BlockSpec((width, cols), whole),
            pl.BlockSpec((tile, HEAD), row),
            pl.BlockSpec((tile, HEAD), row),
            pl.BlockSpec((1, HEAD), whole),
            pl.BlockSpec((1, HEAD), whole),
        ],
        [
            pl.BlockSpec((heads, tile, HEAD), lambda i: (0, i, 0)),
            pl.BlockSpec((2, tile, HEAD), lambda i: (0, i, 0)),
            pl.BlockSpec((tile, width), row),
            pl.BlockSpec((tile, HEAD), row),
        ],
        [
            struct((heads, rows, HEAD), BF),
            struct((2, rows, HEAD), BF),
            struct((rows, width), BF),
            struct((rows, HEAD), F32),
        ],
        flops=2 * rows * width * cols,
        moved=2 * (2 * rows * width + width * cols + rows * cols),
    )(x, gain, w, cos, sin, qg, kg)


def causal(count):
    q_at = lax.broadcasted_iota(jnp.int32, (count, CONT, CONT), 1)
    k_at = lax.broadcasted_iota(jnp.int32, (count, CONT, CONT), 2)
    return (k_at <= q_at).reshape(count * CONT, CONT)


def attend_body(heads, per, blocks, rows, row_ref, q_ref, kp_ref, vp_ref, kv_ref, o_ref, l_ref, vp_one, vl_one, acc):
    at = pl.program_id(0)
    part = pl.program_id(1)
    row = row_ref[0]

    @pl.when((at == 0) & (part == 0))
    def _():
        for j in range(blocks):
            vp_one[j * rows : (j + 1) * rows, :HEAD] = vp_ref[j, 0]
        vp_one[:, HEAD:] = jnp.ones((blocks * rows, HEAD), BF)
        vl_one[:, :HEAD] = kv_ref[1]
        vl_one[:, HEAD:] = jnp.ones((rows, HEAD), BF)

    q = q_ref[...].reshape(per * CONT, HEAD)
    here = pl.ds(pl.multiple_of(at * CONT, CONT), CONT)
    weights = jnp.where(causal(per), jnp.exp2(dot_nt(q, kv_ref[0, here, :])), 0.0).astype(BF)
    acc[...] = dot_nn(weights, vl_one[here, :])

    @pl.when(row < blocks)
    def _():
        for j in range(rows // CONT - 1):

            @pl.when(j < at)
            def _():
                piece = slice(j * CONT, (j + 1) * CONT)
                weights = jnp.exp2(dot_nt(q, kv_ref[0, piece, :])).astype(BF)
                acc[...] += dot_nn(weights, vl_one[piece, :])

        @pl.loop(0, row)
        def _(j):
            weights = jnp.exp2(dot_nt(q, kp_ref[j, 0])).astype(BF)
            acc[...] += dot_nn(weights, vp_one[pl.ds(pl.multiple_of(j * rows, rows), rows), :])

    @pl.when(row >= blocks)
    def _():
        keys = kp_ref[...].reshape(blocks * rows, HEAD)
        weights = jnp.exp2(dot_nt(q, keys)).astype(BF)
        acc[...] += dot_nn(weights, vp_one[...])

    total = acc[:, HEAD:]
    out = (acc[:, :HEAD] / total).astype(BF)
    logs = jnp.log2(total)
    lane = lax.broadcasted_iota(jnp.int32, (CONT, HEAD), 1)

    @pl.when(part == 0)
    def _():
        l_ref[...] = jnp.zeros((CONT, HEAD), F32)

    held = l_ref[...]
    for p in range(per):
        o_ref[:, p * HEAD : (p + 1) * HEAD] = out[p * CONT : (p + 1) * CONT]
        held = jnp.where(lane == part * per + p, logs[p * CONT : (p + 1) * CONT], held)
    l_ref[...] = held


def attend(row, q, every, kv, blocks):
    heads, rows, _ = q.shape
    per = min(4, heads)
    every, place = every
    keys = blocks * rows
    return call(
        partial(attend_body, heads, per, blocks, rows),
        "attend",
        (rows // CONT, heads // per),
        [
            pl.BlockSpec((per, CONT, HEAD), lambda i, h, s: (h, i, 0)),
            pl.BlockSpec((blocks, 1, rows, HEAD), lambda i, h, s: (0, 2 * place, 0, 0)),
            pl.BlockSpec((blocks, 1, rows, HEAD), lambda i, h, s: (0, 2 * place + 1, 0, 0)),
            pl.BlockSpec((2, rows, HEAD), lambda i, h, s: (0, 0, 0)),
        ],
        [
            pl.BlockSpec((CONT, per * HEAD), lambda i, h, s: (i, h)),
            pl.BlockSpec((CONT, HEAD), lambda i, h, s: (i, 0)),
        ],
        [struct((rows, heads * HEAD), BF), struct((rows, HEAD), F32)],
        scratch=[
            pltpu.VMEM((keys, 2 * HEAD), BF),
            pltpu.VMEM((rows, 2 * HEAD), BF),
            pltpu.VMEM((per * CONT, 2 * HEAD), F32),
        ],
        flops=8 * rows * heads * (keys + CONT) * HEAD,
        moved=2 * HEAD * (2 * rows * heads + 2 * keys),
        prefetch=1,
    )(row, q, every, every, kv)


def attend_back_body(
    heads, per, blocks, rows,
    row_ref, q_ref, kp_ref, vp_ref, kv_ref, do_ref, o_ref, l_ref, r_ref, cos_ref, sin_ref, qg_ref,
    dq_ref, dp_ref, dl_ref, g_ref,
    dq, dkp, dvp,
):
    at = pl.program_id(0)
    part = pl.program_id(1)
    row = row_ref[0]

    @pl.when((at == 0) & (part == 0))
    def _():
        dkp[...] = jnp.zeros_like(dkp)
        dvp[...] = jnp.zeros_like(dvp)
        dl_ref[...] = jnp.zeros_like(dl_ref)
        g_ref[...] = jnp.zeros_like(g_ref)

    q = q_ref[...].reshape(per * CONT, HEAD)
    lane = lax.broadcasted_iota(jnp.int32, (CONT, HEAD), 1)
    line = lax.broadcasted_iota(jnp.int32, (HEAD, CONT), 0)
    logs_t = l_ref[...].T
    do_parts, logs, centers, scales = [], [], [], []
    for p in range(per):
        do_part = do_ref[:, p * HEAD : (p + 1) * HEAD]
        do_parts.append(do_part)
        both = do_part.astype(F32) * o_ref[:, p * HEAD : (p + 1) * HEAD].astype(F32)
        centers.append(jnp.sum(both.T, axis=0, keepdims=True))
        head = part * per + p
        logs.append(jnp.sum(jnp.where(line == head, logs_t, 0.0), axis=0, keepdims=True))
        scales.append(jnp.sum(jnp.where(lane == head, r_ref[...], 0.0), axis=-1, keepdims=True))
    do = jnp.concatenate(do_parts, axis=0)
    center = jnp.concatenate(centers, axis=1)
    log = jnp.concatenate(logs, axis=1)

    def block(k, v, mask):
        probs = jnp.exp2(dot_nt(k, q) - log)
        if mask is not None:
            probs = jnp.where(mask, probs, 0.0)
        ds = (probs * (dot_nt(v, do) - center)).astype(BF)
        return dot_tn(ds, k), dot_nn(ds, q), dot_nn(probs.astype(BF), do)

    k_at = lax.broadcasted_iota(jnp.int32, (CONT, CONT), 0)
    q_at = lax.broadcasted_iota(jnp.int32, (CONT, CONT), 1)
    seen = jnp.concatenate([k_at <= q_at] * per, axis=1)
    here = pl.ds(pl.multiple_of(at * CONT, CONT), CONT)
    a, b, c = block(kv_ref[0, here, :], kv_ref[1, here, :], seen)
    dq[...] = a
    dl_ref[0, here, :] += b
    dl_ref[1, here, :] += c

    @pl.when(row < blocks)
    def _():
        for j in range(rows // CONT - 1):

            @pl.when(j < at)
            def _():
                piece = slice(j * CONT, (j + 1) * CONT)
                a, b, c = block(kv_ref[0, piece, :], kv_ref[1, piece, :], None)
                dq[...] += a
                dl_ref[0, piece, :] += b
                dl_ref[1, piece, :] += c

    @pl.loop(0, jnp.minimum(row, blocks))
    def _(j):
        a, b, c = block(kp_ref[j, 0], vp_ref[j, 0], None)
        piece = pl.ds(pl.multiple_of(j * rows, rows), rows)
        dq[...] += a
        dkp[piece, :] += b
        dvp[piece, :] += c

    cos = cos_ref[...]
    sin = sin_ref[...]
    gain = qg_ref[...]
    tally = jnp.zeros((1, HEAD), F32)
    for p in range(per):
        dy = turn_back(dq[p * CONT : (p + 1) * CONT, :] * (SCALE2 * LN2), cos, sin)
        hat = turn_back(q[p * CONT : (p + 1) * CONT].astype(F32), cos, sin) * (1.0 / SCALE2) / gain
        tally += jnp.sum(dy * hat, axis=0, keepdims=True)
        dyg = dy * gain
        raw = scales[p] * (dyg - hat * jnp.mean(dyg * hat, axis=-1, keepdims=True))
        dq_ref[:, p * HEAD : (p + 1) * HEAD] = raw.astype(BF)
    g_ref[0:1, :] += tally

    @pl.when((at == rows // CONT - 1) & (part == heads // per - 1))
    def _():
        dp_ref[0] = (dkp[...] * LN2).astype(BF)
        dp_ref[1] = dvp[...].astype(BF)
        dl_ref[0] = dl_ref[0] * LN2


def attend_back(row, q, every, kv, blocks, do, o, logs, scales, cos, sin, qg):
    heads, rows, _ = q.shape
    per = min(8, heads)
    every, place = every
    keys = blocks * rows
    tile = lambda i, h, s: (i, 0)
    head = lambda i, h, s: (i, h)
    return call(
        partial(attend_back_body, heads, per, blocks, rows),
        "attend_back",
        (rows // CONT, heads // per),
        [
            pl.BlockSpec((per, CONT, HEAD), lambda i, h, s: (h, i, 0)),
            pl.BlockSpec((blocks, 1, rows, HEAD), lambda i, h, s: (0, 2 * place, 0, 0)),
            pl.BlockSpec((blocks, 1, rows, HEAD), lambda i, h, s: (0, 2 * place + 1, 0, 0)),
            pl.BlockSpec((2, rows, HEAD), lambda i, h, s: (0, 0, 0)),
            pl.BlockSpec((CONT, per * HEAD), head),
            pl.BlockSpec((CONT, per * HEAD), head),
            pl.BlockSpec((CONT, HEAD), tile),
            pl.BlockSpec((CONT, HEAD), tile),
            pl.BlockSpec((CONT, HEAD), tile),
            pl.BlockSpec((CONT, HEAD), tile),
            pl.BlockSpec((1, HEAD), lambda i, h, s: (0, 0)),
        ],
        [
            pl.BlockSpec((CONT, per * HEAD), head),
            pl.BlockSpec((2, keys, HEAD), lambda i, h, s: (0, 0, 0)),
            pl.BlockSpec((2, rows, HEAD), lambda i, h, s: (0, 0, 0)),
            pl.BlockSpec((8, HEAD), lambda i, h, s: (0, 0)),
        ],
        [
            struct((rows, heads * HEAD), BF),
            struct((2, keys, HEAD), BF),
            struct((2, rows, HEAD), F32),
            struct((8, HEAD), F32),
        ],
        scratch=[
            pltpu.VMEM((per * CONT, HEAD), F32),
            pltpu.VMEM((keys, HEAD), F32),
            pltpu.VMEM((keys, HEAD), F32),
        ],
        flops=20 * rows * heads * (keys + CONT) * HEAD,
        moved=2 * HEAD * (4 * rows * heads + 4 * keys),
        prefetch=1,
    )(row, q, every, every, kv, do, o, logs, scales, cos, sin, qg)


def dispatch_body(count, cap, rank_ref, rows_ref, *out_refs):
    tokens = rows_ref.shape[1]
    slot = lax.broadcasted_iota(jnp.int32, (cap, tokens), 0)
    for d in range(count):
        hot = (rank_ref[0, d : d + 1, :] == slot).astype(F32).astype(BF)
        out_refs[d][0] = dot_nn(hot, rows_ref[0]).astype(BF)


def dispatch(rank, rows, cap):
    sources, count, tokens = rank.shape
    width = rows.shape[2]
    return call(
        partial(dispatch_body, count, cap),
        "dispatch",
        (sources,),
        [
            pl.BlockSpec((1, count, tokens), lambda s: (s, 0, 0)),
            pl.BlockSpec((1, tokens, width), lambda s: (s, 0, 0)),
        ],
        [pl.BlockSpec((1, cap, width), lambda s: (s, 0, 0))] * count,
        [struct((sources, cap, width), BF)] * count,
        flops=2 * sources * count * cap * tokens * width,
        moved=2 * sources * width * (tokens + count * cap),
    )(rank, rows)


def route_body(count, cap, ids_ref, rank_ref, rows_ref, mask_ref, router_ref, gate_ref, *out_refs):
    tokens = rows_ref.shape[1]
    rows = rows_ref[0]
    logits = dot_nt(router_ref[...], rows)
    weights = jnp.exp(logits - jnp.max(logits, axis=0, keepdims=True))
    probs = weights / jnp.sum(weights, axis=0, keepdims=True)
    picked = probs * mask_ref[0]
    gates = picked / jnp.sum(picked, axis=0, keepdims=True)
    expert_at = lax.broadcasted_iota(jnp.int32, gates.shape, 0)
    slot = lax.broadcasted_iota(jnp.int32, (cap, tokens), 0)
    for d in range(count):
        here = rank_ref[0, d : d + 1, :] == slot
        out_refs[d][0] = dot_nn(here.astype(F32).astype(BF), rows).astype(BF)
        mine = jnp.sum(jnp.where(expert_at == ids_ref[d], gates, 0.0), axis=0, keepdims=True)
        gate_ref[d, 0] = jnp.sum(jnp.where(here, mine, 0.0), axis=1, keepdims=True)


def route_dispatch(ids, rank, rows, mask, router, cap):
    sources, count, tokens = rank.shape
    width = rows.shape[2]
    experts = router.shape[0]
    return call(
        partial(route_body, count, cap),
        "route_dispatch",
        (sources,),
        [
            pl.BlockSpec((1, count, tokens), lambda s, i: (s, 0, 0)),
            pl.BlockSpec((1, tokens, width), lambda s, i: (s, 0, 0)),
            pl.BlockSpec((1, experts, tokens), lambda s, i: (s, 0, 0)),
            pl.BlockSpec((experts, width), lambda s, i: (0, 0)),
        ],
        [
            pl.BlockSpec((count, 1, cap, 1), lambda s, i: (0, s, 0, 0)),
        ]
        + [pl.BlockSpec((1, cap, width), lambda s, i: (s, 0, 0))] * count,
        [struct((count, sources, cap, 1), F32)]
        + [struct((sources, cap, width), BF)] * count,
        flops=2 * sources * count * cap * tokens * width,
        moved=2 * sources * width * (tokens + count * cap),
        prefetch=1,
    )(ids, rank, rows, mask, router)


def share_body(g_ref, w_ref, out_ref):
    out_ref[...] = dot_nt(g_ref[...], w_ref[...]).astype(out_ref.dtype)


def input_share(grads, w, dtype):
    rows, cols = grads.shape
    width = w.shape[0]
    tile = 256
    return call(
        share_body,
        "input_share",
        (rows // tile,),
        [
            pl.BlockSpec((tile, cols), lambda i: (i, 0)),
            pl.BlockSpec((width, cols), lambda i: (0, 0)),
        ],
        pl.BlockSpec((tile, width), lambda i: (i, 0)),
        struct((rows, width), dtype),
        flops=2 * rows * width * cols,
        moved=2 * (rows * width + width * cols + rows * cols),
    )(grads, w)


def combine_body(count, cap, scored, rank_ref, *refs):
    tokens = rank_ref.shape[1]
    slot = lax.broadcasted_iota(jnp.int32, (tokens, cap), 1)
    hots = [(rank_ref[0, :, d : d + 1] == slot).astype(F32).astype(BF) for d in range(count)]

    def gathered(parts):
        if cap % HEAD:
            return sum(dot_nn(hot, part[0]) for hot, part in zip(hots, parts))
        return dot_nn(
            jnp.concatenate(hots, axis=1), jnp.concatenate([p[0] for p in parts], axis=0)
        )

    refs[count * (2 if scored else 1)][0] = gathered(refs[:count]).astype(BF)
    if scored:
        scores = gathered(refs[count : 2 * count])
        lane = lax.broadcasted_iota(jnp.int32, scores.shape, 1)
        for d in range(count):
            mine = jnp.where(lane // 4 == d, scores, 0.0)
            refs[-1][0, :, d : d + 1] = jnp.sum(mine, axis=-1, keepdims=True)


def combine(rank_t, parts, scores=()):
    sources, tokens, count = rank_t.shape
    cap = parts[0].shape[0] // sources
    width = parts[0].shape[1]
    at = lambda s: (s, 0, 0)
    cut = lambda v: v.reshape(sources, cap, v.shape[1])
    out_specs = [pl.BlockSpec((1, tokens, width), at)]
    out_shape = [struct((sources, tokens, width), BF)]
    if scores:
        out_specs.append(pl.BlockSpec((1, tokens, count), at))
        out_shape.append(struct((sources, tokens, count), F32))
    return call(
        partial(combine_body, count, cap, bool(scores)),
        "combine",
        (sources,),
        [pl.BlockSpec((1, tokens, count), at)]
        + [pl.BlockSpec((1, cap, width), at)] * count
        + [pl.BlockSpec((1, cap, HEAD), at)] * len(scores),
        out_specs,
        out_shape,
    )(rank_t, *[cut(p) for p in parts], *[cut(p) for p in scores])


def expert_body(
    slot, x_ref, up_ref, gate_ref, wga_ref, wgb_ref, wua_ref, wub_ref, wda_ref, wdb_ref,
    db_ref, m_ref, duw_ref, dg_ref,
):
    half = wga_ref.shape[1]
    hidden = wga_ref.shape[2]
    xa, xb = x_ref[:, :half], x_ref[:, half:]
    gate = gate_ref[...]
    u = dot_nn(xa, wga_ref[0]) + dot_nn(xb, wgb_ref[0])
    w = dot_nn(xa, wua_ref[0]) + dot_nn(xb, wub_ref[0])
    sigma = 1.0 / (1.0 + jnp.exp(-u))
    silu = u * sigma
    inner = silu * w
    low = inner.astype(BF)
    m_ref[...] = (inner * gate).astype(BF)
    up = up_ref[...]
    back = jnp.concatenate([dot_nt(up, wda_ref[0]), dot_nt(up, wdb_ref[0])], axis=1)
    score = jnp.sum(low.astype(F32) * back, axis=-1, keepdims=True)
    lane = lax.broadcasted_iota(jnp.int32, dg_ref.shape, 1)
    high = score.astype(BF)
    rest = score - high.astype(F32)
    middle = rest.astype(BF)
    last = (rest - middle.astype(F32)).astype(BF)
    pieces = jnp.where(lane == 4 * slot, high.astype(F32), 0.0)
    pieces = jnp.where(lane == 4 * slot + 1, middle.astype(F32), pieces)
    dg_ref[...] = jnp.where(lane == 4 * slot + 2, last.astype(F32), pieces).astype(BF)
    back = back * gate
    du = (back * w * sigma * (1.0 + u * (1.0 - sigma))).astype(BF)
    dw = (back * silu).astype(BF)
    duw_ref[:, :hidden] = du
    duw_ref[:, hidden:] = dw
    db_ref[:, :half] = (dot_nt(du, wga_ref[0]) + dot_nt(dw, wua_ref[0])).astype(BF)
    db_ref[:, half:] = (dot_nt(du, wgb_ref[0]) + dot_nt(dw, wub_ref[0])).astype(BF)


def expert(slot, x, up, gate, weights):
    rows, width = x.shape
    hidden = weights[0][0].shape[2]
    tile = min(256, rows)
    at = lambda i: (i, 0)
    specs, arrays = [], []
    for parts in weights:
        shape = (1, parts[0].shape[1] * len(parts) // 2, parts[0].shape[2])
        for j in range(2):
            place = j if len(parts) == 1 else 0
            specs.append(pl.BlockSpec(shape, lambda i, place=place: (0, place, 0)))
            arrays.append(parts[0] if len(parts) == 1 else parts[j])
    return call(
        partial(expert_body, slot),
        "expert",
        (rows // tile,),
        [
            pl.BlockSpec((tile, width), at),
            pl.BlockSpec((tile, width), at),
            pl.BlockSpec((tile, 1), at),
        ]
        + specs,
        [
            pl.BlockSpec((tile, width), at),
            pl.BlockSpec((tile, hidden), at),
            pl.BlockSpec((tile, 2 * hidden), at),
            pl.BlockSpec((tile, HEAD), at),
        ],
        [
            struct((rows, width), BF),
            struct((rows, hidden), BF),
            struct((rows, 2 * hidden), BF),
            struct((rows, HEAD), BF),
        ],
        flops=10 * rows * width * hidden,
        moved=2 * (3 * rows * width + 3 * rows * hidden + 3 * width * hidden),
    )(x, up, gate, *arrays)


def swap(v, step, count):
    return lax.ppermute(v, "col", [(i, i ^ step) for i in range(count)])


def near(v, count):
    return [swap(v, d, count) for d in ((1, 2) if count == 4 else range(1, count))]


def far(one, two, count):
    half = one.shape[1] // 2
    return [swap(one[:, :half], 2, count), swap(two[:, half:], 1, count)]


def halves(v):
    return v[:, : v.shape[1] // 2], v[:, v.shape[1] // 2 :]


def whole(parts):
    return parts[0] if len(parts) == 1 else jnp.concatenate(parts, axis=1)


def deliver_far(part, count):
    half = part.shape[0] // 2
    return swap(part[:half], 1, count), swap(part[half:], 2, count)


def join(part, got, first):
    half = part.shape[0] // 2
    wide = jnp.pad(got.astype(F32), ((0, half) if first else (half, 0), (0, 0)))
    return (part.astype(F32) + wide).astype(BF)


def after(value, *earlier):
    return lax.optimization_barrier((value,) + earlier)[0]


def norm_back(grad, hat, spread, gain):
    scaled = grad * gain
    return spread * (scaled - hat * jnp.mean(scaled * hat, axis=-1, keepdims=True))


def per_device(
    layer_input, out_grad, routes, positions, w_q, key_value_weight, w_out, router,
    ln_attn, ln_moe, q_gain, k_gain, w_gate, w_up, w_down,
):
    rows, width = layer_input.shape[1:]
    row_count, col_count = lax.axis_size("row"), lax.axis_size("col")
    row_at, col_at = lax.axis_index("row"), lax.axis_index("col")
    devices = row_count * col_count
    experts = w_gate.shape[0] * devices
    assert w_gate.shape[0] == 1
    cap = rows * TOPK // experts
    tokens = rows * devices
    heads = w_q.shape[1] // HEAD
    sharing = QUERY_HEADS // KEY_VALUE_HEADS // heads
    blocks = PROMPT_TOKENS // rows
    slots = range(col_count)
    others = list(slots[1:])
    members = [col_at ^ d for d in slots]
    row_word = row_at.astype(jnp.int32).reshape(1)

    x_own = layer_input[0]
    up_own = out_grad[0]

    kv_cols = KEY_VALUE_HEADS * HEAD

    def kv_pick(weight, member):
        head = member // sharing
        return [
            lax.dynamic_slice_in_dim(weight, head * HEAD, HEAD, 1),
            lax.dynamic_slice_in_dim(weight, kv_cols + head * HEAD, HEAD, 1),
        ]

    cols = (heads + 2) * HEAD
    piece, head_piece = ln_attn.shape[0], q_gain.shape[0]
    rest = [jnp.pad(g, (0, piece - head_piece))[:, None] for g in (q_gain, k_gain)]
    rest = [router, ln_attn[:, None], ln_moe[:, None]] + rest
    wide = jnp.concatenate([w_q] + kv_pick(key_value_weight, col_at) + rest, axis=1)
    wide = jnp.pad(wide, ((0, 0), (0, -wide.shape[1] % HEAD)))
    wide = lax.all_gather(wide, "row", axis=0, tiled=True)
    extra = wide[:, cols:]
    router_all = extra[:, :experts]
    gain_one = extra[:, experts].astype(F32)[None]
    gain_two = extra[:, experts + 1].astype(F32)[None]
    head_gains = extra.reshape(row_count, piece, -1)[:, :head_piece].astype(F32)
    gain_q = head_gains[:, :, experts + 2].reshape(1, HEAD)
    gain_k = head_gains[:, :, experts + 3].reshape(1, HEAD)

    four = col_count == 4
    beside = near(layer_input, col_count)

    routes_all = lax.all_gather(routes[0], "row", axis=0)
    expert_ids = jnp.arange(experts, dtype=jnp.int32)
    flat_routes = routes_all.transpose(0, 2, 1)
    mask_all = jnp.any(flat_routes[:, :, None, :] == expert_ids[None, None, :, None], axis=1)
    mine_ids = jnp.stack([row_at * col_count + m for m in members]).astype(jnp.int32)
    has = jnp.stack(
        [lax.dynamic_index_in_dim(mask_all, e, 1, keepdims=False) for e in mine_ids], axis=1
    )
    place = jnp.arange(rows)
    before = (place[:, None] <= place[None, :]).astype(BF)
    order = jnp.einsum("rdt,tu->rdu", has.astype(BF), before, preferred_element_type=F32)
    rank = jnp.where(has, order.astype(jnp.int32) - 1, -1)
    rank_t = rank.transpose(0, 2, 1)
    mask_all = mask_all.astype(F32)

    def over_col(v):
        step = 1
        while step < col_count:
            v = v + swap(v, step, col_count)
            step *= 2
        return v

    load = over_col(jnp.sum(mask_all, axis=(0, 2))) / (tokens * TOPK)

    inv_freq = THETA ** (-2.0 * jnp.arange(HEAD // 2, dtype=F32) / HEAD)
    coses, sines = [], []
    for m in members:
        spots = lax.dynamic_index_in_dim(positions, m, 0, keepdims=False).astype(F32)
        angles = spots[:, None] * inv_freq[None, :]
        cos, sin = jnp.cos(angles), jnp.sin(angles)
        coses.append(jnp.concatenate([cos, cos], axis=1))
        sines.append(jnp.concatenate([-sin, sin], axis=1))

    beside, rank, rank_t, mask_all, coses, sines, load = lax.optimization_barrier(
        (beside, rank, rank_t, mask_all, coses, sines, load)
    )
    out_all = lax.all_gather(after(w_out, beside), "row", axis=1, tiled=True)
    xs = [x_own] + [v[0] for v in beside]
    if four:
        xs.append(jnp.concatenate(far(*beside, col_count), axis=1)[0])
    qs, kvs, normed, scales, every = [[None] * col_count for _ in range(5)]
    line = others + [0]
    batch = max(1, col_count // 2)
    for first in range(0, col_count, batch):
        ahead = line[first : first + batch]
        for d in ahead:
            qs[d], kvs[d], normed[d], scales[d] = qkv(
                xs[d], gain_one, wide, coses[d], sines[d], gain_q, gain_k, heads
            )
        got = jnp.concatenate([kvs[d] for d in ahead], axis=0)
        if first == 0:
            got, out_all, xs[-1] = lax.optimization_barrier((got, out_all, xs[-1]))
        got = lax.all_gather(got, "row", axis=0)
        for j, d in enumerate(ahead):
            every[d] = (got, j)
    gates, ups = after((w_gate, w_up), xs[-1])
    if four:
        gates_near, ups_near = [[near(v, col_count) for v in halves(w)] for w in (gates, ups)]
    else:
        gates_near, ups_near = [near(gates, col_count)], [near(ups, col_count)]
    mixes, logs = [None] * col_count, [None] * col_count
    hidden = x_own.astype(F32)
    share, sent = None, []
    for at, d in enumerate(line):
        q = qs[d]
        if at > 0:
            q = after(q, share)
        else:
            q, gates_near[0] = lax.optimization_barrier((q, gates_near[0]))
        mixes[d], logs[d] = attend(row_word, q, every[d], kvs[d], blocks)
        mix = mixes[d]
        if at == 0:
            mix, gates_near[-1] = lax.optimization_barrier((mix, gates_near[-1]))
        elif at == 1:
            mix, ups_near[0] = lax.optimization_barrier((mix, ups_near[0]))
        elif d == 0:
            mix, sent[: at - 1] = lax.optimization_barrier((mix, sent[: at - 1]))
        share = jnp.dot(mix, out_all, preferred_element_type=F32)
        if d != 0:
            share = share.astype(BF)
            sent.append(swap(share, d, col_count))
    share, sent = lax.optimization_barrier((share, sent))
    for got in sent:
        hidden = hidden + got.astype(F32)
    hidden = hidden + share
    up_all = lax.all_gather(after(up_own, mixes[line[0]]), "row", axis=0)

    spread = lax.rsqrt(jnp.mean(hidden * hidden, axis=-1, keepdims=True) + EPS)
    second = (hidden * spread * gain_two).astype(BF)
    second_all = lax.all_gather(second, "row", axis=0)

    downs_near = near(after(w_down, share), col_count)
    gate_all = [[w_gate]] + [list(v) for v in zip(*gates_near)]
    up_w_all = [[w_up]] + [list(v) for v in zip(*ups_near)]
    down_all = [[w_down]] + [[w] for w in downs_near]
    if four:
        rank, ups_near, down_all = lax.optimization_barrier((rank, ups_near, down_all))
        up_w_all = [[w_up]] + [list(v) for v in zip(*ups_near)]
        gates_near, _ = lax.optimization_barrier((gates_near, ups_near))
        far_of = lambda one, two: [swap(one[0], 2, col_count), swap(two[1], 1, col_count)]
        gate_all.append(far_of(*zip(*gates_near)))

    expert_up = [v.reshape(row_count * cap, width) for v in dispatch(rank, up_all, cap)]
    router_t = router_all.T
    second_all, expert_up, gate_all = lax.optimization_barrier((second_all, expert_up, gate_all))
    gate_pairs, *expert_in = route_dispatch(
        mine_ids, rank, second_all, mask_all, router_t, cap
    )
    expert_in = [v.reshape(row_count * cap, width) for v in expert_in]
    gate_pairs = gate_pairs.reshape(col_count, row_count * cap, 1)
    if four:
        up_w_all.append(far_of(*zip(*ups_near)))
        expert_in[0], up_w_all = lax.optimization_barrier((expert_in[0], up_w_all))
        down_far = far_of(*[halves(v[0]) for v in down_all[1:3]])
    kv_all = lax.all_gather(after(key_value_weight, expert_in[0]), "row", axis=0, tiled=True)
    dbs, ms, duws, dgs = [[None] * col_count for _ in range(4)]
    grad_gu, grad_dn = [None] * col_count, [None] * col_count

    def gate_up_grad(d):
        grad_gu[d] = dot_tn(expert_in[d], duws[d]).astype(F32 if d == 0 else BF)

    def down_grad(d):
        grad_dn[d] = dot_tn(ms[d], expert_up[d]).astype(F32 if d == 0 else BF)

    far_sent = []
    order = [0, 3, 1, 2] if four else list(slots)
    for at, d in enumerate(order):
        if at > 0:
            held = [g for g in grad_gu + grad_dn if g is not None]
            expert_in[d] = after(expert_in[d], dgs[order[at - 1]], held)
        if four and at == 1:
            expert_in[d], down_far = lax.optimization_barrier((expert_in[d], down_far))
            down_all.append(down_far)
        weights = [gate_all[d], up_w_all[d], down_all[d]]
        dbs[d], ms[d], duws[d], dgs[d] = expert(
            d, expert_in[d], expert_up[d], gate_pairs[d], weights
        )
        if four and at == 1:
            gate_up_grad(d)
            down_grad(d)
            far_sent = [deliver_far(grad_gu[d], col_count), deliver_far(grad_dn[d], col_count)]
    if four:
        dbs[0], far_sent[0] = lax.optimization_barrier((dbs[0], far_sent[0]))
    dbs[0], kv_all = lax.optimization_barrier((dbs[0], kv_all))
    db_part, score_grads = combine(rank_t, dbs, dgs)
    db_sum = lax.psum_scatter(db_part, "row", scatter_dimension=0)
    duws, ms, _ = lax.optimization_barrier((duws, ms, db_part))
    remaining = (1, 2) if four else range(1, col_count)
    for d in remaining:
        gate_up_grad(d)
    exchange = lambda sends: [swap(v, d, col_count) for d, v in enumerate(sends, 1)]
    gu_sends = grad_gu[1:]
    if four:
        gu_two, gu_one = far_sent[0]
        gu_sends = [join(grad_gu[1], gu_one, False), join(grad_gu[2], gu_two, True)]
    if four:
        gu_sends, far_sent[1] = lax.optimization_barrier((gu_sends, far_sent[1]))
    gu_got = exchange(gu_sends)
    ms, gu_sends = lax.optimization_barrier((ms, gu_sends))
    for d in remaining:
        down_grad(d)
    dn_sends = grad_dn[1:]
    if four:
        dn_two, dn_one = far_sent[1]
        dn_sends = [join(grad_dn[1], dn_one, False), join(grad_dn[2], dn_two, True)]
    gate_up_grad(0)
    down_grad(0)
    ys = [dot_nn(m, whole(w)[0]).astype(BF) for m, w in zip(ms, down_all)]
    (y_part,) = combine(rank_t, ys)

    score_grads = lax.all_to_all(score_grads, "row", split_axis=0, concat_axis=0, tiled=True)
    mask_own = jnp.any(routes[0].T[:, None, :] == expert_ids[None, :, None], axis=0)
    logits = lax.dot_general(
        router_all, second, (((0,), (1,)), ((), ())), preferred_element_type=F32
    )
    probs = jax.nn.softmax(logits, axis=0)
    picked = jnp.where(mask_own, probs, 0.0)
    total = jnp.sum(picked, axis=0, keepdims=True)
    gates = picked / total
    to_member = jnp.stack(members)[:, None] == jnp.arange(col_count)[None, :]
    gate_grad = jnp.sum(
        jnp.where(to_member, score_grads[..., None], 0.0), axis=2
    )
    gate_grad = gate_grad.transpose(0, 2, 1).reshape(experts, rows)
    weighted = jnp.sum(gate_grad * gates, axis=0, keepdims=True)
    prob_grad = (
        jnp.where(mask_own, (gate_grad - weighted) / total, 0.0)
        + AUX_COEF * experts * load[:, None] / tokens
    )
    logit_low = (probs * (prob_grad - jnp.sum(probs * prob_grad, axis=0, keepdims=True))).astype(BF)
    grad_router = lax.dot_general(
        second, logit_low, (((0,), (1,)), ((), ())), preferred_element_type=F32
    )
    router_part = lax.dot_general(
        logit_low, router_all, (((0,), (1,)), ((), ())), preferred_element_type=F32
    )

    kv_weight = jnp.concatenate([w for m in members for w in kv_pick(kv_all, m)], axis=1)
    db_sum, gu_got, y_part, router_part, grad_router, kv_weight, own_grads, dn_sends = (
        lax.optimization_barrier(
            (
                db_sum, gu_got, y_part, router_part, grad_router, kv_weight,
                (grad_gu[0], grad_dn[0]), dn_sends,
            )
        )
    )
    y_sum = lax.psum_scatter(y_part, "row", scatter_dimension=0)
    second_grad = db_sum.astype(F32) + router_part
    hat = hidden * spread
    gain_two_grad = jnp.sum(second_grad * hat, axis=0)
    hidden_grad = up_own.astype(F32) + norm_back(second_grad, hat, spread, gain_two)
    branch = hidden_grad.astype(BF)

    beside = near(branch[None], col_count)
    branches = [branch] + [v[0] for v in beside]
    grad_qs, prompts, pairs, shares, sent, grad_kvs, kv_moved = [], [], [], [], [], [], []
    gain_q_grad, gain_k_grad = 0.0, 0.0

    def back_turn(v, cos, sin):
        moved = v * sin
        half = HEAD // 2
        return v * cos + jnp.concatenate([moved[:, half:], moved[:, :half]], axis=1)

    normed_all = jnp.stack(normed, axis=0)
    over_tokens = lambda a, b: lax.dot_general(
        a, b, (((0, 1), (0, 1)), ((), ())), preferred_element_type=F32
    )
    mixes_all = jnp.stack(mixes, axis=0)
    grad_out = None

    def to_owners(prompt):
        chunk = prompt.shape[2]
        return jnp.concatenate(
            [
                lax.ppermute(prompt, "row", [(rows // chunk * i + a, i) for i in range(blocks)])
                for a in range(rows // chunk)
            ],
            axis=2,
        )

    for d in slots:
        if d == col_count - 1:
            grad_out = jnp.stack(branches, axis=0)
            grad_out = over_tokens(mixes_all, after(grad_out, shares[-1])).astype(BF)
        if d == 1:
            beside, shares[0] = lax.optimization_barrier((beside, shares[0]))
            branches = [branch] + [v[0] for v in beside]
            if four:
                branches.append(jnp.concatenate(far(*beside, col_count), axis=1)[0])
            dn_sends, _ = lax.optimization_barrier((dn_sends, branches[-1]))
            dn_got = exchange(dn_sends)
        elif d > 1:
            branches[d], shares[-1] = lax.optimization_barrier((branches[d], shares[-1]))
        if d == 2 and four:
            branches[2], branches[3] = lax.optimization_barrier((branches[2], branches[3]))
        if d == col_count - 1:
            branches[d], dn_got, grad_out, y_sum = lax.optimization_barrier(
                (branches[d], dn_got, grad_out, y_sum)
            )
            grad_out = lax.psum_scatter(grad_out, "row", scatter_dimension=1, tiled=True)
        mix_grad = dot_nt(branches[d], out_all).astype(BF)
        grad_q, grad_prompt, pair, gain_part = attend_back(
            row_word, qs[d], every[d], kvs[d], blocks, mix_grad, mixes[d], logs[d], scales[d],
            coses[d], sines[d], gain_q,
        )
        grad_qs.append(grad_q)
        prompts.append(grad_prompt)
        pairs.append(pair)
        gain_q_grad = gain_q_grad + gain_part[0]
        if d == col_count - 1:
            grad_q, prompts[-1], pairs[-1], sent, grad_out = lax.optimization_barrier(
                (grad_q, prompts[-1], pairs[-1], sent, grad_out)
            )
        share = input_share(grad_q, wide, F32 if d == 0 else BF)
        shares.append(share)
        if d == 2:
            sent[0] = swap(after(shares[1], share), 1, col_count)
        if d > 0:
            sent.append(swap(share, d, col_count))
    grad_q = over_tokens(normed_all, after(jnp.stack(grad_qs, axis=0), shares[-1]))
    gain_one_grad = jnp.sum(grad_q * wide[:, : heads * HEAD].astype(F32), axis=1)
    grad_q = grad_q.astype(BF)
    prompt = jnp.stack(prompts, axis=0)
    prompt = lax.psum_scatter(prompt, "row", scatter_dimension=2, tiled=True)
    ffe = w_gate.shape[2]
    own_gu = after(own_grads[0], grad_q)
    grad_gate = own_gu[:, :ffe] + sum(v[:, :ffe].astype(F32) for v in gu_got)
    grad_up = own_gu[:, ffe:] + sum(v[:, ffe:].astype(F32) for v in gu_got)
    prompt, grad_gate, grad_up, _ = lax.optimization_barrier((prompt, grad_gate, grad_up, grad_q))
    prompt = to_owners(prompt)
    for d in slots:
        pair = pairs[d] + prompt[d].astype(F32)
        key_dy = back_turn(pair[0], coses[d], sines[d])
        key_hat = back_turn(kvs[d][0].astype(F32), coses[d], sines[d]) / gain_k
        gain_k_grad = gain_k_grad + jnp.sum(key_dy * key_hat, axis=0)
        key_raw = norm_back(key_dy, key_hat, scales[d][:, heads : heads + 1], gain_k)
        grad_kv = jnp.concatenate([key_raw.astype(BF), pair[1].astype(BF)], axis=1)
        grad_kvs.append(grad_kv)
        kv_moved.append(grad_kv if d == 0 else swap(grad_kv, d, col_count))
    grad_q = lax.psum_scatter(grad_q, "row", scatter_dimension=0, tiled=True)

    grad_kv = over_tokens(normed_all, jnp.stack(grad_kvs, axis=0))
    gain_one_grad = gain_one_grad + jnp.sum(
        grad_kv * wide[:, heads * HEAD : cols].astype(F32), axis=1
    )
    gain_one_grad = gain_one_grad / gain_one[0]
    grad_kv = lax.all_to_all(
        grad_kv.astype(BF).reshape(devices, -1, 2 * HEAD),
        ("row", "col"),
        split_axis=0,
        concat_axis=0,
        tiled=True,
    )
    grad_kv = jnp.sum(grad_kv.astype(F32).reshape(row_count, col_count, -1, 2 * HEAD), axis=0)
    grad_kv = grad_kv.reshape(KEY_VALUE_HEADS, sharing, -1, 2, HEAD).sum(axis=1)
    grad_kv = grad_kv.transpose(1, 2, 0, 3).reshape(-1, 2 * kv_cols)
    tail = [grad_router, gain_two_grad, gain_one_grad, gain_q_grad, gain_k_grad]
    tail = [v.reshape(devices, -1) for v in tail]
    tail.append(jnp.broadcast_to(jnp.sum(probs, axis=1)[None], (devices, experts)))
    cuts = [0]
    for v in tail:
        cuts.append(cuts[-1] + v.shape[1])
    tail = lax.all_to_all(
        jnp.concatenate(tail, axis=1), ("row", "col"), split_axis=0, concat_axis=0, tiled=True
    )
    tail = jnp.sum(tail, axis=0)
    grad_router, gain_two_grad, gain_one_grad, gain_q_grad, gain_k_grad, mean_probs = [
        tail[a:b] for a, b in zip(cuts[:-1], cuts[1:])
    ]
    mean_probs = mean_probs / tokens
    aux_loss = experts * jnp.sum(load * mean_probs)
    expert_load = jnp.stack([experts * load, experts * mean_probs])

    kv_share = dot_nt(jnp.concatenate(kv_moved, axis=1), kv_weight)
    input_sum = shares[0] + kv_share
    for got in sent:
        input_sum = input_sum + got.astype(F32)
    x_wide = x_own.astype(F32)
    x_spread = lax.rsqrt(jnp.mean(x_wide * x_wide, axis=-1, keepdims=True) + EPS)
    x_hat = x_wide * x_spread
    input_grad = hidden_grad + norm_back(input_sum, x_hat, x_spread, gain_one)

    grad_down = after(own_grads[1], kv_share) + sum(v.astype(F32) for v in dn_got)
    layer_output = (hidden + y_sum.astype(F32)).astype(BF)

    return (
        layer_output[None],
        aux_loss,
        input_grad[None],
        grad_q.astype(F32),
        grad_kv,
        grad_out.astype(F32),
        grad_router.reshape(width // devices, experts),
        gain_one_grad,
        gain_two_grad,
        gain_q_grad,
        gain_k_grad,
        grad_gate[None],
        grad_up[None],
        grad_down[None],
        expert_load,
    )


def solution(mesh):
    in_specs = (
        P("col", "row", None),
        P("col", "row", None),
        P("col", "row", None),
        P(None, "row"),
        P("row", "col"),
        P("row", None),
        P("col", "row"),
        P("row", None),
        P("row"),
        P("row"),
        P("row"),
        P("row"),
        P(("row", "col"), None, None),
        P(("row", "col"), None, None),
        P(("row", "col"), None, None),
    )
    out_specs = (
        P("col", "row", None),
        P(),
        P("col", "row", None),
        P("row", "col"),
        P(("row", "col"), None),
        P("col", "row"),
        P(("row", "col"), None),
        P(("row", "col")),
        P(("row", "col")),
        P(("row", "col")),
        P(("row", "col")),
        P(("row", "col"), None, None),
        P(("row", "col"), None, None),
        P(("row", "col"), None, None),
        P(),
    )
    return jax.shard_map(
        per_device, mesh=mesh, in_specs=in_specs, out_specs=out_specs, check_vma=False
    )
```

```python
from functools import partial
import math

import jax
import jax.numpy as jnp
from jax import lax
from jax.experimental import pallas as pl
from jax.experimental.pallas import tpu as pltpu
from jax.sharding import PartitionSpec as P

QUERY_HEADS = 32
KEY_VALUE_HEADS = 4
HEAD = 128
TOPK = 8
CONT = 256
PROMPT_TOKENS = 2048

EPS = 1e-06
THETA = 1000000.0
AUX_COEF = 0.001
LN2 = math.log(2.0)
SCALE2 = 1.0 / (math.sqrt(HEAD) * LN2)
VMEM = 56 * 1024 * 1024

BF = jnp.bfloat16
F32 = jnp.float32


def dot_nn(a, b):
    return lax.dot_general(a, b, (((1,), (0,)), ((), ())), preferred_element_type=F32)


def dot_nt(a, b):
    return lax.dot_general(a, b, (((1,), (1,)), ((), ())), preferred_element_type=F32)


def dot_tn(a, b):
    return lax.dot_general(a, b, (((0,), (0,)), ((), ())), preferred_element_type=F32)


def call(body, name, grid, in_specs, out_specs, out_shape, scratch=(), flops=0, moved=0, prefetch=0):
    return pl.pallas_call(
        body,
        name=name,
        grid_spec=pltpu.PrefetchScalarGridSpec(
            num_scalar_prefetch=prefetch,
            grid=grid,
            in_specs=in_specs,
            out_specs=out_specs,
            scratch_shapes=list(scratch),
        ),
        out_shape=out_shape,
        cost_estimate=pl.CostEstimate(
            flops=int(flops), bytes_accessed=int(moved), transcendentals=0
        ),
        compiler_params=pltpu.CompilerParams(
            dimension_semantics=("arbitrary",) * len(grid), vmem_limit_bytes=VMEM
        ),
    )


def struct(shape, dtype):
    return jax.ShapeDtypeStruct(shape, dtype)


def turn(v, cos, sin):
    return v * cos + pltpu.roll(v, HEAD // 2, 1) * sin


def turn_back(v, cos, sin):
    return v * cos + pltpu.roll(v * sin, HEAD // 2, 1)


def qkv_body(heads, x_ref, gain_ref, w_ref, cos_ref, sin_ref, qg_ref, kg_ref, q_ref, kv_ref, a_ref, r_ref):
    x = x_ref[...].astype(F32)
    normed = x * lax.rsqrt(jnp.mean(x * x, axis=-1, keepdims=True) + EPS) * gain_ref[...]
    low = normed.astype(BF)
    a_ref[...] = low
    raw = dot_nn(low, w_ref[...])
    cos = cos_ref[...]
    sin = sin_ref[...]
    lane = lax.broadcasted_iota(jnp.int32, (x.shape[0], HEAD), 1)
    scales = jnp.zeros((x.shape[0], HEAD), F32)
    for h in range(heads + 1):
        v = raw[:, h * HEAD : (h + 1) * HEAD]
        r = lax.rsqrt(jnp.mean(v * v, axis=-1, keepdims=True) + EPS)
        scales = jnp.where(lane == h, r, scales)
        if h < heads:
            q_ref[h] = (turn(v * r * qg_ref[...], cos, sin) * SCALE2).astype(BF)
        else:
            kv_ref[0] = turn(v * r * kg_ref[...], cos, sin).astype(BF)
    kv_ref[1] = raw[:, (heads + 1) * HEAD :].astype(BF)
    r_ref[...] = scales


def qkv(x, gain, w, cos, sin, qg, kg, heads):
    rows, width = x.shape
    cols = (heads + 2) * HEAD
    tile = 256
    whole = lambda i: (0, 0)
    row = lambda i: (i, 0)
    return call(
        partial(qkv_body, heads),
        "qkv",
        (rows // tile,),
        [
            pl.BlockSpec((tile, width), row),
            pl.BlockSpec((1, width), whole),
            pl.BlockSpec((width, cols), whole),
            pl.BlockSpec((tile, HEAD), row),
            pl.BlockSpec((tile, HEAD), row),
            pl.BlockSpec((1, HEAD), whole),
            pl.BlockSpec((1, HEAD), whole),
        ],
        [
            pl.BlockSpec((heads, tile, HEAD), lambda i: (0, i, 0)),
            pl.BlockSpec((2, tile, HEAD), lambda i: (0, i, 0)),
            pl.BlockSpec((tile, width), row),
            pl.BlockSpec((tile, HEAD), row),
        ],
        [
            struct((heads, rows, HEAD), BF),
            struct((2, rows, HEAD), BF),
            struct((rows, width), BF),
            struct((rows, HEAD), F32),
        ],
        flops=2 * rows * width * cols,
        moved=2 * (2 * rows * width + width * cols + rows * cols),
    )(x, gain, w, cos, sin, qg, kg)


def causal(count):
    q_at = lax.broadcasted_iota(jnp.int32, (count, CONT, CONT), 1)
    k_at = lax.broadcasted_iota(jnp.int32, (count, CONT, CONT), 2)
    return (k_at <= q_at).reshape(count * CONT, CONT)


def attend_body(heads, per, blocks, rows, row_ref, q_ref, kp_ref, vp_ref, kv_ref, o_ref, l_ref, vp_one, vl_one, acc):
    at = pl.program_id(0)
    part = pl.program_id(1)
    row = row_ref[0]

    @pl.when((at == 0) & (part == 0))
    def _():
        for j in range(blocks):
            vp_one[j * rows : (j + 1) * rows, :HEAD] = vp_ref[j, 0]
        vp_one[:, HEAD:] = jnp.ones((blocks * rows, HEAD), BF)
        vl_one[:, :HEAD] = kv_ref[1]
        vl_one[:, HEAD:] = jnp.ones((rows, HEAD), BF)

    q = q_ref[...].reshape(per * CONT, HEAD)
    here = pl.ds(pl.multiple_of(at * CONT, CONT), CONT)
    weights = jnp.where(causal(per), jnp.exp2(dot_nt(q, kv_ref[0, here, :])), 0.0).astype(BF)
    acc[...] = dot_nn(weights, vl_one[here, :])

    @pl.when(row < blocks)
    def _():
        for j in range(rows // CONT - 1):

            @pl.when(j < at)
            def _():
                piece = slice(j * CONT, (j + 1) * CONT)
                weights = jnp.exp2(dot_nt(q, kv_ref[0, piece, :])).astype(BF)
                acc[...] += dot_nn(weights, vl_one[piece, :])

        @pl.loop(0, row)
        def _(j):
            weights = jnp.exp2(dot_nt(q, kp_ref[j, 0])).astype(BF)
            acc[...] += dot_nn(weights, vp_one[pl.ds(pl.multiple_of(j * rows, rows), rows), :])

    @pl.when(row >= blocks)
    def _():
        keys = kp_ref[...].reshape(blocks * rows, HEAD)
        weights = jnp.exp2(dot_nt(q, keys)).astype(BF)
        acc[...] += dot_nn(weights, vp_one[...])

    total = acc[:, HEAD:]
    out = (acc[:, :HEAD] / total).astype(BF)
    logs = jnp.log2(total)
    lane = lax.broadcasted_iota(jnp.int32, (CONT, HEAD), 1)

    @pl.when(part == 0)
    def _():
        l_ref[...] = jnp.zeros((CONT, HEAD), F32)

    held = l_ref[...]
    for p in range(per):
        o_ref[:, p * HEAD : (p + 1) * HEAD] = out[p * CONT : (p + 1) * CONT]
        held = jnp.where(lane == part * per + p, logs[p * CONT : (p + 1) * CONT], held)
    l_ref[...] = held


def attend(row, q, every, kv, blocks):
    heads, rows, _ = q.shape
    per = min(4, heads)
    every, place = every
    keys = blocks * rows
    return call(
        partial(attend_body, heads, per, blocks, rows),
        "attend",
        (rows // CONT, heads // per),
        [
            pl.BlockSpec((per, CONT, HEAD), lambda i, h, s: (h, i, 0)),
            pl.BlockSpec((blocks, 1, rows, HEAD), lambda i, h, s: (0, 2 * place, 0, 0)),
            pl.BlockSpec((blocks, 1, rows, HEAD), lambda i, h, s: (0, 2 * place + 1, 0, 0)),
            pl.BlockSpec((2, rows, HEAD), lambda i, h, s: (0, 0, 0)),
        ],
        [
            pl.BlockSpec((CONT, per * HEAD), lambda i, h, s: (i, h)),
            pl.BlockSpec((CONT, HEAD), lambda i, h, s: (i, 0)),
        ],
        [struct((rows, heads * HEAD), BF), struct((rows, HEAD), F32)],
        scratch=[
            pltpu.VMEM((keys, 2 * HEAD), BF),
            pltpu.VMEM((rows, 2 * HEAD), BF),
            pltpu.VMEM((per * CONT, 2 * HEAD), F32),
        ],
        flops=8 * rows * heads * (keys + CONT) * HEAD,
        moved=2 * HEAD * (2 * rows * heads + 2 * keys),
        prefetch=1,
    )(row, q, every, every, kv)


def attend_back_body(
    heads, per, blocks, rows,
    row_ref, q_ref, kp_ref, vp_ref, kv_ref, do_ref, o_ref, l_ref, r_ref, cos_ref, sin_ref, qg_ref,
    dq_ref, dp_ref, dl_ref, g_ref,
    dq, dkp, dvp,
):
    at = pl.program_id(0)
    part = pl.program_id(1)
    row = row_ref[0]

    @pl.when((at == 0) & (part == 0))
    def _():
        dkp[...] = jnp.zeros_like(dkp)
        dvp[...] = jnp.zeros_like(dvp)
        dl_ref[...] = jnp.zeros_like(dl_ref)
        g_ref[...] = jnp.zeros_like(g_ref)

    q = q_ref[...].reshape(per * CONT, HEAD)
    lane = lax.broadcasted_iota(jnp.int32, (CONT, HEAD), 1)
    line = lax.broadcasted_iota(jnp.int32, (HEAD, CONT), 0)
    logs_t = l_ref[...].T
    do_parts, logs, centers, scales = [], [], [], []
    for p in range(per):
        do_part = do_ref[:, p * HEAD : (p + 1) * HEAD]
        do_parts.append(do_part)
        both = do_part.astype(F32) * o_ref[:, p * HEAD : (p + 1) * HEAD].astype(F32)
        centers.append(jnp.sum(both.T, axis=0, keepdims=True))
        head = part * per + p
        logs.append(jnp.sum(jnp.where(line == head, logs_t, 0.0), axis=0, keepdims=True))
        scales.append(jnp.sum(jnp.where(lane == head, r_ref[...], 0.0), axis=-1, keepdims=True))
    do = jnp.concatenate(do_parts, axis=0)
    center = jnp.concatenate(centers, axis=1)
    log = jnp.concatenate(logs, axis=1)

    def block(k, v, mask):
        probs = jnp.exp2(dot_nt(k, q) - log)
        if mask is not None:
            probs = jnp.where(mask, probs, 0.0)
        ds = (probs * (dot_nt(v, do) - center)).astype(BF)
        return dot_tn(ds, k), dot_nn(ds, q), dot_nn(probs.astype(BF), do)

    k_at = lax.broadcasted_iota(jnp.int32, (CONT, CONT), 0)
    q_at = lax.broadcasted_iota(jnp.int32, (CONT, CONT), 1)
    seen = jnp.concatenate([k_at <= q_at] * per, axis=1)
    here = pl.ds(pl.multiple_of(at * CONT, CONT), CONT)
    a, b, c = block(kv_ref[0, here, :], kv_ref[1, here, :], seen)
    dq[...] = a
    dl_ref[0, here, :] += b
    dl_ref[1, here, :] += c

    @pl.when(row < blocks)
    def _():
        for j in range(rows // CONT - 1):

            @pl.when(j < at)
            def _():
                piece = slice(j * CONT, (j + 1) * CONT)
                a, b, c = block(kv_ref[0, piece, :], kv_ref[1, piece, :], None)
                dq[...] += a
                dl_ref[0, piece, :] += b
                dl_ref[1, piece, :] += c

    @pl.loop(0, jnp.minimum(row, blocks))
    def _(j):
        a, b, c = block(kp_ref[j, 0], vp_ref[j, 0], None)
        piece = pl.ds(pl.multiple_of(j * rows, rows), rows)
        dq[...] += a
        dkp[piece, :] += b
        dvp[piece, :] += c

    cos = cos_ref[...]
    sin = sin_ref[...]
    gain = qg_ref[...]
    tally = jnp.zeros((1, HEAD), F32)
    for p in range(per):
        dy = turn_back(dq[p * CONT : (p + 1) * CONT, :] * (SCALE2 * LN2), cos, sin)
        hat = turn_back(q[p * CONT : (p + 1) * CONT].astype(F32), cos, sin) * (1.0 / SCALE2) / gain
        tally += jnp.sum(dy * hat, axis=0, keepdims=True)
        dyg = dy * gain
        raw = scales[p] * (dyg - hat * jnp.mean(dyg * hat, axis=-1, keepdims=True))
        dq_ref[:, p * HEAD : (p + 1) * HEAD] = raw.astype(BF)
    g_ref[0:1, :] += tally

    @pl.when((at == rows // CONT - 1) & (part == heads // per - 1))
    def _():
        dp_ref[0] = (dkp[...] * LN2).astype(BF)
        dp_ref[1] = dvp[...].astype(BF)
        dl_ref[0] = dl_ref[0] * LN2


def attend_back(row, q, every, kv, blocks, do, o, logs, scales, cos, sin, qg):
    heads, rows, _ = q.shape
    per = min(8, heads)
    every, place = every
    keys = blocks * rows
    tile = lambda i, h, s: (i, 0)
    head = lambda i, h, s: (i, h)
    return call(
        partial(attend_back_body, heads, per, blocks, rows),
        "attend_back",
        (rows // CONT, heads // per),
        [
            pl.BlockSpec((per, CONT, HEAD), lambda i, h, s: (h, i, 0)),
            pl.BlockSpec((blocks, 1, rows, HEAD), lambda i, h, s: (0, 2 * place, 0, 0)),
            pl.BlockSpec((blocks, 1, rows, HEAD), lambda i, h, s: (0, 2 * place + 1, 0, 0)),
            pl.BlockSpec((2, rows, HEAD), lambda i, h, s: (0, 0, 0)),
            pl.BlockSpec((CONT, per * HEAD), head),
            pl.BlockSpec((CONT, per * HEAD), head),
            pl.BlockSpec((CONT, HEAD), tile),
            pl.BlockSpec((CONT, HEAD), tile),
            pl.BlockSpec((CONT, HEAD), tile),
            pl.BlockSpec((CONT, HEAD), tile),
            pl.BlockSpec((1, HEAD), lambda i, h, s: (0, 0)),
        ],
        [
            pl.BlockSpec((CONT, per * HEAD), head),
            pl.BlockSpec((2, keys, HEAD), lambda i, h, s: (0, 0, 0)),
            pl.BlockSpec((2, rows, HEAD), lambda i, h, s: (0, 0, 0)),
            pl.BlockSpec((8, HEAD), lambda i, h, s: (0, 0)),
        ],
        [
            struct((rows, heads * HEAD), BF),
            struct((2, keys, HEAD), BF),
            struct((2, rows, HEAD), F32),
            struct((8, HEAD), F32),
        ],
        scratch=[
            pltpu.VMEM((per * CONT, HEAD), F32),
            pltpu.VMEM((keys, HEAD), F32),
            pltpu.VMEM((keys, HEAD), F32),
        ],
        flops=20 * rows * heads * (keys + CONT) * HEAD,
        moved=2 * HEAD * (4 * rows * heads + 4 * keys),
        prefetch=1,
    )(row, q, every, every, kv, do, o, logs, scales, cos, sin, qg)


def dispatch_body(count, cap, rank_ref, rows_ref, *out_refs):
    tokens = rows_ref.shape[1]
    slot = lax.broadcasted_iota(jnp.int32, (cap, tokens), 0)
    for d in range(count):
        hot = (rank_ref[0, d : d + 1, :] == slot).astype(F32).astype(BF)
        out_refs[d][0] = dot_nn(hot, rows_ref[0]).astype(BF)


def dispatch(rank, rows, cap):
    sources, count, tokens = rank.shape
    width = rows.shape[2]
    return call(
        partial(dispatch_body, count, cap),
        "dispatch",
        (sources,),
        [
            pl.BlockSpec((1, count, tokens), lambda s: (s, 0, 0)),
            pl.BlockSpec((1, tokens, width), lambda s: (s, 0, 0)),
        ],
        [pl.BlockSpec((1, cap, width), lambda s: (s, 0, 0))] * count,
        [struct((sources, cap, width), BF)] * count,
        flops=2 * sources * count * cap * tokens * width,
        moved=2 * sources * width * (tokens + count * cap),
    )(rank, rows)


def route_body(count, cap, ids_ref, rank_ref, rows_ref, mask_ref, router_ref, gate_ref, *out_refs):
    tokens = rows_ref.shape[1]
    rows = rows_ref[0]
    logits = dot_nt(router_ref[...], rows)
    weights = jnp.exp(logits - jnp.max(logits, axis=0, keepdims=True))
    probs = weights / jnp.sum(weights, axis=0, keepdims=True)
    picked = probs * mask_ref[0]
    gates = picked / jnp.sum(picked, axis=0, keepdims=True)
    expert_at = lax.broadcasted_iota(jnp.int32, gates.shape, 0)
    slot = lax.broadcasted_iota(jnp.int32, (cap, tokens), 0)
    for d in range(count):
        here = rank_ref[0, d : d + 1, :] == slot
        out_refs[d][0] = dot_nn(here.astype(F32).astype(BF), rows).astype(BF)
        mine = jnp.sum(jnp.where(expert_at == ids_ref[d], gates, 0.0), axis=0, keepdims=True)
        gate_ref[d, 0] = jnp.sum(jnp.where(here, mine, 0.0), axis=1, keepdims=True)


def route_dispatch(ids, rank, rows, mask, router, cap):
    sources, count, tokens = rank.shape
    width = rows.shape[2]
    experts = router.shape[0]
    return call(
        partial(route_body, count, cap),
        "route_dispatch",
        (sources,),
        [
            pl.BlockSpec((1, count, tokens), lambda s, i: (s, 0, 0)),
            pl.BlockSpec((1, tokens, width), lambda s, i: (s, 0, 0)),
            pl.BlockSpec((1, experts, tokens), lambda s, i: (s, 0, 0)),
            pl.BlockSpec((experts, width), lambda s, i: (0, 0)),
        ],
        [
            pl.BlockSpec((count, 1, cap, 1), lambda s, i: (0, s, 0, 0)),
        ]
        + [pl.BlockSpec((1, cap, width), lambda s, i: (s, 0, 0))] * count,
        [struct((count, sources, cap, 1), F32)]
        + [struct((sources, cap, width), BF)] * count,
        flops=2 * sources * count * cap * tokens * width,
        moved=2 * sources * width * (tokens + count * cap),
        prefetch=1,
    )(ids, rank, rows, mask, router)


def share_body(g_ref, w_ref, out_ref):
    out_ref[...] = dot_nt(g_ref[...], w_ref[...]).astype(out_ref.dtype)


def input_share(grads, w, dtype):
    rows, cols = grads.shape
    width = w.shape[0]
    tile = 256
    return call(
        share_body,
        "input_share",
        (rows // tile,),
        [
            pl.BlockSpec((tile, cols), lambda i: (i, 0)),
            pl.BlockSpec((width, cols), lambda i: (0, 0)),
        ],
        pl.BlockSpec((tile, width), lambda i: (i, 0)),
        struct((rows, width), dtype),
        flops=2 * rows * width * cols,
        moved=2 * (rows * width + width * cols + rows * cols),
    )(grads, w)


def combine_body(count, cap, scored, rank_ref, *refs):
    tokens = rank_ref.shape[1]
    slot = lax.broadcasted_iota(jnp.int32, (tokens, cap), 1)
    hots = [(rank_ref[0, :, d : d + 1] == slot).astype(F32).astype(BF) for d in range(count)]

    def gathered(parts):
        if cap % HEAD:
            return sum(dot_nn(hot, part[0]) for hot, part in zip(hots, parts))
        return dot_nn(
            jnp.concatenate(hots, axis=1), jnp.concatenate([p[0] for p in parts], axis=0)
        )

    refs[count * (2 if scored else 1)][0] = gathered(refs[:count]).astype(BF)
    if scored:
        scores = gathered(refs[count : 2 * count])
        lane = lax.broadcasted_iota(jnp.int32, scores.shape, 1)
        for d in range(count):
            mine = jnp.where(lane // 4 == d, scores, 0.0)
            refs[-1][0, :, d : d + 1] = jnp.sum(mine, axis=-1, keepdims=True)


def combine(rank_t, parts, scores=()):
    sources, tokens, count = rank_t.shape
    cap = parts[0].shape[0] // sources
    width = parts[0].shape[1]
    at = lambda s: (s, 0, 0)
    cut = lambda v: v.reshape(sources, cap, v.shape[1])
    out_specs = [pl.BlockSpec((1, tokens, width), at)]
    out_shape = [struct((sources, tokens, width), BF)]
    if scores:
        out_specs.append(pl.BlockSpec((1, tokens, count), at))
        out_shape.append(struct((sources, tokens, count), F32))
    return call(
        partial(combine_body, count, cap, bool(scores)),
        "combine",
        (sources,),
        [pl.BlockSpec((1, tokens, count), at)]
        + [pl.BlockSpec((1, cap, width), at)] * count
        + [pl.BlockSpec((1, cap, HEAD), at)] * len(scores),
        out_specs,
        out_shape,
    )(rank_t, *[cut(p) for p in parts], *[cut(p) for p in scores])


def expert_body(
    slot, x_ref, up_ref, gate_ref, wga_ref, wgb_ref, wua_ref, wub_ref, wda_ref, wdb_ref,
    db_ref, m_ref, duw_ref, dg_ref,
):
    half = wga_ref.shape[1]
    hidden = wga_ref.shape[2]
    xa, xb = x_ref[:, :half], x_ref[:, half:]
    gate = gate_ref[...]
    u = dot_nn(xa, wga_ref[0]) + dot_nn(xb, wgb_ref[0])
    w = dot_nn(xa, wua_ref[0]) + dot_nn(xb, wub_ref[0])
    sigma = 1.0 / (1.0 + jnp.exp(-u))
    silu = u * sigma
    inner = silu * w
    low = inner.astype(BF)
    m_ref[...] = (inner * gate).astype(BF)
    up = up_ref[...]
    back = jnp.concatenate([dot_nt(up, wda_ref[0]), dot_nt(up, wdb_ref[0])], axis=1)
    score = jnp.sum(low.astype(F32) * back, axis=-1, keepdims=True)
    lane = lax.broadcasted_iota(jnp.int32, dg_ref.shape, 1)
    high = score.astype(BF)
    rest = score - high.astype(F32)
    middle = rest.astype(BF)
    last = (rest - middle.astype(F32)).astype(BF)
    pieces = jnp.where(lane == 4 * slot, high.astype(F32), 0.0)
    pieces = jnp.where(lane == 4 * slot + 1, middle.astype(F32), pieces)
    dg_ref[...] = jnp.where(lane == 4 * slot + 2, last.astype(F32), pieces).astype(BF)
    back = back * gate
    du = (back * w * sigma * (1.0 + u * (1.0 - sigma))).astype(BF)
    dw = (back * silu).astype(BF)
    duw_ref[:, :hidden] = du
    duw_ref[:, hidden:] = dw
    db_ref[:, :half] = (dot_nt(du, wga_ref[0]) + dot_nt(dw, wua_ref[0])).astype(BF)
    db_ref[:, half:] = (dot_nt(du, wgb_ref[0]) + dot_nt(dw, wub_ref[0])).astype(BF)


def expert(slot, x, up, gate, weights):
    rows, width = x.shape
    hidden = weights[0][0].shape[2]
    tile = min(256, rows)
    at = lambda i: (i, 0)
    specs, arrays = [], []
    for parts in weights:
        shape = (1, parts[0].shape[1] * len(parts) // 2, parts[0].shape[2])
        for j in range(2):
            place = j if len(parts) == 1 else 0
            specs.append(pl.BlockSpec(shape, lambda i, place=place: (0, place, 0)))
            arrays.append(parts[0] if len(parts) == 1 else parts[j])
    return call(
        partial(expert_body, slot),
        "expert",
        (rows // tile,),
        [
            pl.BlockSpec((tile, width), at),
            pl.BlockSpec((tile, width), at),
            pl.BlockSpec((tile, 1), at),
        ]
        + specs,
        [
            pl.BlockSpec((tile, width), at),
            pl.BlockSpec((tile, hidden), at),
            pl.BlockSpec((tile, 2 * hidden), at),
            pl.BlockSpec((tile, HEAD), at),
        ],
        [
            struct((rows, width), BF),
            struct((rows, hidden), BF),
            struct((rows, 2 * hidden), BF),
            struct((rows, HEAD), BF),
        ],
        flops=10 * rows * width * hidden,
        moved=2 * (3 * rows * width + 3 * rows * hidden + 3 * width * hidden),
    )(x, up, gate, *arrays)


def swap(v, step, count):
    return lax.ppermute(v, "col", [(i, i ^ step) for i in range(count)])


def near(v, count):
    return [swap(v, d, count) for d in ((1, 2) if count == 4 else range(1, count))]


def far(one, two, count):
    half = one.shape[1] // 2
    return [swap(one[:, :half], 2, count), swap(two[:, half:], 1, count)]


def halves(v):
    return v[:, : v.shape[1] // 2], v[:, v.shape[1] // 2 :]


def whole(parts):
    return parts[0] if len(parts) == 1 else jnp.concatenate(parts, axis=1)


def deliver_far(part, count):
    half = part.shape[0] // 2
    return swap(part[:half], 1, count), swap(part[half:], 2, count)


def join(part, got, first):
    half = part.shape[0] // 2
    wide = jnp.pad(got.astype(F32), ((0, half) if first else (half, 0), (0, 0)))
    return (part.astype(F32) + wide).astype(BF)


def after(value, *earlier):
    return lax.optimization_barrier((value,) + earlier)[0]


def norm_back(grad, hat, spread, gain):
    scaled = grad * gain
    return spread * (scaled - hat * jnp.mean(scaled * hat, axis=-1, keepdims=True))


def per_device(
    layer_input, out_grad, routes, positions, w_q, key_value_weight, w_out, router,
    ln_attn, ln_moe, q_gain, k_gain, w_gate, w_up, w_down,
):
    rows, width = layer_input.shape[1:]
    row_count, col_count = lax.axis_size("row"), lax.axis_size("col")
    row_at, col_at = lax.axis_index("row"), lax.axis_index("col")
    devices = row_count * col_count
    experts = w_gate.shape[0] * devices
    assert w_gate.shape[0] == 1
    cap = rows * TOPK // experts
    tokens = rows * devices
    heads = w_q.shape[1] // HEAD
    sharing = QUERY_HEADS // KEY_VALUE_HEADS // heads
    blocks = PROMPT_TOKENS // rows
    slots = range(col_count)
    others = list(slots[1:])
    members = [col_at ^ d for d in slots]
    row_word = row_at.astype(jnp.int32).reshape(1)

    x_own = layer_input[0]
    up_own = out_grad[0]

    kv_cols = KEY_VALUE_HEADS * HEAD

    def kv_pick(weight, member):
        head = member // sharing
        return [
            lax.dynamic_slice_in_dim(weight, head * HEAD, HEAD, 1),
            lax.dynamic_slice_in_dim(weight, kv_cols + head * HEAD, HEAD, 1),
        ]

    cols = (heads + 2) * HEAD
    piece, head_piece = ln_attn.shape[0], q_gain.shape[0]
    rest = [jnp.pad(g, (0, piece - head_piece))[:, None] for g in (q_gain, k_gain)]
    rest = [router, ln_attn[:, None], ln_moe[:, None]] + rest
    wide = jnp.concatenate([w_q] + kv_pick(key_value_weight, col_at) + rest, axis=1)
    wide = jnp.pad(wide, ((0, 0), (0, -wide.shape[1] % HEAD)))
    wide = lax.all_gather(wide, "row", axis=0, tiled=True)
    extra = wide[:, cols:]
    router_all = extra[:, :experts]
    gain_one = extra[:, experts].astype(F32)[None]
    gain_two = extra[:, experts + 1].astype(F32)[None]
    head_gains = extra.reshape(row_count, piece, -1)[:, :head_piece].astype(F32)
    gain_q = head_gains[:, :, experts + 2].reshape(1, HEAD)
    gain_k = head_gains[:, :, experts + 3].reshape(1, HEAD)

    four = col_count == 4
    beside = near(layer_input, col_count)

    routes_all = lax.all_gather(routes[0], "row", axis=0)
    expert_ids = jnp.arange(experts, dtype=jnp.int32)
    flat_routes = routes_all.transpose(0, 2, 1)
    mask_all = jnp.any(flat_routes[:, :, None, :] == expert_ids[None, None, :, None], axis=1)
    mine_ids = jnp.stack([row_at * col_count + m for m in members]).astype(jnp.int32)
    has = jnp.stack(
        [lax.dynamic_index_in_dim(mask_all, e, 1, keepdims=False) for e in mine_ids], axis=1
    )
    place = jnp.arange(rows)
    before = (place[:, None] <= place[None, :]).astype(BF)
    order = jnp.einsum("rdt,tu->rdu", has.astype(BF), before, preferred_element_type=F32)
    rank = jnp.where(has, order.astype(jnp.int32) - 1, -1)
    rank_t = rank.transpose(0, 2, 1)
    mask_all = mask_all.astype(F32)

    def over_col(v):
        step = 1
        while step < col_count:
            v = v + swap(v, step, col_count)
            step *= 2
        return v

    load = over_col(jnp.sum(mask_all, axis=(0, 2))) / (tokens * TOPK)

    inv_freq = THETA ** (-2.0 * jnp.arange(HEAD // 2, dtype=F32) / HEAD)
    coses, sines = [], []
    for m in members:
        spots = lax.dynamic_index_in_dim(positions, m, 0, keepdims=False).astype(F32)
        angles = spots[:, None] * inv_freq[None, :]
        cos, sin = jnp.cos(angles), jnp.sin(angles)
        coses.append(jnp.concatenate([cos, cos], axis=1))
        sines.append(jnp.concatenate([-sin, sin], axis=1))

    beside, rank, rank_t, mask_all, coses, sines, load = lax.optimization_barrier(
        (beside, rank, rank_t, mask_all, coses, sines, load)
    )
    out_all = lax.all_gather(after(w_out, beside), "row", axis=1, tiled=True)
    xs = [x_own] + [v[0] for v in beside]
    if four:
        xs.append(jnp.concatenate(far(*beside, col_count), axis=1)[0])
    qs, kvs, normed, scales, every = [[None] * col_count for _ in range(5)]
    line = others + [0]
    batch = max(1, col_count // 2)
    for first in range(0, col_count, batch):
        ahead = line[first : first + batch]
        for d in ahead:
            qs[d], kvs[d], normed[d], scales[d] = qkv(
                xs[d], gain_one, wide, coses[d], sines[d], gain_q, gain_k, heads
            )
        got = jnp.concatenate([kvs[d] for d in ahead], axis=0)
        if first == 0:
            got, out_all, xs[-1] = lax.optimization_barrier((got, out_all, xs[-1]))
        got = lax.all_gather(got, "row", axis=0)
        for j, d in enumerate(ahead):
            every[d] = (got, j)
    gates, ups = after((w_gate, w_up), xs[-1])
    if four:
        gates_near, ups_near = [[near(v, col_count) for v in halves(w)] for w in (gates, ups)]
    else:
        gates_near, ups_near = [near(gates, col_count)], [near(ups, col_count)]
    mixes, logs = [None] * col_count, [None] * col_count
    hidden = x_own.astype(F32)
    share, sent = None, []
    for at, d in enumerate(line):
        q = qs[d]
        if at > 0:
            q = after(q, share)
        else:
            q, gates_near[0] = lax.optimization_barrier((q, gates_near[0]))
        mixes[d], logs[d] = attend(row_word, q, every[d], kvs[d], blocks)
        mix = mixes[d]
        if at == 0:
            mix, gates_near[-1] = lax.optimization_barrier((mix, gates_near[-1]))
        elif at == 1:
            mix, ups_near[0] = lax.optimization_barrier((mix, ups_near[0]))
        elif d == 0:
            mix, sent[: at - 1] = lax.optimization_barrier((mix, sent[: at - 1]))
        share = jnp.dot(mix, out_all, preferred_element_type=F32)
        if d != 0:
            share = share.astype(BF)
            sent.append(swap(share, d, col_count))
    share, sent = lax.optimization_barrier((share, sent))
    for got in sent:
        hidden = hidden + got.astype(F32)
    hidden = hidden + share
    up_all = lax.all_gather(after(up_own, mixes[line[0]]), "row", axis=0)

    spread = lax.rsqrt(jnp.mean(hidden * hidden, axis=-1, keepdims=True) + EPS)
    second = (hidden * spread * gain_two).astype(BF)
    second_all = lax.all_gather(second, "row", axis=0)

    downs_near = near(after(w_down, share), col_count)
    gate_all = [[w_gate]] + [list(v) for v in zip(*gates_near)]
    up_w_all = [[w_up]] + [list(v) for v in zip(*ups_near)]
    down_all = [[w_down]] + [[w] for w in downs_near]
    if four:
        rank, ups_near, down_all = lax.optimization_barrier((rank, ups_near, down_all))
        up_w_all = [[w_up]] + [list(v) for v in zip(*ups_near)]
        gates_near, _ = lax.optimization_barrier((gates_near, ups_near))
        far_of = lambda one, two: [swap(one[0], 2, col_count), swap(two[1], 1, col_count)]
        gate_all.append(far_of(*zip(*gates_near)))

    expert_up = [v.reshape(row_count * cap, width) for v in dispatch(rank, up_all, cap)]
    router_t = router_all.T
    second_all, expert_up, gate_all = lax.optimization_barrier((second_all, expert_up, gate_all))
    gate_pairs, *expert_in = route_dispatch(
        mine_ids, rank, second_all, mask_all, router_t, cap
    )
    expert_in = [v.reshape(row_count * cap, width) for v in expert_in]
    gate_pairs = gate_pairs.reshape(col_count, row_count * cap, 1)
    if four:
        up_w_all.append(far_of(*zip(*ups_near)))
        expert_in[0], up_w_all = lax.optimization_barrier((expert_in[0], up_w_all))
        down_far = far_of(*[halves(v[0]) for v in down_all[1:3]])
    kv_all = lax.all_gather(after(key_value_weight, expert_in[0]), "row", axis=0, tiled=True)
    dbs, ms, duws, dgs = [[None] * col_count for _ in range(4)]
    grad_gu, grad_dn = [None] * col_count, [None] * col_count

    def gate_up_grad(d):
        grad_gu[d] = dot_tn(expert_in[d], duws[d]).astype(F32 if d == 0 else BF)

    def down_grad(d):
        grad_dn[d] = dot_tn(ms[d], expert_up[d]).astype(F32 if d == 0 else BF)

    far_sent = []
    order = [0, 3, 1, 2] if four else list(slots)
    for at, d in enumerate(order):
        if at > 0:
            held = [g for g in grad_gu + grad_dn if g is not None]
            expert_in[d] = after(expert_in[d], dgs[order[at - 1]], held)
        if four and at == 1:
            expert_in[d], down_far = lax.optimization_barrier((expert_in[d], down_far))
            down_all.append(down_far)
        weights = [gate_all[d], up_w_all[d], down_all[d]]
        dbs[d], ms[d], duws[d], dgs[d] = expert(
            d, expert_in[d], expert_up[d], gate_pairs[d], weights
        )
        if four and at == 1:
            gate_up_grad(d)
            down_grad(d)
            far_sent = [deliver_far(grad_gu[d], col_count), deliver_far(grad_dn[d], col_count)]
    if four:
        dbs[0], far_sent[0] = lax.optimization_barrier((dbs[0], far_sent[0]))
    dbs[0], kv_all = lax.optimization_barrier((dbs[0], kv_all))
    db_part, score_grads = combine(rank_t, dbs, dgs)
    db_sum = lax.psum_scatter(db_part, "row", scatter_dimension=0)
    duws, ms, _ = lax.optimization_barrier((duws, ms, db_part))
    remaining = (1, 2) if four else range(1, col_count)
    for d in remaining:
        gate_up_grad(d)
    exchange = lambda sends: [swap(v, d, col_count) for d, v in enumerate(sends, 1)]
    gu_sends = grad_gu[1:]
    if four:
        gu_two, gu_one = far_sent[0]
        gu_sends = [join(grad_gu[1], gu_one, False), join(grad_gu[2], gu_two, True)]
    if four:
        gu_sends, far_sent[1] = lax.optimization_barrier((gu_sends, far_sent[1]))
    gu_got = exchange(gu_sends)
    ms, gu_sends = lax.optimization_barrier((ms, gu_sends))
    for d in remaining:
        down_grad(d)
    dn_sends = grad_dn[1:]
    if four:
        dn_two, dn_one = far_sent[1]
        dn_sends = [join(grad_dn[1], dn_one, False), join(grad_dn[2], dn_two, True)]
    gate_up_grad(0)
    down_grad(0)
    ys = [dot_nn(m, whole(w)[0]).astype(BF) for m, w in zip(ms, down_all)]
    (y_part,) = combine(rank_t, ys)

    score_grads = lax.all_to_all(score_grads, "row", split_axis=0, concat_axis=0, tiled=True)
    mask_own = jnp.any(routes[0].T[:, None, :] == expert_ids[None, :, None], axis=0)
    logits = lax.dot_general(
        router_all, second, (((0,), (1,)), ((), ())), preferred_element_type=F32
    )
    probs = jax.nn.softmax(logits, axis=0)
    picked = jnp.where(mask_own, probs, 0.0)
    total = jnp.sum(picked, axis=0, keepdims=True)
    gates = picked / total
    to_member = jnp.stack(members)[:, None] == jnp.arange(col_count)[None, :]
    gate_grad = jnp.sum(
        jnp.where(to_member, score_grads[..., None], 0.0), axis=2
    )
    gate_grad = gate_grad.transpose(0, 2, 1).reshape(experts, rows)
    weighted = jnp.sum(gate_grad * gates, axis=0, keepdims=True)
    prob_grad = (
        jnp.where(mask_own, (gate_grad - weighted) / total, 0.0)
        + AUX_COEF * experts * load[:, None] / tokens
    )
    logit_low = (probs * (prob_grad - jnp.sum(probs * prob_grad, axis=0, keepdims=True))).astype(BF)
    grad_router = lax.dot_general(
        second, logit_low, (((0,), (1,)), ((), ())), preferred_element_type=F32
    )
    router_part = lax.dot_general(
        logit_low, router_all, (((0,), (1,)), ((), ())), preferred_element_type=F32
    )

    kv_weight = jnp.concatenate([w for m in members for w in kv_pick(kv_all, m)], axis=1)
    db_sum, gu_got, y_part, router_part, grad_router, kv_weight, own_grads, dn_sends = (
        lax.optimization_barrier(
            (
                db_sum, gu_got, y_part, router_part, grad_router, kv_weight,
                (grad_gu[0], grad_dn[0]), dn_sends,
            )
        )
    )
    y_sum = lax.psum_scatter(y_part, "row", scatter_dimension=0)
    second_grad = db_sum.astype(F32) + router_part
    hat = hidden * spread
    gain_two_grad = jnp.sum(second_grad * hat, axis=0)
    hidden_grad = up_own.astype(F32) + norm_back(second_grad, hat, spread, gain_two)
    branch = hidden_grad.astype(BF)

    beside = near(branch[None], col_count)
    branches = [branch] + [v[0] for v in beside]
    grad_qs, prompts, pairs, shares, sent, grad_kvs, kv_moved = [], [], [], [], [], [], []
    gain_q_grad, gain_k_grad = 0.0, 0.0

    def back_turn(v, cos, sin):
        moved = v * sin
        half = HEAD // 2
        return v * cos + jnp.concatenate([moved[:, half:], moved[:, :half]], axis=1)

    normed_all = jnp.stack(normed, axis=0)
    over_tokens = lambda a, b: lax.dot_general(
        a, b, (((0, 1), (0, 1)), ((), ())), preferred_element_type=F32
    )
    mixes_all = jnp.stack(mixes, axis=0)
    grad_out = None

    def to_owners(prompt):
        chunk = prompt.shape[2]
        return jnp.concatenate(
            [
                lax.ppermute(prompt, "row", [(rows // chunk * i + a, i) for i in range(blocks)])
                for a in range(rows // chunk)
            ],
            axis=2,
        )

    for d in slots:
        if d == col_count - 1:
            grad_out = jnp.stack(branches, axis=0)
            grad_out = over_tokens(mixes_all, after(grad_out, shares[-1])).astype(BF)
        if d == 1:
            beside, shares[0] = lax.optimization_barrier((beside, shares[0]))
            branches = [branch] + [v[0] for v in beside]
            if four:
                branches.append(jnp.concatenate(far(*beside, col_count), axis=1)[0])
            dn_sends, _ = lax.optimization_barrier((dn_sends, branches[-1]))
            dn_got = exchange(dn_sends)
        elif d > 1:
            branches[d], shares[-1] = lax.optimization_barrier((branches[d], shares[-1]))
        if d == 2 and four:
            branches[2], branches[3] = lax.optimization_barrier((branches[2], branches[3]))
        if d == col_count - 1:
            branches[d], dn_got, grad_out, y_sum = lax.optimization_barrier(
                (branches[d], dn_got, grad_out, y_sum)
            )
            grad_out = lax.psum_scatter(grad_out, "row", scatter_dimension=1, tiled=True)
        mix_grad = dot_nt(branches[d], out_all).astype(BF)
        grad_q, grad_prompt, pair, gain_part = attend_back(
            row_word, qs[d], every[d], kvs[d], blocks, mix_grad, mixes[d], logs[d], scales[d],
            coses[d], sines[d], gain_q,
        )
        grad_qs.append(grad_q)
        prompts.append(grad_prompt)
        pairs.append(pair)
        gain_q_grad = gain_q_grad + gain_part[0]
        if d == col_count - 1:
            grad_q, prompts[-1], pairs[-1], sent, grad_out = lax.optimization_barrier(
                (grad_q, prompts[-1], pairs[-1], sent, grad_out)
            )
        share = input_share(grad_q, wide, F32 if d == 0 else BF)
        shares.append(share)
        if d == 2:
            sent[0] = swap(after(shares[1], share), 1, col_count)
        if d > 0:
            sent.append(swap(share, d, col_count))
    grad_q = over_tokens(normed_all, after(jnp.stack(grad_qs, axis=0), shares[-1]))
    gain_one_grad = jnp.sum(grad_q * wide[:, : heads * HEAD].astype(F32), axis=1)
    grad_q = grad_q.astype(BF)
    prompt = jnp.stack(prompts, axis=0)
    prompt = lax.psum_scatter(prompt, "row", scatter_dimension=2, tiled=True)
    prompt, grad_q = lax.optimization_barrier((prompt, grad_q))
    prompt = to_owners(prompt)
    for d in slots:
        pair = pairs[d] + prompt[d].astype(F32)
        key_dy = back_turn(pair[0], coses[d], sines[d])
        key_hat = back_turn(kvs[d][0].astype(F32), coses[d], sines[d]) / gain_k
        gain_k_grad = gain_k_grad + jnp.sum(key_dy * key_hat, axis=0)
        key_raw = norm_back(key_dy, key_hat, scales[d][:, heads : heads + 1], gain_k)
        grad_kv = jnp.concatenate([key_raw.astype(BF), pair[1].astype(BF)], axis=1)
        grad_kvs.append(grad_kv)
        kv_moved.append(grad_kv if d == 0 else swap(grad_kv, d, col_count))
    grad_q = lax.psum_scatter(grad_q, "row", scatter_dimension=0, tiled=True)

    grad_kv = over_tokens(normed_all, jnp.stack(grad_kvs, axis=0))
    gain_one_grad = gain_one_grad + jnp.sum(
        grad_kv * wide[:, heads * HEAD : cols].astype(F32), axis=1
    )
    gain_one_grad = gain_one_grad / gain_one[0]
    grad_kv = lax.all_to_all(
        grad_kv.astype(BF).reshape(devices, -1, 2 * HEAD),
        ("row", "col"),
        split_axis=0,
        concat_axis=0,
        tiled=True,
    )
    grad_kv = jnp.sum(grad_kv.astype(F32).reshape(row_count, col_count, -1, 2 * HEAD), axis=0)
    grad_kv = grad_kv.reshape(KEY_VALUE_HEADS, sharing, -1, 2, HEAD).sum(axis=1)
    grad_kv = grad_kv.transpose(1, 2, 0, 3).reshape(-1, 2 * kv_cols)
    tail = [grad_router, gain_two_grad, gain_one_grad, gain_q_grad, gain_k_grad]
    tail = [v.reshape(devices, -1) for v in tail]
    tail.append(jnp.broadcast_to(jnp.sum(probs, axis=1)[None], (devices, experts)))
    cuts = [0]
    for v in tail:
        cuts.append(cuts[-1] + v.shape[1])
    tail = lax.all_to_all(
        jnp.concatenate(tail, axis=1), ("row", "col"), split_axis=0, concat_axis=0, tiled=True
    )
    tail = jnp.sum(tail, axis=0)
    grad_router, gain_two_grad, gain_one_grad, gain_q_grad, gain_k_grad, mean_probs = [
        tail[a:b] for a, b in zip(cuts[:-1], cuts[1:])
    ]
    mean_probs = mean_probs / tokens
    aux_loss = experts * jnp.sum(load * mean_probs)
    expert_load = jnp.stack([experts * load, experts * mean_probs])

    kv_share = dot_nt(jnp.concatenate(kv_moved, axis=1), kv_weight)
    input_sum = shares[0] + kv_share
    for got in sent:
        input_sum = input_sum + got.astype(F32)
    x_wide = x_own.astype(F32)
    x_spread = lax.rsqrt(jnp.mean(x_wide * x_wide, axis=-1, keepdims=True) + EPS)
    x_hat = x_wide * x_spread
    input_grad = hidden_grad + norm_back(input_sum, x_hat, x_spread, gain_one)

    own_grads, _ = lax.optimization_barrier((own_grads, kv_share))
    ffe = w_gate.shape[2]
    grad_gate = own_grads[0][:, :ffe] + sum(v[:, :ffe].astype(F32) for v in gu_got)
    grad_up = own_grads[0][:, ffe:] + sum(v[:, ffe:].astype(F32) for v in gu_got)
    grad_down = own_grads[1] + sum(v.astype(F32) for v in dn_got)
    layer_output = (hidden + y_sum.astype(F32)).astype(BF)

    return (
        layer_output[None],
        aux_loss,
        input_grad[None],
        grad_q.astype(F32),
        grad_kv,
        grad_out.astype(F32),
        grad_router.reshape(width // devices, experts),
        gain_one_grad,
        gain_two_grad,
        gain_q_grad,
        gain_k_grad,
        grad_gate[None],
        grad_up[None],
        grad_down[None],
        expert_load,
    )


def solution(mesh):
    in_specs = (
        P("col", "row", None),
        P("col", "row", None),
        P("col", "row", None),
        P(None, "row"),
        P("row", "col"),
        P("row", None),
        P("col", "row"),
        P("row", None),
        P("row"),
        P("row"),
        P("row"),
        P("row"),
        P(("row", "col"), None, None),
        P(("row", "col"), None, None),
        P(("row", "col"), None, None),
    )
    out_specs = (
        P("col", "row", None),
        P(),
        P("col", "row", None),
        P("row", "col"),
        P(("row", "col"), None),
        P("col", "row"),
        P(("row", "col"), None),
        P(("row", "col")),
        P(("row", "col")),
        P(("row", "col")),
        P(("row", "col")),
        P(("row", "col"), None, None),
        P(("row", "col"), None, None),
        P(("row", "col"), None, None),
        P(),
    )
    return jax.shard_map(
        per_device, mesh=mesh, in_specs=in_specs, out_specs=out_specs, check_vma=False
    )
```
